256 devices in a mesh: seq: 64 (over y, z, core), batch: 4 (over x).
Axes of the slice: x: 4, y: 4, z: 8, core: 2. Of those that a mesh axis runs over, the one named last changes fastest.
Arguments:
- query: bfloat16 [65536, 512], P(('batch', 'seq')), parts along dimension 0, may hold values from -104 to 104
- key_rows: bfloat16 [65536, 512], P(('batch', 'seq')), parts along dimension 0, may hold values from -4 to 4
- value_rows: bfloat16 [65536, 512], P(('batch', 'seq')), parts along dimension 0, may hold values from -6 to 6
- out_grad: bfloat16 [65536, 512], P(('batch', 'seq')), parts along dimension 0, may hold values from -6 to 6
Outputs:
- attended: bfloat16 [65536, 512], P(('batch', 'seq')), parts along dimension 0
- query_grad: bfloat16 [65536, 512], P(('batch', 'seq')), parts along dimension 0
- key_grad: bfloat16 [65536, 512], P(('batch', 'seq')), parts along dimension 0
- value_grad: bfloat16 [65536, 512], P(('batch', 'seq')), parts along dimension 0
The draws below stay inside these ranges and needn't reach their ends.
There are 4 independent parts, one for each index of `batch`. The reference program is written for one: setup_inputs(seed, part) draws one part's arguments, and reference() takes and returns one part's arrays. A program takes and returns all parts, laid end to end along the dimension named above; each array names one. Nothing has to cross between parts.
All inputs are finite; a program needn't handle non-finite values.
Results may differ from the reference program's by a relative error of at most 0.02.
Values may be sent and summed in bfloat16 or wider, within the bound.
No kernel may reach another device: no remote copies, remote signals or barrier semaphores. Data moves between devices by JAX's collectives and lax.ppermute only.
A program may use at most 128 MiB of HBM per device.

```python
import jax
import jax.numpy as jnp
from jax import lax

HEADS = 4
HEAD = 128
D = 512
B = 128
LEVELS = 3
TOKENS = 16384


def aligned_rows(base_key, align_share):
    query_key, key_key, pick_key, strength_key = jax.random.split(base_key, 4)
    query_base = jax.random.truncated_normal(query_key, -4.0, 4.0, (TOKENS, HEADS * HEAD), jnp.float32)
    key_base = jax.random.truncated_normal(key_key, -4.0, 4.0, (TOKENS, HEADS * HEAD), jnp.float32)
    chosen = (jax.random.uniform(pick_key, (TOKENS,), jnp.float32) < align_share) & (jnp.arange(TOKENS) >= 8)
    partner = jnp.roll(chosen, -2)
    key_final = jnp.where(partner[:, None], 0.99 * jnp.roll(key_base, 1, axis=0), key_base)
    strength = jax.random.uniform(strength_key, (TOKENS, 1), jnp.float32, 10.0, 26.0)
    query_final = jnp.where(chosen[:, None], strength * jnp.roll(key_final, 3, axis=0), query_base)
    return (query_final, key_final)


def draw_query(key, part):
    drawn = aligned_rows(key, 0.0)
    return drawn[0].astype(jnp.bfloat16)


def draw_key_rows(key, part):
    drawn = aligned_rows(key, 0.0)
    return drawn[1].astype(jnp.bfloat16)


def block_scale(key, dims, cuts, low, high):
    gain = 1.0
    for position, parts in cuts:
        steps = jax.random.uniform(jax.random.fold_in(jax.random.fold_in(key, 6), position), (parts,), jnp.float32, low / len(cuts), high / len(cuts))
        gain = gain * jnp.repeat(jnp.exp(steps), dims[position] // parts).reshape((-1,) + (1,) * (len(dims) - 1 - position))
    return gain


def centred(own_key, shape, scale, most, cuts=(), kind=jnp.bfloat16):
    loudness = block_scale(own_key, shape, cuts, -0.22, 0.18) if cuts else 1.0
    values = jax.random.normal(own_key, shape, jnp.float32) * scale * loudness
    return jnp.minimum(jnp.maximum(values, -most), most).astype(kind)


def setup_inputs(seed: int = 0, part: int = 0) -> dict:
    key_of = jax.random.split(jax.random.key(seed), 5)
    part_keys = jax.random.split(jax.random.fold_in(key_of[4], part), 5)
    query = draw_query(jax.random.fold_in(jax.random.fold_in(key_of[4], part), 71), part)
    key_rows = draw_key_rows(jax.random.fold_in(jax.random.fold_in(key_of[4], part), 71), part)
    value_rows = centred(part_keys[2], (TOKENS, D), 1.0, 6.0, ((0, 64),))
    out_grad = centred(part_keys[3], (TOKENS, D), 1.0, 6.0, ((0, 64),))
    return dict(query=query, key_rows=key_rows, value_rows=value_rows, out_grad=out_grad)


def coarsen(tok_rows):
    paired = tok_rows.reshape(tok_rows.shape[0] // 2, 2, tok_rows.shape[1]).astype(jnp.float32)
    return lax.optimization_barrier((jnp.sum(paired, axis=1) * 0.5).astype(jnp.bfloat16))


def expand(values, coarse_level):
    return jnp.repeat(values, 2 ** coarse_level, axis=0)


def visible(query_pos, key_pos, level_length, coarse_level, block_rows):
    inside = (key_pos[:, None, :] >= 0) & (key_pos[:, None, :] < level_length)
    if coarse_level > 0:
        half_rows = block_rows // 2
        distance = jnp.abs(query_pos[:, :, None] // half_rows - key_pos[:, None, :] // half_rows)
        inside = inside & (distance >= 2)
    return inside[:, :, None, :]


def windowed(tok_rows):
    groups = tok_rows.shape[0] // B
    padding = jnp.zeros((B, tok_rows.shape[1]), tok_rows.dtype)
    stacked = jnp.concatenate([padding, tok_rows, padding], axis=0).reshape(groups + 2, B, tok_rows.shape[1])
    return jnp.concatenate([stacked[:-2], stacked[1:-1], stacked[2:]], axis=1)


def unwindowed(grads):
    groups = grads.shape[0]
    lower_part = jnp.pad(grads[:, :B], ((0, 2), (0, 0), (0, 0)))
    middle_part = jnp.pad(grads[:, B:2 * B], ((1, 1), (0, 0), (0, 0)))
    upper_part = jnp.pad(grads[:, 2 * B:], ((2, 0), (0, 0), (0, 0)))
    return (lower_part + middle_part + upper_part)[1:-1].reshape(groups * B, grads.shape[2])


def reference(query, key_rows, value_rows, out_grad):
    highest = lax.Precision.HIGHEST
    score_scale = HEAD ** -0.5
    feat_width = HEADS * HEAD
    query_levels = [query]
    key_levels = [key_rows]
    value_levels = [value_rows]
    for coarse_level in range(1, LEVELS + 1):
        query_levels.append(coarsen(query_levels[-1]))
        key_levels.append(coarsen(key_levels[-1]))
        value_levels.append(coarsen(value_levels[-1]))
    records = []
    for coarse_level in range(LEVELS + 1):
        level_rows = TOKENS // 2 ** coarse_level
        groups = level_rows // B
        query_blocks = query_levels[coarse_level].reshape(groups, B, HEADS, HEAD).astype(jnp.float32)
        key_blocks = windowed(key_levels[coarse_level]).reshape(groups, 3 * B, HEADS, HEAD).astype(jnp.float32)
        value_blocks = windowed(value_levels[coarse_level]).reshape(groups, 3 * B, HEADS, HEAD).astype(jnp.float32)
        query_pos = jnp.arange(level_rows, dtype=jnp.int32).reshape(groups, B)
        key_pos = (jnp.arange(groups, dtype=jnp.int32)[:, None] - 1) * B + jnp.arange(3 * B, dtype=jnp.int32)[None, :]
        mask_rows = visible(query_pos, key_pos, level_rows, coarse_level, B)
        scores = jnp.einsum("bqhd,bkhd->bqhk", query_blocks, key_blocks, precision=highest) * score_scale
        row_peak = jnp.max(jnp.where(mask_rows, scores, -jnp.inf), axis=-1)
        safe_peak = jnp.where(row_peak > -jnp.inf, row_peak, 0.0)
        weights = jnp.where(mask_rows, jnp.exp(scores - safe_peak[..., None]), 0.0)
        row_total = jnp.sum(weights, axis=-1)
        rounded = lax.optimization_barrier(weights.astype(jnp.bfloat16)).astype(jnp.float32)
        row_mix = jnp.einsum("bqhk,bkhd->bqhd", rounded, value_blocks, precision=highest)
        records.append((query_blocks, key_blocks, value_blocks, weights, rounded,
                        row_peak.reshape(level_rows, HEADS), row_total.reshape(level_rows, HEADS),
                        row_mix.reshape(level_rows, HEADS, HEAD)))
    peaks = [expand(records[coarse_level][5], coarse_level) for coarse_level in range(LEVELS + 1)]
    overall = peaks[0]
    for coarse_level in range(1, LEVELS + 1):
        overall = jnp.maximum(overall, peaks[coarse_level])
    factors = [2.0 ** coarse_level * jnp.exp(peaks[coarse_level] - overall) for coarse_level in range(LEVELS + 1)]
    normaliser = factors[0] * records[0][6]
    numerator = factors[0][..., None] * records[0][7]
    for coarse_level in range(1, LEVELS + 1):
        normaliser = normaliser + factors[coarse_level] * expand(records[coarse_level][6], coarse_level)
        numerator = numerator + factors[coarse_level][..., None] * expand(records[coarse_level][7], coarse_level)
    result = numerator / normaliser[..., None]
    attended = result.reshape(TOKENS, feat_width).astype(jnp.bfloat16)
    grad_heads = out_grad.astype(jnp.float32).reshape(TOKENS, HEADS, HEAD)
    drift_rows = jnp.sum(grad_heads * result, axis=-1)
    query_acc = jnp.zeros((TOKENS, feat_width), jnp.float32)
    key_acc = jnp.zeros((TOKENS, feat_width), jnp.float32)
    value_acc = jnp.zeros((TOKENS, feat_width), jnp.float32)
    for coarse_level in range(LEVELS + 1):
        query_blocks, key_blocks, value_blocks, weights, rounded = records[coarse_level][:5]
        level_rows = TOKENS // 2 ** coarse_level
        groups = level_rows // B
        share = factors[coarse_level] / normaliser
        weighted = jnp.sum((share[..., None] * grad_heads).reshape(level_rows, 2 ** coarse_level, HEADS, HEAD), axis=1)
        weighted = lax.optimization_barrier(weighted.astype(jnp.bfloat16)).astype(jnp.float32)
        drift = jnp.sum((share * drift_rows).reshape(level_rows, 2 ** coarse_level, HEADS), axis=1)
        grad_blocks = weighted.reshape(groups, B, HEADS, HEAD)
        drift_blocks = drift.reshape(groups, B, HEADS)
        value_part = jnp.einsum("bqhk,bqhd->bkhd", rounded, grad_blocks, precision=highest)
        inner = jnp.einsum("bqhd,bkhd->bqhk", grad_blocks, value_blocks, precision=highest)
        dscore = weights * (inner - drift_blocks[..., None])
        dscore = lax.optimization_barrier(dscore.astype(jnp.bfloat16)).astype(jnp.float32)
        query_part = jnp.einsum("bqhk,bkhd->bqhd", dscore, key_blocks, precision=highest) * score_scale
        key_part = jnp.einsum("bqhk,bqhd->bkhd", dscore, query_blocks, precision=highest) * score_scale
        weight_down = 0.5 ** coarse_level
        query_acc = query_acc + expand(query_part.reshape(level_rows, feat_width), coarse_level) * weight_down
        key_acc = key_acc + expand(unwindowed(key_part.reshape(groups, 3 * B, feat_width)), coarse_level) * weight_down
        value_acc = value_acc + expand(unwindowed(value_part.reshape(groups, 3 * B, feat_width)), coarse_level) * weight_down
    return (attended, query_acc.astype(jnp.bfloat16), key_acc.astype(jnp.bfloat16), value_acc.astype(jnp.bfloat16))
```

```python
import jax
import jax.numpy as jnp
from jax import lax
from jax.experimental import pallas as pl
from jax.experimental.pallas import tpu as pltpu
from jax.sharding import PartitionSpec as P

HEADS = 4
HEAD = 128
D = HEADS * HEAD
ROWS = 256
FULL = 2 * D
SCALE = HEAD**-0.5
LOG2E = 1.4426950408889634
EXP_SCALE = SCALE * LOG2E
NEG = -1e30
VMEM_LIMIT = 40 * 1024 * 1024
BF = jnp.bfloat16
F32 = jnp.float32

RUN = 16


def place():
    index = lax.axis_index("seq")
    return lax.rem(index, 2), lax.div(index, 2)


def part(number, size):
    return pl.ds(pl.multiple_of(number * size, size), size)


def head(h):
    return slice(h * HEAD, (h + 1) * HEAD)


def order_matrix(back=False):
    a = lax.broadcasted_iota(jnp.int32, (128, 128), 0)
    b = lax.broadcasted_iota(jnp.int32, (128, 128), 1)
    row, token = (b, a) if back else (a, b)
    hit = row == (token & 7) * RUN + lax.shift_right_logical(token, 3)
    return jnp.where(hit, 1.0, 0.0).astype(BF)


def reorder(matrix, x):
    blocks = [jnp.dot(matrix, x[i : i + 128], preferred_element_type=F32) for i in range(0, x.shape[0], 128)]
    return jnp.concatenate(blocks, axis=0).astype(BF)


def coarse(x):
    rows, lanes = x.shape
    y = x.astype(F32).reshape(rows // (2 * RUN), 2, RUN, lanes)
    return ((y[:, 0] + y[:, 1]) * 0.5).reshape(rows // 2, lanes).astype(BF)


def expand(x, level=1):
    rows, lanes = x.shape
    step = 2**level
    y = jnp.broadcast_to(x.reshape(rows // RUN, 1, RUN, lanes), (rows // RUN, step, RUN, lanes))
    return y.reshape(rows * step, lanes)


def fold(x, level):
    rows, lanes = x.shape
    step = 2**level
    y = x.reshape(rows // (step * RUN), step, RUN, lanes)
    total = y[:, 0]
    for s in range(1, step):
        total = total + y[:, s]
    return total.reshape(rows // step, lanes)


def nt(a, b):
    return lax.dot_general(a, b, (((1,), (1,)), ((), ())), preferred_element_type=F32)


def tn(a, b):
    return lax.dot_general(a, b, (((0,), (0,)), ((), ())), preferred_element_type=F32)


def nn(a, b):
    return jnp.dot(a, b, preferred_element_type=F32)


def lanes128(value):
    return jnp.broadcast_to(value, (value.shape[0], HEAD))


def wide(value, count):
    return value if count == 1 else jnp.concatenate([value] * count, axis=1)


def penalty(ok):
    return jnp.where(ok, 0.0, NEG).astype(F32)


def half_masks():
    row = lax.broadcasted_iota(jnp.int32, (128, 128), 0) >= 64
    key = lax.broadcasted_iota(jnp.int32, (128, 128), 1) >= 64
    left = jnp.where(jnp.logical_and(~row, key), NEG, 0.0).astype(F32)
    right = jnp.where(jnp.logical_and(row, ~key), NEG, 0.0).astype(F32)
    return left, right


def soft(units):
    scores = [nt(q, k) if bias is None else nt(q, k) + bias for q, k, _, bias in units]
    peaks = [jnp.max(s, axis=1, keepdims=True) for s in scores]
    weights = [jnp.exp2((s - peak) * EXP_SCALE) for s, peak in zip(scores, peaks)]
    rounded = [e.astype(BF) for e in weights]
    mixes = [nn(eb, v) for eb, (_, _, v, _) in zip(rounded, units)]
    sums = [jnp.sum(e, axis=1, keepdims=True) for e in weights]
    return [
        (eb, lanes128(peak * EXP_SCALE), lanes128(den), mix)
        for eb, peak, den, mix in zip(rounded, peaks, sums, mixes)
    ]


def backward(units):
    inners = [nt(grad, v) for _, _, v, _, grad, _ in units]
    dvs = [tn(eb, grad) for _, _, _, eb, grad, _ in units]
    dscores = [
        (eb.astype(F32) * (inner - wide(drift, eb.shape[1] // HEAD))).astype(BF)
        for inner, (_, _, _, eb, _, drift) in zip(inners, units)
    ]
    dqs = [nn(dscore, k) * SCALE for dscore, (_, k, _, _, _, _) in zip(dscores, units)]
    dks = [tn(dscore, q) * SCALE for dscore, (q, _, _, _, _, _) in zip(dscores, units)]
    return list(zip(dqs, dks, dvs))


def merge(top, z, y, pieces):
    best = top
    peaks = [expand(m, level) if level else m for m, _, _, level in pieces]
    for m in peaks:
        best = jnp.maximum(best, m)
    f = jnp.exp2(top - best)
    z, y = f * z, f * y
    factors = []
    for m, (_, d, n, level) in zip(peaks, pieces):
        f = jnp.exp2(m - best)
        if level:
            f = f * 2.0**level
            d, n = expand(d, level), expand(n, level)
        factors.append(f)
        z = z + f * d
        y = y + f * n
    return best, z, y, factors


def placed(value, first, rows):
    zeros = jnp.zeros((rows, value.shape[1]), F32)
    return jnp.concatenate([jnp.where(first, value, zeros), jnp.where(first, zeros, value)], axis=0)


def pre_kernel(raw, kv, l1, l2, l3, sib):
    core, _ = place()
    matrix = order_matrix()
    for i in range(2):
        lanes = slice(i * D, (i + 1) * D)
        fine = reorder(matrix, raw[:, lanes])
        kv[:, lanes] = fine
        fine = coarse(fine)
        l1[:, lanes] = fine
        fine = coarse(fine)
        l2[:, lanes] = fine
        l3[:, lanes] = coarse(fine)
    sib[:128] = kv[part(1 - core, 128), :]
    sib[128:] = l1[part(core, 64), :]


def pack_kernel(kv, l1, l3, s2, msg1, msg2):
    core, _ = place()
    msg1[:128] = kv[part(core, 128), :]
    msg1[128:192] = l1[part(1 - core, 64), :]
    msg1[192:] = s2[...]
    msg2[:32] = l3[...]
    msg2[32:] = coarse(s2[...])


def local_kernel(q_ref, g_ref, kv, sib, q0, g0, q1, q2, q3, win, s1, e0, e1, m0, m1, top, zsum, ysum, d1, n1):
    core, _ = place()
    matrix = order_matrix()
    q0[...] = reorder(matrix, q_ref[...])
    g0[...] = reorder(matrix, g_ref[...])
    q1[...] = coarse(q0[...])
    q2[...] = coarse(q1[...])
    q3[...] = coarse(q2[...])
    win[:256] = kv[...]
    win[256:] = sib[:128]
    s1[part(core, 64), :] = coarse(sib[:128])
    s1[part(1 - core, 64), :] = sib[128:]
    left, right = half_masks()
    bias = jnp.where(core == 0, right, left)
    for h in range(HEADS):
        kl, vl = head(h), head(HEADS + h)
        blocks = ((1 - core, 384), (core, 256))
        units = [(q1[:, kl], s1[:, kl], s1[:, vl], bias)]
        units += [(q0[part(n, 128), kl], win[:keys, kl], win[:keys, vl], None) for n, keys in blocks]
        first, *fine = soft(units)
        e1[h], m1[h], d1[h], n1[h] = first
        for i, (number, keys) in enumerate(blocks):
            rows, half = part(number, 128), part(number, 64)
            e, m, d, n = fine[i]
            e0[h, i * 128 : (i + 1) * 128, :keys] = e
            m0[h, i * 128 : (i + 1) * 128] = m
            top[h, rows], zsum[h, rows], ysum[h, rows], _ = merge(
                m, d, n, [(m1[h, half], d1[h, half], n1[h, half], 1)]
            )


def second_split_kernel(r1, after, l1, send):
    core, _ = place()
    l1[part(core, 64), :] = r1[128:192]
    l1[part(1 - core, 64), :] = coarse(r1[:128])
    send[:64] = coarse(l1[...])
    send[64:] = r1[192:]


def third_split_kernel(r2, r3, after, send):
    send[:64] = r2[...]
    send[64:] = r3[...]


def outer_kernel(q0, q1, r1, l1, top, zsum, ysum, top_out, z_out, y_out, e0, e1, m0, m1, d1, n1):
    core, chip = place()
    is0 = core == 0
    bad = penalty(jnp.where(is0, chip >= 1, chip <= 30))
    left, right = half_masks()
    bias = jnp.where(is0, left, right) + bad
    outer = part(core, 128)
    units = []
    for h in range(HEADS):
        kl, vl = head(h), head(HEADS + h)
        units.append((q1[:, kl], l1[:, kl], l1[:, vl], bias))
        units.append((q0[outer, kl], r1[:128, kl], r1[:128, vl], bad))
    results = soft(units)
    for h in range(HEADS):
        e1[h], m1[h], d1[h], n1[h] = results[2 * h]
        e0[h], m, d, n = results[2 * h + 1]
        m0[h] = m
        for number in (core, 1 - core):
            rows, half = part(number, 128), part(number, 64)
            pieces = [(m1[h, half], d1[h, half], n1[h, half], 1)]
            if number is core:
                pieces.append((m, d, n, 0))
            top_out[h, rows], z_out[h, rows], y_out[h, rows], _ = merge(
                top[h, rows], zsum[h, rows], ysum[h, rows], pieces
            )


def second_kernel(q2, r1, got, top, zsum, ysum, after, win, e2, m2, top_out, z_out, y_out):
    core, chip = place()
    is0 = core == 0
    win[:64] = r1[192:]
    win[64:192] = got[...]
    win[192:] = jnp.zeros((64, FULL), BF)
    lane = lax.broadcasted_iota(jnp.int32, (1, 256), 1)
    left_ok, right_ok = chip >= 1, chip <= 30
    own_bad = penalty(jnp.where(is0, left_ok, right_ok))
    sib_bad = penalty(jnp.where(is0, right_ok, left_ok))
    bias = jnp.where(lane < 64, own_bad, jnp.where(lane < 192, sib_bad, NEG))
    results = soft([(q2[:, head(h)], win[:, head(h)], win[:, head(HEADS + h)], bias) for h in range(HEADS)])
    for h in range(HEADS):
        e2[h], m2[h], d, n = results[h]
        for c in range(2):
            r, a = slice(c * 128, (c + 1) * 128), slice(c * 32, (c + 1) * 32)
            top_out[h, r], z_out[h, r], y_out[h, r], _ = merge(
                top[h, r], zsum[h, r], ysum[h, r], [(m2[h, a], d[a], n[a], 2)]
            )


def far_kernel(
    q2, q3, g_ref, top, zsum, ysum, w2, e2, m2, r2, r3, got,
    att, best_out, inv_out, delta_out, dq2, dq3, own2, own3, cross3, send,
    w3,
):
    core, chip = place()
    is0 = core == 0
    w3[:64] = r2[...]
    w3[64:128] = got[:64]
    w3[128:160] = r3[...]
    w3[160:192] = got[64:]
    w3[192:] = jnp.zeros((64, FULL), BF)
    low2, high2 = chip >= 2, chip <= 29
    even = lax.rem(chip, 2) == 0
    cross_bad = penalty(jnp.where(even, chip <= 28, chip >= 3))
    lane = lax.broadcasted_iota(jnp.int32, (1, 256), 1)
    own_bad = penalty(jnp.where(is0, low2, high2))
    sib_bad = penalty(jnp.where(is0, high2, low2))
    bias3 = jnp.where(
        lane < 64, own_bad, jnp.where(lane < 128, sib_bad, jnp.where(lane < 192, cross_bad, NEG))
    )
    third = soft([(q3[:, head(h)], w3[:, head(h)], w3[:, head(HEADS + h)], bias3) for h in range(HEADS)])
    units = []
    for h in range(HEADS):
        kl, vl = head(h), head(HEADS + h)
        e3, m3, d3, n3 = third[h]
        grads = ([], [])
        drifts = ([], [])
        for c in range(2):
            r = slice(c * 128, (c + 1) * 128)
            a, b = slice(c * 32, (c + 1) * 32), slice(c * 16, (c + 1) * 16)
            best, z, y, factors = merge(top[h, r], zsum[h, r], ysum[h, r], [(m3[b], d3[b], n3[b], 3)])
            inv = 1.0 / z
            y = y * inv
            att[r, kl] = y.astype(BF)
            g = g_ref[r, kl].astype(F32)
            delta = lanes128(jnp.sum(g * y, axis=1, keepdims=True))
            best_out[h, r] = best
            inv_out[h, r] = inv
            delta_out[h, r] = delta
            factors = [4.0 * jnp.exp2(expand(m2[h, a], 2) - best)] + factors
            for i in range(2):
                share = factors[i] * inv
                grads[i].append(fold(share * g, i + 2))
                drifts[i].append(fold(share * delta, i + 2))
        for i, (q, w, e) in enumerate(((q2, w2, e2[h]), (q3, w3, e3))):
            grad = jnp.concatenate(grads[i], axis=0).astype(BF)
            units.append((q[:, kl], w[:, kl], w[:, vl], e, grad, jnp.concatenate(drifts[i], axis=0)))
    results = backward(units)
    for h in range(HEADS):
        for i in range(2):
            dq, dk, dv = results[2 * h + i]
            (dq2, dq3)[i][h] = dq
            for lanes, value in ((head(h), dk), (head(HEADS + h), dv)):
                if i == 0:
                    own2[:, lanes] = value[:64]
                    send[:128, lanes] = value[64:192].astype(BF)
                else:
                    own3[:, lanes] = value[:64]
                    send[128:192, lanes] = value[64:128].astype(BF)
                    cross3[:, lanes] = value[128:160]
                    send[192:, lanes] = value[160:192].astype(BF)


def coarse_grad(m, best, inv, g, delta):
    grads, drifts = [], []
    for c in range(2):
        r, half = slice(c * 128, (c + 1) * 128), slice(c * 64, (c + 1) * 64)
        share = jnp.exp2(expand(m[half]) - best[r]) * (2.0 * inv[r])
        grads.append(fold(share * g[r].astype(F32), 1))
        drifts.append(fold(share * delta[r], 1))
    return jnp.concatenate(grads, axis=0).astype(BF), jnp.concatenate(drifts, axis=0)


def outer_back_kernel(
    q0, q1, g_ref, r1, l1, e0, e1, m0, m1, best, inv_ref, delta_ref,
    dq0, dq1, d0, d1,
):
    core, _ = place()
    outer = part(core, 128)
    units = []
    for h in range(HEADS):
        kl, vl = head(h), head(HEADS + h)
        share = jnp.exp2(m0[h] - best[h, outer]) * inv_ref[h, outer]
        grad = (share * g_ref[outer, kl].astype(F32)).astype(BF)
        drift = share * delta_ref[h, outer]
        units.append((q0[outer, kl], r1[:128, kl], r1[:128, vl], e0[h], grad, drift))
        grad, drift = coarse_grad(m1[h], best[h], inv_ref[h], g_ref[:, kl], delta_ref[h])
        units.append((q1[:, kl], l1[:, kl], l1[:, vl], e1[h], grad, drift))
    results = backward(units)
    for h in range(HEADS):
        kl, vl = head(h), head(HEADS + h)
        dq0[h], d0[:, kl], d0[:, vl] = results[2 * h]
        dq1[h], d1[:, kl], d1[:, vl] = results[2 * h + 1]


def join_kernel(own2, own3, cross3, d0, d1, got, msg1, msg2, msg3):
    core, _ = place()
    is0 = core == 0
    for j in range(2 * HEADS):
        lanes = head(j)
        msg1[192:, lanes] = (own2[:, lanes] + got[64:128, lanes].astype(F32)).astype(BF)
        first = d1[:, lanes] + expand(0.5 * got[:64, lanes].astype(F32))
        low, high = first[:64], first[64:]
        msg1[128:192, lanes] = jnp.where(is0, low, high).astype(BF)
        msg1[:128, lanes] = (d0[:, lanes] + expand(0.5 * jnp.where(is0, high, low))).astype(BF)
        msg2[:, lanes] = (own3[:, lanes] + got[128:192, lanes].astype(F32)).astype(BF)
        msg3[:, lanes] = (cross3[:, lanes] + got[192:, lanes].astype(F32)).astype(BF)


def rest_kernel(
    q0, q1, g_ref, win, s1, e0, e1, m0, m1, best, inv_ref, delta_ref, dqo0, dqo1, dq2, dq3, att_ref, after,
    att, dq_out, acc, send,
    t0,
):
    core, _ = place()
    is0 = core == 0
    matrix = order_matrix(back=True)
    att[...] = reorder(matrix, att_ref[...])
    for h in range(HEADS):
        kl, vl = head(h), head(HEADS + h)
        grad, drift = coarse_grad(m1[h], best[h], inv_ref[h], g_ref[:, kl], delta_ref[h])
        units = [(q1[:, kl], s1[:, kl], s1[:, vl], e1[h], grad, drift)]
        for i, (number, keys) in enumerate(((1 - core, 384), (core, 256))):
            rows, kept = part(number, 128), slice(i * 128, (i + 1) * 128)
            share = jnp.exp2(m0[h, kept] - best[h, rows]) * inv_ref[h, rows]
            grad = (share * g_ref[rows, kl].astype(F32)).astype(BF)
            drift = share * delta_ref[h, rows]
            units.append((q0[rows, kl], win[:keys, kl], win[:keys, vl], e0[h, kept, :keys], grad, drift))
        (dq, dk, dv), (dq_in, dk_in, dv_in), (dq_out0, dk_out, dv_out) = backward(units)
        t0[h, part(1 - core, 128)] = dq_in
        t0[h, part(core, 128)] = dq_out0 + dqo0[h]
        acc[:, kl] = dk_in[:256] + dk_out
        acc[:, vl] = dv_in[:256] + dv_out
        dq = dq + dqo1[h] + expand(0.5 * (dq2[h] + expand(0.5 * dq3[h])))
        dq_out[:, kl] = reorder(matrix, (t0[h] + expand(0.5 * dq)).astype(BF))
        for lanes, value, fine in ((kl, dk, dk_in), (vl, dv, dv_in)):
            low, high = value[:64], value[64:]
            send[:128, lanes] = (fine[256:] + expand(0.5 * jnp.where(is0, low, high))).astype(BF)
            send[128:, lanes] = jnp.where(is0, high, low).astype(BF)


def add_kernel(own, r1, r2, r3, acc, send):
    core, _ = place()
    is0 = core == 0
    for j in range(2 * HEADS):
        lanes = head(j)
        sib3 = r2[32:, lanes].astype(F32)
        send[:, lanes] = (r1[192:, lanes].astype(F32) + expand(0.5 * sib3)).astype(BF)
        own3 = r2[:32, lanes].astype(F32) + r3[:, lanes].astype(F32)
        first = expand(0.25 * own3, 2) + placed(r1[128:192, lanes].astype(F32), ~is0, 64)
        acc[:, lanes] = own[:, lanes] + expand(0.5 * first) + placed(r1[:128, lanes].astype(F32), is0, 128)


def final_kernel(acc, near, got, dk, dv):
    core, _ = place()
    is0 = core == 0
    matrix = order_matrix(back=True)
    for j in range(2 * HEADS):
        lanes = head(j)
        first = expand(0.5 * got[:, lanes].astype(F32)) + placed(near[128:, lanes].astype(F32), is0, 64)
        total = acc[:, lanes] + expand(0.5 * first) + placed(near[:128, lanes].astype(F32), ~is0, 128)
        (dk if j < HEADS else dv)[:, head(j % HEADS)] = reorder(matrix, total.astype(BF))


SPACES = {"v": pltpu.VMEM, "a": pl.ANY}


def call(kernel, outs, scratch=(), flops=0, specs=None):
    extra = {"in_specs": [pl.BlockSpec(memory_space=SPACES[s]) for s in specs]} if specs else {}
    if flops:
        extra["cost_estimate"] = pl.CostEstimate(flops=flops, bytes_accessed=1 << 20, transcendentals=0)
    return pl.pallas_call(
        kernel,
        out_shape=[jax.ShapeDtypeStruct(shape, dtype) for shape, dtype in outs],
        out_specs=[pl.BlockSpec(memory_space=pltpu.VMEM)] * len(outs),
        scratch_shapes=[s if not isinstance(s, tuple) else pltpu.VMEM(*s) for s in scratch],
        compiler_params=pltpu.CompilerParams(vmem_limit_bytes=VMEM_LIMIT),
        **extra,
    )


def per_device(query, key_rows, value_rows, out_grad):
    count = lax.axis_size("seq")
    sibling = [(i, i + 1) for i in range(0, count, 2)]
    next1 = [(i, i + 1) for i in range(1, count - 1, 2)]
    next2 = [(i, i + 3) for i in range(1, count - 3, 2)]
    next3 = [(i, i + 6) for i in range(count - 6) if (i // 2) % 2 == 0]

    def swap(value, pairs):
        return lax.ppermute(value, "seq", pairs + [(b, a) for a, b in pairs])

    def rows(n, dtype=BF):
        return ((n, FULL), dtype)

    def heads(n, dtype=F32, lanes=HEAD):
        return ((HEADS, n, lanes), dtype)

    stat = heads(256)
    out = ((ROWS, D), BF)
    kv, l1, l2, l3, near = call(
        pre_kernel,
        [rows(256), rows(128), rows(64), rows(32), rows(192)],
    )(jnp.concatenate([key_rows, value_rows], axis=1))
    s2 = swap(l2, sibling)
    r3 = swap(l3, next3)
    msg1, msg2 = call(pack_kernel, [rows(256), rows(64)])(kv, l1, l3, s2)
    r1 = swap(msg1, next1)
    r2 = swap(msg2, next2)
    near = swap(near, sibling)
    q0, g0, q1, q2, q3, win, s1, e0, e1, m0, m1, top, zsum, ysum = call(
        local_kernel,
        [out, out, ((128, D), BF), ((64, D), BF), ((32, D), BF), rows(384), rows(128)]
        + [heads(256, BF, 384), heads(128, BF), stat, heads(128), stat, stat, stat],
        [heads(128), heads(128)],
        flops=1 << 31,
    )(query, out_grad, kv, near)
    outer1, send = call(second_split_kernel, [rows(128), rows(128)], specs="va")(r1, top)
    got2 = swap(send, sibling)
    top, zsum, ysum, eo0, eo1, mo0, mo1 = call(
        outer_kernel,
        [stat] * 3 + [heads(128, BF), heads(128, BF), heads(128), heads(128)],
        [heads(128), heads(128)],
        flops=1 << 30,
    )(q0, q1, r1, outer1, top, zsum, ysum)
    (send,) = call(third_split_kernel, [rows(96)], specs="vva")(r2, r3, top)
    got3 = swap(send, sibling)
    w2, e2, m2, top, zsum, ysum = call(
        second_kernel,
        [rows(256), heads(64, BF, 256), heads(64), stat, stat, stat],
        flops=1 << 28,
        specs="v" * 6 + "a",
    )(q2, r1, got2, top, zsum, ysum, send)
    att, best, inv, delta, dq2, dq3, own2, own3, cross3, send = call(
        far_kernel,
        [out, stat, stat, stat, heads(64), heads(32), rows(64, F32), rows(64, F32), rows(32, F32), rows(224)],
        [rows(256)],
    )(q2, q3, g0, top, zsum, ysum, w2, e2, m2, r2, r3, got3)
    got = swap(send, sibling)
    dqo0, dqo1, d0, d1 = call(
        outer_back_kernel, [heads(128), heads(128), rows(128, F32), rows(128, F32)], flops=1 << 30
    )(q0, q1, g0, r1, outer1, eo0, eo1, mo0, mo1, best, inv, delta)
    msg1, msg2, msg3 = call(join_kernel, [rows(256), rows(64), rows(32)])(own2, own3, cross3, d0, d1, got)
    r1 = swap(msg1, next1)
    r2 = swap(msg2, next2)
    r3 = swap(msg3, next3)
    attended, query_grad, acc, send = call(
        rest_kernel,
        [out, out, rows(256, F32), rows(192)],
        [stat],
        flops=1 << 31,
        specs="v" * 17 + "a",
    )(q0, q1, g0, win, s1, e0, e1, m0, m1, best, inv, delta, dqo0, dqo1, dq2, dq3, att, msg1)
    near = swap(send, sibling)
    acc, send = call(add_kernel, [rows(256, F32), rows(64)], flops=1 << 34)(acc, r1, r2, r3)
    got = swap(send, sibling)
    key_grad, value_grad = call(final_kernel, [out, out])(acc, near, got)
    return attended, query_grad, key_grad, value_grad


def solution(mesh):
    spec = P(("batch", "seq"), None)
    return jax.shard_map(
        per_device, mesh=mesh, in_specs=(spec,) * 4, out_specs=(spec,) * 4, check_vma=False
    )
```

```python
import jax
import jax.numpy as jnp
from jax import lax
from jax.experimental import pallas as pl
from jax.experimental.pallas import tpu as pltpu
from jax.sharding import PartitionSpec as P

HEADS = 4
HEAD = 128
D = HEADS * HEAD
ROWS = 256
FULL = 2 * D
SCALE = HEAD**-0.5
LOG2E = 1.4426950408889634
EXP_SCALE = SCALE * LOG2E
NEG = -1e30
VMEM_LIMIT = 40 * 1024 * 1024
BF = jnp.bfloat16
F32 = jnp.float32

RUN = 16


def place():
    index = lax.axis_index("seq")
    return lax.rem(index, 2), lax.div(index, 2)


def part(number, size):
    return pl.ds(pl.multiple_of(number * size, size), size)


def head(h):
    return slice(h * HEAD, (h + 1) * HEAD)


def order_matrix(back=False):
    a = lax.broadcasted_iota(jnp.int32, (128, 128), 0)
    b = lax.broadcasted_iota(jnp.int32, (128, 128), 1)
    row, token = (b, a) if back else (a, b)
    hit = row == (token & 7) * RUN + lax.shift_right_logical(token, 3)
    return jnp.where(hit, 1.0, 0.0).astype(BF)


def reorder(matrix, x):
    blocks = [jnp.dot(matrix, x[i : i + 128], preferred_element_type=F32) for i in range(0, x.shape[0], 128)]
    return jnp.concatenate(blocks, axis=0).astype(BF)


def coarse(x):
    rows, lanes = x.shape
    y = x.astype(F32).reshape(rows // (2 * RUN), 2, RUN, lanes)
    return ((y[:, 0] + y[:, 1]) * 0.5).reshape(rows // 2, lanes).astype(BF)


def expand(x, level=1):
    rows, lanes = x.shape
    step = 2**level
    y = jnp.broadcast_to(x.reshape(rows // RUN, 1, RUN, lanes), (rows // RUN, step, RUN, lanes))
    return y.reshape(rows * step, lanes)


def fold(x, level):
    rows, lanes = x.shape
    step = 2**level
    y = x.reshape(rows // (step * RUN), step, RUN, lanes)
    total = y[:, 0]
    for s in range(1, step):
        total = total + y[:, s]
    return total.reshape(rows // step, lanes)


def nt(a, b):
    return lax.dot_general(a, b, (((1,), (1,)), ((), ())), preferred_element_type=F32)


def tn(a, b):
    return lax.dot_general(a, b, (((0,), (0,)), ((), ())), preferred_element_type=F32)


def nn(a, b):
    return jnp.dot(a, b, preferred_element_type=F32)


def lanes128(value):
    return jnp.broadcast_to(value, (value.shape[0], HEAD))


def wide(value, count):
    return value if count == 1 else jnp.concatenate([value] * count, axis=1)


def penalty(ok):
    return jnp.where(ok, 0.0, NEG).astype(F32)


def half_masks():
    row = lax.broadcasted_iota(jnp.int32, (128, 128), 0) >= 64
    key = lax.broadcasted_iota(jnp.int32, (128, 128), 1) >= 64
    left = jnp.where(jnp.logical_and(~row, key), NEG, 0.0).astype(F32)
    right = jnp.where(jnp.logical_and(row, ~key), NEG, 0.0).astype(F32)
    return left, right


def soft(units):
    scores = [nt(q, k) if bias is None else nt(q, k) + bias for q, k, _, bias in units]
    peaks = [jnp.max(s, axis=1, keepdims=True) for s in scores]
    weights = [jnp.exp2((s - peak) * EXP_SCALE) for s, peak in zip(scores, peaks)]
    rounded = [e.astype(BF) for e in weights]
    mixes = [nn(eb, v) for eb, (_, _, v, _) in zip(rounded, units)]
    sums = [jnp.sum(e, axis=1, keepdims=True) for e in weights]
    return [
        (eb, lanes128(peak * EXP_SCALE), lanes128(den), mix)
        for eb, peak, den, mix in zip(rounded, peaks, sums, mixes)
    ]


def backward(units):
    inners = [nt(grad, v) for _, _, v, _, grad, _ in units]
    dvs = [tn(eb, grad) for _, _, _, eb, grad, _ in units]
    dscores = [
        (eb.astype(F32) * (inner - wide(drift, eb.shape[1] // HEAD))).astype(BF)
        for inner, (_, _, _, eb, _, drift) in zip(inners, units)
    ]
    dqs = [nn(dscore, k) * SCALE for dscore, (_, k, _, _, _, _) in zip(dscores, units)]
    dks = [tn(dscore, q) * SCALE for dscore, (q, _, _, _, _, _) in zip(dscores, units)]
    return list(zip(dqs, dks, dvs))


def merge(top, z, y, pieces):
    best = top
    peaks = [expand(m, level) if level else m for m, _, _, level in pieces]
    for m in peaks:
        best = jnp.maximum(best, m)
    f = jnp.exp2(top - best)
    z, y = f * z, f * y
    factors = []
    for m, (_, d, n, level) in zip(peaks, pieces):
        f = jnp.exp2(m - best)
        if level:
            f = f * 2.0**level
            d, n = expand(d, level), expand(n, level)
        factors.append(f)
        z = z + f * d
        y = y + f * n
    return best, z, y, factors


def placed(value, first, rows):
    zeros = jnp.zeros((rows, value.shape[1]), F32)
    return jnp.concatenate([jnp.where(first, value, zeros), jnp.where(first, zeros, value)], axis=0)


def pre_kernel(raw, kv, l1, l3):
    matrix = order_matrix()
    for i in range(2):
        lanes = slice(i * D, (i + 1) * D)
        fine = reorder(matrix, raw[:, lanes])
        kv[:, lanes] = fine
        fine = coarse(fine)
        l1[:, lanes] = fine
        l3[:, lanes] = coarse(coarse(fine))


def pack_kernel(kv, l1, l3, ks, vs, near, s1, msg1, msg2):
    core, _ = place()
    matrix = order_matrix()
    for i, raw in enumerate((ks, vs)):
        lanes = slice(i * D, (i + 1) * D)
        fine = reorder(matrix, raw[...])
        near[:, lanes] = jnp.where(core == 0, fine[:128], fine[128:])
        first = coarse(fine)
        s1[:, lanes] = first
        second = coarse(first)
        msg1[192:, lanes] = second
        msg2[32:, lanes] = coarse(second)
    msg1[:128] = kv[part(core, 128), :]
    msg1[128:192] = l1[part(1 - core, 64), :]
    msg2[:32] = l3[...]


def local_kernel(q_ref, g_ref, kv, near, s1, q0, g0, q1, q2, q3, win, e0, e1, m0, m1, top, zsum, ysum, d1, n1):
    core, _ = place()
    matrix = order_matrix()
    q0[...] = reorder(matrix, q_ref[...])
    g0[...] = reorder(matrix, g_ref[...])
    q1[...] = coarse(q0[...])
    q2[...] = coarse(q1[...])
    q3[...] = coarse(q2[...])
    win[:256] = kv[...]
    win[256:] = near[...]
    left, right = half_masks()
    bias = jnp.where(core == 0, right, left)
    for h in range(HEADS):
        kl, vl = head(h), head(HEADS + h)
        blocks = ((1 - core, 384), (core, 256))
        units = [(q1[:, kl], s1[:, kl], s1[:, vl], bias)]
        units += [(q0[part(n, 128), kl], win[:keys, kl], win[:keys, vl], None) for n, keys in blocks]
        first, *fine = soft(units)
        e1[h], m1[h], d1[h], n1[h] = first
        for i, (number, keys) in enumerate(blocks):
            rows, half = part(number, 128), part(number, 64)
            e, m, d, n = fine[i]
            e0[h, i * 128 : (i + 1) * 128, :keys] = e
            m0[h, i * 128 : (i + 1) * 128] = m
            top[h, rows], zsum[h, rows], ysum[h, rows], _ = merge(
                m, d, n, [(m1[h, half], d1[h, half], n1[h, half], 1)]
            )


def second_split_kernel(r1, after, l1, send):
    core, _ = place()
    l1[part(core, 64), :] = r1[128:192]
    l1[part(1 - core, 64), :] = coarse(r1[:128])
    send[:64] = coarse(l1[...])
    send[64:] = r1[192:]


def third_split_kernel(r2, r3, after, send):
    send[:64] = r2[...]
    send[64:] = r3[...]


def outer_kernel(q0, q1, r1, l1, top, zsum, ysum, top_out, z_out, y_out, e0, e1, m0, m1, d1, n1):
    core, chip = place()
    is0 = core == 0
    bad = penalty(jnp.where(is0, chip >= 1, chip <= 30))
    left, right = half_masks()
    bias = jnp.where(is0, left, right) + bad
    outer = part(core, 128)
    units = []
    for h in range(HEADS):
        kl, vl = head(h), head(HEADS + h)
        units.append((q1[:, kl], l1[:, kl], l1[:, vl], bias))
        units.append((q0[outer, kl], r1[:128, kl], r1[:128, vl], bad))
    results = soft(units)
    for h in range(HEADS):
        e1[h], m1[h], d1[h], n1[h] = results[2 * h]
        e0[h], m, d, n = results[2 * h + 1]
        m0[h] = m
        for number in (core, 1 - core):
            rows, half = part(number, 128), part(number, 64)
            pieces = [(m1[h, half], d1[h, half], n1[h, half], 1)]
            if number is core:
                pieces.append((m, d, n, 0))
            top_out[h, rows], z_out[h, rows], y_out[h, rows], _ = merge(
                top[h, rows], zsum[h, rows], ysum[h, rows], pieces
            )


def second_kernel(q2, r1, got, top, zsum, ysum, win, e2, m2, top_out, z_out, y_out):
    core, chip = place()
    is0 = core == 0
    win[:64] = r1[192:]
    win[64:192] = got[...]
    win[192:] = jnp.zeros((64, FULL), BF)
    lane = lax.broadcasted_iota(jnp.int32, (1, 256), 1)
    left_ok, right_ok = chip >= 1, chip <= 30
    own_bad = penalty(jnp.where(is0, left_ok, right_ok))
    sib_bad = penalty(jnp.where(is0, right_ok, left_ok))
    bias = jnp.where(lane < 64, own_bad, jnp.where(lane < 192, sib_bad, NEG))
    results = soft([(q2[:, head(h)], win[:, head(h)], win[:, head(HEADS + h)], bias) for h in range(HEADS)])
    for h in range(HEADS):
        e2[h], m2[h], d, n = results[h]
        for c in range(2):
            r, a = slice(c * 128, (c + 1) * 128), slice(c * 32, (c + 1) * 32)
            top_out[h, r], z_out[h, r], y_out[h, r], _ = merge(
                top[h, r], zsum[h, r], ysum[h, r], [(m2[h, a], d[a], n[a], 2)]
            )


def far_kernel(
    q2, q3, g_ref, top, zsum, ysum, w2, e2, m2, r2, r3, got,
    att, best_out, inv_out, delta_out, dq2, dq3, own2, own3, cross3, send,
    w3,
):
    core, chip = place()
    is0 = core == 0
    w3[:64] = r2[...]
    w3[64:128] = got[:64]
    w3[128:192] = jnp.where(lax.rem(core + chip, 2) == 1, r3[...], got[64:])
    w3[192:] = jnp.zeros((64, FULL), BF)
    holder = lax.rem(core + chip, 2) == 1
    low2, high2 = chip >= 2, chip <= 29
    even = lax.rem(chip, 2) == 0
    cross_bad = penalty(jnp.where(even, chip <= 28, chip >= 3))
    lane = lax.broadcasted_iota(jnp.int32, (1, 256), 1)
    own_bad = penalty(jnp.where(is0, high2, low2))
    sib_bad = penalty(jnp.where(is0, low2, high2))
    bias3 = jnp.where(
        lane < 64, own_bad, jnp.where(lane < 128, sib_bad, jnp.where(lane < 192, cross_bad, NEG))
    )
    third = soft([(q3[:, head(h)], w3[:, head(h)], w3[:, head(HEADS + h)], bias3) for h in range(HEADS)])
    units = []
    for h in range(HEADS):
        kl, vl = head(h), head(HEADS + h)
        e3, m3, d3, n3 = third[h]
        grads = ([], [])
        drifts = ([], [])
        for c in range(2):
            r = slice(c * 128, (c + 1) * 128)
            a, b = slice(c * 32, (c + 1) * 32), slice(c * 16, (c + 1) * 16)
            best, z, y, factors = merge(top[h, r], zsum[h, r], ysum[h, r], [(m3[b], d3[b], n3[b], 3)])
            inv = 1.0 / z
            y = y * inv
            att[r, kl] = y.astype(BF)
            g = g_ref[r, kl].astype(F32)
            delta = lanes128(jnp.sum(g * y, axis=1, keepdims=True))
            best_out[h, r] = best
            inv_out[h, r] = inv
            delta_out[h, r] = delta
            factors = [4.0 * jnp.exp2(expand(m2[h, a], 2) - best)] + factors
            for i in range(2):
                share = factors[i] * inv
                grads[i].append(fold(share * g, i + 2))
                drifts[i].append(fold(share * delta, i + 2))
        for i, (q, w, e) in enumerate(((q2, w2, e2[h]), (q3, w3, e3))):
            grad = jnp.concatenate(grads[i], axis=0).astype(BF)
            units.append((q[:, kl], w[:, kl], w[:, vl], e, grad, jnp.concatenate(drifts[i], axis=0)))
    results = backward(units)
    for h in range(HEADS):
        for i in range(2):
            dq, dk, dv = results[2 * h + i]
            (dq2, dq3)[i][h] = dq
            for lanes, value in ((head(h), dk), (head(HEADS + h), dv)):
                if i == 0:
                    own2[:, lanes] = value[:64]
                    send[:128, lanes] = value[64:192].astype(BF)
                else:
                    own3[:, lanes] = value[:64]
                    send[128:192, lanes] = value[64:128].astype(BF)
                    cross3[:, lanes] = jnp.where(holder, value[128:160], value[160:192])
                    send[192:, lanes] = jnp.where(holder, value[160:192], value[128:160]).astype(BF)


def coarse_grad(m, best, inv, g, delta):
    grads, drifts = [], []
    for c in range(2):
        r, half = slice(c * 128, (c + 1) * 128), slice(c * 64, (c + 1) * 64)
        share = jnp.exp2(expand(m[half]) - best[r]) * (2.0 * inv[r])
        grads.append(fold(share * g[r].astype(F32), 1))
        drifts.append(fold(share * delta[r], 1))
    return jnp.concatenate(grads, axis=0).astype(BF), jnp.concatenate(drifts, axis=0)


def outer_back_kernel(
    q0, q1, g_ref, r1, l1, e0, e1, m0, m1, best, inv_ref, delta_ref,
    dq0, dq1, d0, d1,
):
    core, _ = place()
    outer = part(core, 128)
    units = []
    for h in range(HEADS):
        kl, vl = head(h), head(HEADS + h)
        share = jnp.exp2(m0[h] - best[h, outer]) * inv_ref[h, outer]
        grad = (share * g_ref[outer, kl].astype(F32)).astype(BF)
        drift = share * delta_ref[h, outer]
        units.append((q0[outer, kl], r1[:128, kl], r1[:128, vl], e0[h], grad, drift))
        grad, drift = coarse_grad(m1[h], best[h], inv_ref[h], g_ref[:, kl], delta_ref[h])
        units.append((q1[:, kl], l1[:, kl], l1[:, vl], e1[h], grad, drift))
    results = backward(units)
    for h in range(HEADS):
        kl, vl = head(h), head(HEADS + h)
        dq0[h], d0[:, kl], d0[:, vl] = results[2 * h]
        dq1[h], d1[:, kl], d1[:, vl] = results[2 * h + 1]


def join_kernel(own2, own3, cross3, d0, d1, got, msg1, msg2, msg3):
    core, _ = place()
    is0 = core == 0
    for j in range(2 * HEADS):
        lanes = head(j)
        msg1[192:, lanes] = (own2[:, lanes] + got[64:128, lanes].astype(F32)).astype(BF)
        first = d1[:, lanes] + expand(0.5 * got[:64, lanes].astype(F32))
        low, high = first[:64], first[64:]
        msg1[128:192, lanes] = jnp.where(is0, low, high).astype(BF)
        msg1[:128, lanes] = (d0[:, lanes] + expand(0.5 * jnp.where(is0, high, low))).astype(BF)
        msg2[:, lanes] = (own3[:, lanes] + got[128:192, lanes].astype(F32)).astype(BF)
        msg3[:, lanes] = (cross3[:, lanes] + got[192:, lanes].astype(F32)).astype(BF)


def rest_kernel(
    q0, q1, g_ref, win, s1, e0, e1, m0, m1, best, inv_ref, delta_ref, dqo0, dqo1, dq2, dq3, att_ref, after,
    att, dq_out, acc, send,
    t0,
):
    core, _ = place()
    is0 = core == 0
    matrix = order_matrix(back=True)
    att[...] = reorder(matrix, att_ref[...])
    for h in range(HEADS):
        kl, vl = head(h), head(HEADS + h)
        grad, drift = coarse_grad(m1[h], best[h], inv_ref[h], g_ref[:, kl], delta_ref[h])
        units = [(q1[:, kl], s1[:, kl], s1[:, vl], e1[h], grad, drift)]
        for i, (number, keys) in enumerate(((1 - core, 384), (core, 256))):
            rows, kept = part(number, 128), slice(i * 128, (i + 1) * 128)
            share = jnp.exp2(m0[h, kept] - best[h, rows]) * inv_ref[h, rows]
            grad = (share * g_ref[rows, kl].astype(F32)).astype(BF)
            drift = share * delta_ref[h, rows]
            units.append((q0[rows, kl], win[:keys, kl], win[:keys, vl], e0[h, kept, :keys], grad, drift))
        (dq, dk, dv), (dq_in, dk_in, dv_in), (dq_out0, dk_out, dv_out) = backward(units)
        t0[h, part(1 - core, 128)] = dq_in
        t0[h, part(core, 128)] = dq_out0 + dqo0[h]
        acc[:, kl] = dk_in[:256] + dk_out
        acc[:, vl] = dv_in[:256] + dv_out
        dq = dq + dqo1[h] + expand(0.5 * (dq2[h] + expand(0.5 * dq3[h])))
        dq_out[:, kl] = reorder(matrix, (t0[h] + expand(0.5 * dq)).astype(BF))
        for lanes, value, fine in ((kl, dk, dk_in), (vl, dv, dv_in)):
            low, high = value[:64], value[64:]
            send[:128, lanes] = (fine[256:] + expand(0.5 * jnp.where(is0, low, high))).astype(BF)
            send[128:, lanes] = jnp.where(is0, high, low).astype(BF)


def add_kernel(own, r1, r2, r3, acc, send):
    core, _ = place()
    is0 = core == 0
    for j in range(2 * HEADS):
        lanes = head(j)
        sib3 = r2[32:, lanes].astype(F32)
        send[:, lanes] = (r1[192:, lanes].astype(F32) + expand(0.5 * sib3)).astype(BF)
        own3 = r2[:32, lanes].astype(F32) + r3[:, lanes].astype(F32)
        first = expand(0.25 * own3, 2) + placed(r1[128:192, lanes].astype(F32), ~is0, 64)
        acc[:, lanes] = own[:, lanes] + expand(0.5 * first) + placed(r1[:128, lanes].astype(F32), is0, 128)


def final_kernel(acc, near, got, dk, dv):
    core, _ = place()
    is0 = core == 0
    matrix = order_matrix(back=True)
    for j in range(2 * HEADS):
        lanes = head(j)
        first = expand(0.5 * got[:, lanes].astype(F32)) + placed(near[128:, lanes].astype(F32), is0, 64)
        total = acc[:, lanes] + expand(0.5 * first) + placed(near[:128, lanes].astype(F32), ~is0, 128)
        (dk if j < HEADS else dv)[:, head(j % HEADS)] = reorder(matrix, total.astype(BF))


SPACES = {"v": pltpu.VMEM, "a": pl.ANY}


def call(kernel, outs, scratch=(), flops=0, specs=None):
    extra = {"in_specs": [pl.BlockSpec(memory_space=SPACES[s]) for s in specs]} if specs else {}
    if flops:
        extra["cost_estimate"] = pl.CostEstimate(flops=flops, bytes_accessed=1 << 20, transcendentals=0)
    return pl.pallas_call(
        kernel,
        out_shape=[jax.ShapeDtypeStruct(shape, dtype) for shape, dtype in outs],
        out_specs=[pl.BlockSpec(memory_space=pltpu.VMEM)] * len(outs),
        scratch_shapes=[s if not isinstance(s, tuple) else pltpu.VMEM(*s) for s in scratch],
        compiler_params=pltpu.CompilerParams(vmem_limit_bytes=VMEM_LIMIT),
        **extra,
    )


def per_device(query, key_rows, value_rows, out_grad):
    count = lax.axis_size("seq")
    sibling = [(i, i + 1) for i in range(0, count, 2)]
    next1 = [(i, i + 1) for i in range(1, count - 1, 2)]
    next2 = [(i, i + 5) for i in range(0, count - 5, 2)]
    forward = [(i, i + 1) for i in range(1, count, 4)]
    next3 = [(i, i + 6) for i in range(count - 6) if (i // 2) % 2 == 0]

    def swap(value, pairs):
        return lax.ppermute(value, "seq", pairs + [(b, a) for a, b in pairs])

    def rows(n, dtype=BF):
        return ((n, FULL), dtype)

    def heads(n, dtype=F32, lanes=HEAD):
        return ((HEADS, n, lanes), dtype)

    stat = heads(256)
    out = ((ROWS, D), BF)
    key_sib = swap(key_rows, sibling)
    value_sib = swap(value_rows, sibling)
    kv, l1, l3 = call(pre_kernel, [rows(256), rows(128), rows(32)])(
        jnp.concatenate([key_rows, value_rows], axis=1)
    )
    near, s1, msg1, msg2 = call(pack_kernel, [rows(128), rows(128), rows(256), rows(64)])(
        kv, l1, l3, key_sib, value_sib
    )
    r2 = swap(msg2, next2)
    r1 = swap(msg1, next1)
    r3 = swap(r2, forward)
    q0, g0, q1, q2, q3, win, e0, e1, m0, m1, top, zsum, ysum = call(
        local_kernel,
        [out, out, ((128, D), BF), ((64, D), BF), ((32, D), BF), rows(384)]
        + [heads(256, BF, 384), heads(128, BF), stat, heads(128), stat, stat, stat],
        [heads(128), heads(128)],
        flops=1 << 33,
    )(query, out_grad, kv, near, s1)
    (send,) = call(third_split_kernel, [rows(128)], specs="vva")(r2, r3, top)
    got3 = swap(send, sibling)
    outer1, send = call(second_split_kernel, [rows(128), rows(128)], specs="va")(r1, send)
    got2 = swap(send, sibling)
    top, zsum, ysum, eo0, eo1, mo0, mo1 = call(
        outer_kernel,
        [stat] * 3 + [heads(128, BF), heads(128, BF), heads(128), heads(128)],
        [heads(128), heads(128)],
        flops=1 << 30,
    )(q0, q1, r1, outer1, top, zsum, ysum)
    w2, e2, m2, top, zsum, ysum = call(
        second_kernel,
        [rows(256), heads(64, BF, 256), heads(64), stat, stat, stat],
        flops=1 << 28,
    )(q2, r1, got2, top, zsum, ysum)
    att, best, inv, delta, dq2, dq3, own2, own3, cross3, send = call(
        far_kernel,
        [out, stat, stat, stat, heads(64), heads(32), rows(64, F32), rows(64, F32), rows(32, F32), rows(224)],
        [rows(256)],
    )(q2, q3, g0, top, zsum, ysum, w2, e2, m2, r2, r3, got3)
    got = swap(send, sibling)
    dqo0, dqo1, d0, d1 = call(
        outer_back_kernel, [heads(128), heads(128), rows(128, F32), rows(128, F32)], flops=1 << 30
    )(q0, q1, g0, r1, outer1, eo0, eo1, mo0, mo1, best, inv, delta)
    msg1, msg2, msg3 = call(join_kernel, [rows(256), rows(64), rows(32)])(own2, own3, cross3, d0, d1, got)
    r1 = swap(msg1, next1)
    r2 = swap(msg2, next2)
    r3 = swap(msg3, next3)
    attended, query_grad, acc, send = call(
        rest_kernel,
        [out, out, rows(256, F32), rows(192)],
        [stat],
        flops=1 << 31,
        specs="v" * 17 + "a",
    )(q0, q1, g0, win, s1, e0, e1, m0, m1, best, inv, delta, dqo0, dqo1, dq2, dq3, att, msg1)
    near = swap(send, sibling)
    acc, send = call(add_kernel, [rows(256, F32), rows(64)], flops=1 << 34)(acc, r1, r2, r3)
    got = swap(send, sibling)
    key_grad, value_grad = call(final_kernel, [out, out])(acc, near, got)
    return attended, query_grad, key_grad, value_grad


def solution(mesh):
    spec = P(("batch", "seq"), None)
    return jax.shard_map(
        per_device, mesh=mesh, in_specs=(spec,) * 4, out_specs=(spec,) * 4, check_vma=False
    )
```

```python
import jax
import jax.numpy as jnp
from jax import lax
from jax.experimental import pallas as pl
from jax.experimental.pallas import tpu as pltpu
from jax.sharding import PartitionSpec as P

HEADS = 4
HEAD = 128
D = HEADS * HEAD
ROWS = 256
FULL = 2 * D
SCALE = HEAD**-0.5
LOG2E = 1.4426950408889634
EXP_SCALE = SCALE * LOG2E
NEG = -1e30
VMEM_LIMIT = 40 * 1024 * 1024
BF = jnp.bfloat16
F32 = jnp.float32

RUN = 16


def place():
    index = lax.axis_index("seq")
    return lax.rem(index, 2), lax.div(index, 2)


def part(number, size):
    return pl.ds(pl.multiple_of(number * size, size), size)


def head(h):
    return slice(h * HEAD, (h + 1) * HEAD)


def order_matrix(back=False):
    a = lax.broadcasted_iota(jnp.int32, (128, 128), 0)
    b = lax.broadcasted_iota(jnp.int32, (128, 128), 1)
    row, token = (b, a) if back else (a, b)
    hit = row == (token & 7) * RUN + lax.shift_right_logical(token, 3)
    return jnp.where(hit, 1.0, 0.0).astype(BF)


def reorder(matrix, x):
    blocks = [jnp.dot(matrix, x[i : i + 128], preferred_element_type=F32) for i in range(0, x.shape[0], 128)]
    return jnp.concatenate(blocks, axis=0).astype(BF)


def coarse(x):
    rows, lanes = x.shape
    y = x.astype(F32).reshape(rows // (2 * RUN), 2, RUN, lanes)
    return ((y[:, 0] + y[:, 1]) * 0.5).reshape(rows // 2, lanes).astype(BF)


def expand(x, level=1):
    rows, lanes = x.shape
    step = 2**level
    y = jnp.broadcast_to(x.reshape(rows // RUN, 1, RUN, lanes), (rows // RUN, step, RUN, lanes))
    return y.reshape(rows * step, lanes)


def fold(x, level):
    rows, lanes = x.shape
    step = 2**level
    y = x.reshape(rows // (step * RUN), step, RUN, lanes)
    total = y[:, 0]
    for s in range(1, step):
        total = total + y[:, s]
    return total.reshape(rows // step, lanes)


def nt(a, b):
    return lax.dot_general(a, b, (((1,), (1,)), ((), ())), preferred_element_type=F32)


def tn(a, b):
    return lax.dot_general(a, b, (((0,), (0,)), ((), ())), preferred_element_type=F32)


def nn(a, b):
    return jnp.dot(a, b, preferred_element_type=F32)


def lanes128(value):
    return jnp.broadcast_to(value, (value.shape[0], HEAD))


def wide(value, count):
    return value if count == 1 else jnp.concatenate([value] * count, axis=1)


def penalty(ok):
    return jnp.where(ok, 0.0, NEG).astype(F32)


def half_masks():
    row = lax.broadcasted_iota(jnp.int32, (128, 128), 0) >= 64
    key = lax.broadcasted_iota(jnp.int32, (128, 128), 1) >= 64
    left = jnp.where(jnp.logical_and(~row, key), NEG, 0.0).astype(F32)
    right = jnp.where(jnp.logical_and(row, ~key), NEG, 0.0).astype(F32)
    return left, right


def soft(units):
    scores = [nt(q, k) if bias is None else nt(q, k) + bias for q, k, _, bias in units]
    peaks = [jnp.max(s, axis=1, keepdims=True) for s in scores]
    weights = [jnp.exp2((s - peak) * EXP_SCALE) for s, peak in zip(scores, peaks)]
    rounded = [e.astype(BF) for e in weights]
    mixes = [nn(eb, v) for eb, (_, _, v, _) in zip(rounded, units)]
    sums = [jnp.sum(e, axis=1, keepdims=True) for e in weights]
    return [
        (eb, lanes128(peak * EXP_SCALE), lanes128(den), mix)
        for eb, peak, den, mix in zip(rounded, peaks, sums, mixes)
    ]


def backward(units):
    inners = [nt(grad, v) for _, _, v, _, grad, _ in units]
    dvs = [tn(eb, grad) for _, _, _, eb, grad, _ in units]
    dscores = [
        (eb.astype(F32) * (inner - wide(drift, eb.shape[1] // HEAD))).astype(BF)
        for inner, (_, _, _, eb, _, drift) in zip(inners, units)
    ]
    dqs = [nn(dscore, k) * SCALE for dscore, (_, k, _, _, _, _) in zip(dscores, units)]
    dks = [tn(dscore, q) * SCALE for dscore, (q, _, _, _, _, _) in zip(dscores, units)]
    return list(zip(dqs, dks, dvs))


def merge(top, z, y, pieces):
    best = top
    peaks = [expand(m, level) if level else m for m, _, _, level in pieces]
    for m in peaks:
        best = jnp.maximum(best, m)
    f = jnp.exp2(top - best)
    z, y = f * z, f * y
    factors = []
    for m, (_, d, n, level) in zip(peaks, pieces):
        f = jnp.exp2(m - best)
        if level:
            f = f * 2.0**level
            d, n = expand(d, level), expand(n, level)
        factors.append(f)
        z = z + f * d
        y = y + f * n
    return best, z, y, factors


def placed(value, first, rows):
    zeros = jnp.zeros((rows, value.shape[1]), F32)
    return jnp.concatenate([jnp.where(first, value, zeros), jnp.where(first, zeros, value)], axis=0)


def pre_kernel(raw, kv, l1, l3):
    matrix = order_matrix()
    for i in range(2):
        lanes = slice(i * D, (i + 1) * D)
        fine = reorder(matrix, raw[:, lanes])
        kv[:, lanes] = fine
        fine = coarse(fine)
        l1[:, lanes] = fine
        l3[:, lanes] = coarse(coarse(fine))


def pack_kernel(kv, l1, l3, ks, vs, near, s1, msg1, msg2):
    core, _ = place()
    matrix = order_matrix()
    for i, raw in enumerate((ks, vs)):
        lanes = slice(i * D, (i + 1) * D)
        fine = reorder(matrix, raw[...])
        near[:, lanes] = jnp.where(core == 0, fine[:128], fine[128:])
        first = coarse(fine)
        s1[:, lanes] = first
        second = coarse(first)
        msg1[192:, lanes] = second
        msg2[32:, lanes] = coarse(second)
    msg1[:128] = kv[part(core, 128), :]
    msg1[128:192] = l1[part(1 - core, 64), :]
    msg2[:32] = l3[...]


def local_kernel(q_ref, g_ref, kv, near, s1, q0, g0, q1, q2, q3, win, e0, e1, m0, m1, top, zsum, ysum, d1, n1):
    core, _ = place()
    matrix = order_matrix()
    q0[...] = reorder(matrix, q_ref[...])
    g0[...] = reorder(matrix, g_ref[...])
    q1[...] = coarse(q0[...])
    q2[...] = coarse(q1[...])
    q3[...] = coarse(q2[...])
    win[:256] = kv[...]
    win[256:] = near[...]
    left, right = half_masks()
    bias = jnp.where(core == 0, right, left)
    for h in range(HEADS):
        kl, vl = head(h), head(HEADS + h)
        blocks = ((1 - core, 384), (core, 256))
        units = [(q1[:, kl], s1[:, kl], s1[:, vl], bias)]
        units += [(q0[part(n, 128), kl], win[:keys, kl], win[:keys, vl], None) for n, keys in blocks]
        first, *fine = soft(units)
        e1[h], m1[h], d1[h], n1[h] = first
        for i, (number, keys) in enumerate(blocks):
            rows, half = part(number, 128), part(number, 64)
            e, m, d, n = fine[i]
            e0[h, i * 128 : (i + 1) * 128, :keys] = e
            m0[h, i * 128 : (i + 1) * 128] = m
            top[h, rows], zsum[h, rows], ysum[h, rows], _ = merge(
                m, d, n, [(m1[h, half], d1[h, half], n1[h, half], 1)]
            )


def second_split_kernel(r1, after, l1, send):
    core, _ = place()
    l1[part(core, 64), :] = r1[128:192]
    l1[part(1 - core, 64), :] = coarse(r1[:128])
    send[:64] = coarse(l1[...])
    send[64:] = r1[192:]


def forward_kernel(r2, after, send):
    send[...] = r2[...]


def third_split_kernel(r2, r3, after, send):
    send[:64] = r2[...]
    send[64:] = r3[...]


def outer_kernel(q0, q1, r1, l1, top, zsum, ysum, top_out, z_out, y_out, e0, e1, m0, m1, d1, n1):
    core, chip = place()
    is0 = core == 0
    bad = penalty(jnp.where(is0, chip >= 1, chip <= 30))
    left, right = half_masks()
    bias = jnp.where(is0, left, right) + bad
    outer = part(core, 128)
    units = []
    for h in range(HEADS):
        kl, vl = head(h), head(HEADS + h)
        units.append((q1[:, kl], l1[:, kl], l1[:, vl], bias))
        units.append((q0[outer, kl], r1[:128, kl], r1[:128, vl], bad))
    results = soft(units)
    for h in range(HEADS):
        e1[h], m1[h], d1[h], n1[h] = results[2 * h]
        e0[h], m, d, n = results[2 * h + 1]
        m0[h] = m
        for number in (core, 1 - core):
            rows, half = part(number, 128), part(number, 64)
            pieces = [(m1[h, half], d1[h, half], n1[h, half], 1)]
            if number is core:
                pieces.append((m, d, n, 0))
            top_out[h, rows], z_out[h, rows], y_out[h, rows], _ = merge(
                top[h, rows], zsum[h, rows], ysum[h, rows], pieces
            )


def second_kernel(q2, r1, got, top, zsum, ysum, after, win, e2, m2, top_out, z_out, y_out):
    core, chip = place()
    is0 = core == 0
    win[:64] = r1[192:]
    win[64:192] = got[...]
    win[192:] = jnp.zeros((64, FULL), BF)
    lane = lax.broadcasted_iota(jnp.int32, (1, 256), 1)
    left_ok, right_ok = chip >= 1, chip <= 30
    own_bad = penalty(jnp.where(is0, left_ok, right_ok))
    sib_bad = penalty(jnp.where(is0, right_ok, left_ok))
    bias = jnp.where(lane < 64, own_bad, jnp.where(lane < 192, sib_bad, NEG))
    results = soft([(q2[:, head(h)], win[:, head(h)], win[:, head(HEADS + h)], bias) for h in range(HEADS)])
    for h in range(HEADS):
        e2[h], m2[h], d, n = results[h]
        for c in range(2):
            r, a = slice(c * 128, (c + 1) * 128), slice(c * 32, (c + 1) * 32)
            top_out[h, r], z_out[h, r], y_out[h, r], _ = merge(
                top[h, r], zsum[h, r], ysum[h, r], [(m2[h, a], d[a], n[a], 2)]
            )


def far_kernel(
    q2, q3, g_ref, top, zsum, ysum, w2, e2, m2, r2, r3, got,
    att, best_out, inv_out, delta_out, dq2, dq3, own2, own3, cross3, send,
    w3,
):
    core, chip = place()
    is0 = core == 0
    w3[:64] = r2[...]
    w3[64:128] = got[:64]
    w3[128:192] = jnp.where(lax.rem(core + chip, 2) == 1, r3[...], got[64:])
    w3[192:] = jnp.zeros((64, FULL), BF)
    holder = lax.rem(core + chip, 2) == 1
    low2, high2 = chip >= 2, chip <= 29
    even = lax.rem(chip, 2) == 0
    cross_bad = penalty(jnp.where(even, chip <= 28, chip >= 3))
    lane = lax.broadcasted_iota(jnp.int32, (1, 256), 1)
    own_bad = penalty(jnp.where(is0, high2, low2))
    sib_bad = penalty(jnp.where(is0, low2, high2))
    bias3 = jnp.where(
        lane < 64, own_bad, jnp.where(lane < 128, sib_bad, jnp.where(lane < 192, cross_bad, NEG))
    )
    third = soft([(q3[:, head(h)], w3[:, head(h)], w3[:, head(HEADS + h)], bias3) for h in range(HEADS)])
    units = []
    for h in range(HEADS):
        kl, vl = head(h), head(HEADS + h)
        e3, m3, d3, n3 = third[h]
        grads = ([], [])
        drifts = ([], [])
        for c in range(2):
            r = slice(c * 128, (c + 1) * 128)
            a, b = slice(c * 32, (c + 1) * 32), slice(c * 16, (c + 1) * 16)
            best, z, y, factors = merge(top[h, r], zsum[h, r], ysum[h, r], [(m3[b], d3[b], n3[b], 3)])
            inv = 1.0 / z
            y = y * inv
            att[r, kl] = y.astype(BF)
            g = g_ref[r, kl].astype(F32)
            delta = lanes128(jnp.sum(g * y, axis=1, keepdims=True))
            best_out[h, r] = best
            inv_out[h, r] = inv
            delta_out[h, r] = delta
            factors = [4.0 * jnp.exp2(expand(m2[h, a], 2) - best)] + factors
            for i in range(2):
                share = factors[i] * inv
                grads[i].append(fold(share * g, i + 2))
                drifts[i].append(fold(share * delta, i + 2))
        for i, (q, w, e) in enumerate(((q2, w2, e2[h]), (q3, w3, e3))):
            grad = jnp.concatenate(grads[i], axis=0).astype(BF)
            units.append((q[:, kl], w[:, kl], w[:, vl], e, grad, jnp.concatenate(drifts[i], axis=0)))
    results = backward(units)
    for h in range(HEADS):
        for i in range(2):
            dq, dk, dv = results[2 * h + i]
            (dq2, dq3)[i][h] = dq
            for lanes, value in ((head(h), dk), (head(HEADS + h), dv)):
                if i == 0:
                    own2[:, lanes] = value[:64]
                    send[:128, lanes] = value[64:192].astype(BF)
                else:
                    own3[:, lanes] = value[:64]
                    send[128:192, lanes] = value[64:128].astype(BF)
                    cross3[:, lanes] = jnp.where(holder, value[128:160], value[160:192])
                    send[192:, lanes] = jnp.where(holder, value[160:192], value[128:160]).astype(BF)


def coarse_grad(m, best, inv, g, delta):
    grads, drifts = [], []
    for c in range(2):
        r, half = slice(c * 128, (c + 1) * 128), slice(c * 64, (c + 1) * 64)
        share = jnp.exp2(expand(m[half]) - best[r]) * (2.0 * inv[r])
        grads.append(fold(share * g[r].astype(F32), 1))
        drifts.append(fold(share * delta[r], 1))
    return jnp.concatenate(grads, axis=0).astype(BF), jnp.concatenate(drifts, axis=0)


def outer_back_kernel(
    q0, q1, g_ref, r1, l1, e0, e1, m0, m1, best, inv_ref, delta_ref,
    dq0, dq1, d0, d1,
):
    core, _ = place()
    outer = part(core, 128)
    units = []
    for h in range(HEADS):
        kl, vl = head(h), head(HEADS + h)
        share = jnp.exp2(m0[h] - best[h, outer]) * inv_ref[h, outer]
        grad = (share * g_ref[outer, kl].astype(F32)).astype(BF)
        drift = share * delta_ref[h, outer]
        units.append((q0[outer, kl], r1[:128, kl], r1[:128, vl], e0[h], grad, drift))
        grad, drift = coarse_grad(m1[h], best[h], inv_ref[h], g_ref[:, kl], delta_ref[h])
        units.append((q1[:, kl], l1[:, kl], l1[:, vl], e1[h], grad, drift))
    results = backward(units)
    for h in range(HEADS):
        kl, vl = head(h), head(HEADS + h)
        dq0[h], d0[:, kl], d0[:, vl] = results[2 * h]
        dq1[h], d1[:, kl], d1[:, vl] = results[2 * h + 1]


def join_kernel(own2, own3, cross3, d0, d1, got, msg1, msg2, msg3):
    core, _ = place()
    is0 = core == 0
    for j in range(2 * HEADS):
        lanes = head(j)
        msg1[192:, lanes] = (own2[:, lanes] + got[64:128, lanes].astype(F32)).astype(BF)
        first = d1[:, lanes] + expand(0.5 * got[:64, lanes].astype(F32))
        low, high = first[:64], first[64:]
        msg1[128:192, lanes] = jnp.where(is0, low, high).astype(BF)
        msg1[:128, lanes] = (d0[:, lanes] + expand(0.5 * jnp.where(is0, high, low))).astype(BF)
        msg2[:, lanes] = (own3[:, lanes] + got[128:192, lanes].astype(F32)).astype(BF)
        msg3[:, lanes] = (cross3[:, lanes] + got[192:, lanes].astype(F32)).astype(BF)


def rest_kernel(
    q0, q1, g_ref, win, s1, e0, e1, m0, m1, best, inv_ref, delta_ref, dqo0, dqo1, dq2, dq3, att_ref, after,
    att, dq_out, acc, send,
    t0,
):
    core, _ = place()
    is0 = core == 0
    matrix = order_matrix(back=True)
    att[...] = reorder(matrix, att_ref[...])
    for h in range(HEADS):
        kl, vl = head(h), head(HEADS + h)
        grad, drift = coarse_grad(m1[h], best[h], inv_ref[h], g_ref[:, kl], delta_ref[h])
        units = [(q1[:, kl], s1[:, kl], s1[:, vl], e1[h], grad, drift)]
        for i, (number, keys) in enumerate(((1 - core, 384), (core, 256))):
            rows, kept = part(number, 128), slice(i * 128, (i + 1) * 128)
            share = jnp.exp2(m0[h, kept] - best[h, rows]) * inv_ref[h, rows]
            grad = (share * g_ref[rows, kl].astype(F32)).astype(BF)
            drift = share * delta_ref[h, rows]
            units.append((q0[rows, kl], win[:keys, kl], win[:keys, vl], e0[h, kept, :keys], grad, drift))
        (dq, dk, dv), (dq_in, dk_in, dv_in), (dq_out0, dk_out, dv_out) = backward(units)
        t0[h, part(1 - core, 128)] = dq_in
        t0[h, part(core, 128)] = dq_out0 + dqo0[h]
        acc[:, kl] = dk_in[:256] + dk_out
        acc[:, vl] = dv_in[:256] + dv_out
        dq = dq + dqo1[h] + expand(0.5 * (dq2[h] + expand(0.5 * dq3[h])))
        dq_out[:, kl] = reorder(matrix, (t0[h] + expand(0.5 * dq)).astype(BF))
        for lanes, value, fine in ((kl, dk, dk_in), (vl, dv, dv_in)):
            low, high = value[:64], value[64:]
            send[:128, lanes] = (fine[256:] + expand(0.5 * jnp.where(is0, low, high))).astype(BF)
            send[128:, lanes] = jnp.where(is0, high, low).astype(BF)


def add_kernel(own, r1, r2, r3, acc, send):
    core, _ = place()
    is0 = core == 0
    for j in range(2 * HEADS):
        lanes = head(j)
        sib3 = r2[32:, lanes].astype(F32)
        send[:, lanes] = (r1[192:, lanes].astype(F32) + expand(0.5 * sib3)).astype(BF)
        own3 = r2[:32, lanes].astype(F32) + r3[:, lanes].astype(F32)
        first = expand(0.25 * own3, 2) + placed(r1[128:192, lanes].astype(F32), ~is0, 64)
        acc[:, lanes] = own[:, lanes] + expand(0.5 * first) + placed(r1[:128, lanes].astype(F32), is0, 128)


def final_kernel(acc, near, got, dk, dv):
    core, _ = place()
    is0 = core == 0
    matrix = order_matrix(back=True)
    for j in range(2 * HEADS):
        lanes = head(j)
        first = expand(0.5 * got[:, lanes].astype(F32)) + placed(near[128:, lanes].astype(F32), is0, 64)
        total = acc[:, lanes] + expand(0.5 * first) + placed(near[:128, lanes].astype(F32), ~is0, 128)
        (dk if j < HEADS else dv)[:, head(j % HEADS)] = reorder(matrix, total.astype(BF))


SPACES = {"v": pltpu.VMEM, "a": pl.ANY}


def call(kernel, outs, scratch=(), flops=0, specs=None):
    extra = {"in_specs": [pl.BlockSpec(memory_space=SPACES[s]) for s in specs]} if specs else {}
    if flops:
        extra["cost_estimate"] = pl.CostEstimate(flops=flops, bytes_accessed=1 << 20, transcendentals=0)
    return pl.pallas_call(
        kernel,
        out_shape=[jax.ShapeDtypeStruct(shape, dtype) for shape, dtype in outs],
        out_specs=[pl.BlockSpec(memory_space=pltpu.VMEM)] * len(outs),
        scratch_shapes=[s if not isinstance(s, tuple) else pltpu.VMEM(*s) for s in scratch],
        compiler_params=pltpu.CompilerParams(vmem_limit_bytes=VMEM_LIMIT),
        **extra,
    )


def per_device(query, key_rows, value_rows, out_grad):
    count = lax.axis_size("seq")
    sibling = [(i, i + 1) for i in range(0, count, 2)]
    next1 = [(i, i + 1) for i in range(1, count - 1, 2)]
    next2 = [(i, i + 5) for i in range(0, count - 5, 2)]
    forward = [(i, i + 1) for i in range(1, count, 4)]
    next3 = [(i, i + 6) for i in range(count - 6) if (i // 2) % 2 == 0]

    def swap(value, pairs):
        return lax.ppermute(value, "seq", pairs + [(b, a) for a, b in pairs])

    def rows(n, dtype=BF):
        return ((n, FULL), dtype)

    def heads(n, dtype=F32, lanes=HEAD):
        return ((HEADS, n, lanes), dtype)

    stat = heads(256)
    out = ((ROWS, D), BF)
    key_sib = swap(key_rows, sibling)
    value_sib = swap(value_rows, sibling)
    kv, l1, l3 = call(pre_kernel, [rows(256), rows(128), rows(32)])(
        jnp.concatenate([key_rows, value_rows], axis=1)
    )
    near, s1, msg1, msg2 = call(pack_kernel, [rows(128), rows(128), rows(256), rows(64)])(
        kv, l1, l3, key_sib, value_sib
    )
    r2 = swap(msg2, next2)
    r1 = swap(msg1, next1)
    q0, g0, q1, q2, q3, win, e0, e1, m0, m1, top, zsum, ysum = call(
        local_kernel,
        [out, out, ((128, D), BF), ((64, D), BF), ((32, D), BF), rows(384)]
        + [heads(256, BF, 384), heads(128, BF), stat, heads(128), stat, stat, stat],
        [heads(128), heads(128)],
        flops=1 << 31,
    )(query, out_grad, kv, near, s1)
    (send,) = call(forward_kernel, [rows(64)], specs="va")(r2, top)
    r3 = swap(send, forward)
    outer1, send = call(second_split_kernel, [rows(128), rows(128)], specs="va")(r1, top)
    got2 = swap(send, sibling)
    top, zsum, ysum, eo0, eo1, mo0, mo1 = call(
        outer_kernel,
        [stat] * 3 + [heads(128, BF), heads(128, BF), heads(128), heads(128)],
        [heads(128), heads(128)],
        flops=1 << 30,
    )(q0, q1, r1, outer1, top, zsum, ysum)
    (send,) = call(third_split_kernel, [rows(128)], specs="vva")(r2, r3, top)
    got3 = swap(send, sibling)
    w2, e2, m2, top, zsum, ysum = call(
        second_kernel,
        [rows(256), heads(64, BF, 256), heads(64), stat, stat, stat],
        flops=1 << 28,
        specs="v" * 6 + "a",
    )(q2, r1, got2, top, zsum, ysum, send)
    att, best, inv, delta, dq2, dq3, own2, own3, cross3, send = call(
        far_kernel,
        [out, stat, stat, stat, heads(64), heads(32), rows(64, F32), rows(64, F32), rows(32, F32), rows(224)],
        [rows(256)],
    )(q2, q3, g0, top, zsum, ysum, w2, e2, m2, r2, r3, got3)
    got = swap(send, sibling)
    dqo0, dqo1, d0, d1 = call(
        outer_back_kernel, [heads(128), heads(128), rows(128, F32), rows(128, F32)], flops=1 << 30
    )(q0, q1, g0, r1, outer1, eo0, eo1, mo0, mo1, best, inv, delta)
    msg1, msg2, msg3 = call(join_kernel, [rows(256), rows(64), rows(32)])(own2, own3, cross3, d0, d1, got)
    r1 = swap(msg1, next1)
    r2 = swap(msg2, next2)
    r3 = swap(msg3, next3)
    attended, query_grad, acc, send = call(
        rest_kernel,
        [out, out, rows(256, F32), rows(192)],
        [stat],
        flops=1 << 31,
        specs="v" * 17 + "a",
    )(q0, q1, g0, win, s1, e0, e1, m0, m1, best, inv, delta, dqo0, dqo1, dq2, dq3, att, msg1)
    near = swap(send, sibling)
    acc, send = call(add_kernel, [rows(256, F32), rows(64)], flops=1 << 34)(acc, r1, r2, r3)
    got = swap(send, sibling)
    key_grad, value_grad = call(final_kernel, [out, out])(acc, near, got)
    return attended, query_grad, key_grad, value_grad


def solution(mesh):
    spec = P(("batch", "seq"), None)
    return jax.shard_map(
        per_device, mesh=mesh, in_specs=(spec,) * 4, out_specs=(spec,) * 4, check_vma=False
    )
```

```python
import jax
import jax.numpy as jnp
from jax import lax
from jax.experimental import pallas as pl
from jax.experimental.pallas import tpu as pltpu
from jax.sharding import PartitionSpec as P

HEADS = 4
HEAD = 128
D = HEADS * HEAD
ROWS = 256
FULL = 2 * D
SCALE = HEAD**-0.5
LOG2E = 1.4426950408889634
EXP_SCALE = SCALE * LOG2E
NEG = -1e30
VMEM_LIMIT = 40 * 1024 * 1024
BF = jnp.bfloat16
F32 = jnp.float32

RUN = 16


def place():
    index = lax.axis_index("seq")
    return lax.rem(index, 2), lax.div(index, 2)


def part(number, size):
    return pl.ds(pl.multiple_of(number * size, size), size)


def head(h):
    return slice(h * HEAD, (h + 1) * HEAD)


def order_matrix(back=False):
    a = lax.broadcasted_iota(jnp.int32, (128, 128), 0)
    b = lax.broadcasted_iota(jnp.int32, (128, 128), 1)
    row, token = (b, a) if back else (a, b)
    hit = row == (token & 7) * RUN + lax.shift_right_logical(token, 3)
    return jnp.where(hit, 1.0, 0.0).astype(BF)


def reorder(matrix, x):
    blocks = [jnp.dot(matrix, x[i : i + 128], preferred_element_type=F32) for i in range(0, x.shape[0], 128)]
    return jnp.concatenate(blocks, axis=0).astype(BF)


def coarse(x):
    rows, lanes = x.shape
    y = x.astype(F32).reshape(rows // (2 * RUN), 2, RUN, lanes)
    return ((y[:, 0] + y[:, 1]) * 0.5).reshape(rows // 2, lanes).astype(BF)


def expand(x, level=1):
    rows, lanes = x.shape
    step = 2**level
    y = jnp.broadcast_to(x.reshape(rows // RUN, 1, RUN, lanes), (rows // RUN, step, RUN, lanes))
    return y.reshape(rows * step, lanes)


def fold(x, level):
    rows, lanes = x.shape
    step = 2**level
    y = x.reshape(rows // (step * RUN), step, RUN, lanes)
    total = y[:, 0]
    for s in range(1, step):
        total = total + y[:, s]
    return total.reshape(rows // step, lanes)


def nt(a, b):
    return lax.dot_general(a, b, (((1,), (1,)), ((), ())), preferred_element_type=F32)


def tn(a, b):
    return lax.dot_general(a, b, (((0,), (0,)), ((), ())), preferred_element_type=F32)


def nn(a, b):
    return jnp.dot(a, b, preferred_element_type=F32)


def lanes128(value):
    return jnp.broadcast_to(value, (value.shape[0], HEAD))


def wide(value, count):
    return value if count == 1 else jnp.concatenate([value] * count, axis=1)


def penalty(ok):
    return jnp.where(ok, 0.0, NEG).astype(F32)


def half_masks():
    row = lax.broadcasted_iota(jnp.int32, (128, 128), 0) >= 64
    key = lax.broadcasted_iota(jnp.int32, (128, 128), 1) >= 64
    left = jnp.where(jnp.logical_and(~row, key), NEG, 0.0).astype(F32)
    right = jnp.where(jnp.logical_and(row, ~key), NEG, 0.0).astype(F32)
    return left, right


def soft(units):
    scores = [nt(q, k) if bias is None else nt(q, k) + bias for q, k, _, bias in units]
    peaks = [jnp.max(s, axis=1, keepdims=True) for s in scores]
    weights = [jnp.exp2((s - peak) * EXP_SCALE) for s, peak in zip(scores, peaks)]
    rounded = [e.astype(BF) for e in weights]
    mixes = [nn(eb, v) for eb, (_, _, v, _) in zip(rounded, units)]
    sums = [jnp.sum(e, axis=1, keepdims=True) for e in weights]
    return [
        (eb, lanes128(peak * EXP_SCALE), lanes128(den), mix)
        for eb, peak, den, mix in zip(rounded, peaks, sums, mixes)
    ]


def backward(units):
    inners = [nt(grad, v) for _, _, v, _, grad, _ in units]
    dvs = [tn(eb, grad) for _, _, _, eb, grad, _ in units]
    dscores = [
        (eb.astype(F32) * (inner - wide(drift, eb.shape[1] // HEAD))).astype(BF)
        for inner, (_, _, _, eb, _, drift) in zip(inners, units)
    ]
    dqs = [nn(dscore, k) * SCALE for dscore, (_, k, _, _, _, _) in zip(dscores, units)]
    dks = [tn(dscore, q) * SCALE for dscore, (q, _, _, _, _, _) in zip(dscores, units)]
    return list(zip(dqs, dks, dvs))


def merge(top, z, y, pieces):
    best = top
    peaks = [expand(m, level) if level else m for m, _, _, level in pieces]
    for m in peaks:
        best = jnp.maximum(best, m)
    f = jnp.exp2(top - best)
    z, y = f * z, f * y
    factors = []
    for m, (_, d, n, level) in zip(peaks, pieces):
        f = jnp.exp2(m - best)
        if level:
            f = f * 2.0**level
            d, n = expand(d, level), expand(n, level)
        factors.append(f)
        z = z + f * d
        y = y + f * n
    return best, z, y, factors


def placed(value, first, rows):
    zeros = jnp.zeros((rows, value.shape[1]), F32)
    return jnp.concatenate([jnp.where(first, value, zeros), jnp.where(first, zeros, value)], axis=0)


def pre_kernel(raw, kv, l1, l3):
    matrix = order_matrix()
    for i in range(2):
        lanes = slice(i * D, (i + 1) * D)
        fine = reorder(matrix, raw[:, lanes])
        kv[:, lanes] = fine
        fine = coarse(fine)
        l1[:, lanes] = fine
        l3[:, lanes] = coarse(coarse(fine))


def pack_kernel(kv, l1, l3, ks, vs, near, s1, msg1, msg2):
    core, _ = place()
    matrix = order_matrix()
    for i, raw in enumerate((ks, vs)):
        lanes = slice(i * D, (i + 1) * D)
        fine = reorder(matrix, raw[...])
        near[:, lanes] = jnp.where(core == 0, fine[:128], fine[128:])
        first = coarse(fine)
        s1[:, lanes] = first
        second = coarse(first)
        msg1[192:, lanes] = second
        msg2[32:, lanes] = coarse(second)
    msg1[:128] = kv[part(core, 128), :]
    msg1[128:192] = l1[part(1 - core, 64), :]
    msg2[:32] = l3[...]


def local_kernel(q_ref, g_ref, kv, near, s1, q0, g0, q1, q2, q3, win, e0, e1, m0, m1, top, zsum, ysum, d1, n1):
    core, _ = place()
    matrix = order_matrix()
    q0[...] = reorder(matrix, q_ref[...])
    g0[...] = reorder(matrix, g_ref[...])
    q1[...] = coarse(q0[...])
    q2[...] = coarse(q1[...])
    q3[...] = coarse(q2[...])
    win[:256] = kv[...]
    win[256:] = near[...]
    left, right = half_masks()
    bias = jnp.where(core == 0, right, left)
    for h in range(HEADS):
        kl, vl = head(h), head(HEADS + h)
        blocks = ((1 - core, 384), (core, 256))
        units = [(q1[:, kl], s1[:, kl], s1[:, vl], bias)]
        units += [(q0[part(n, 128), kl], win[:keys, kl], win[:keys, vl], None) for n, keys in blocks]
        first, *fine = soft(units)
        e1[h], m1[h], d1[h], n1[h] = first
        for i, (number, keys) in enumerate(blocks):
            rows, half = part(number, 128), part(number, 64)
            e, m, d, n = fine[i]
            e0[h, i * 128 : (i + 1) * 128, :keys] = e
            m0[h, i * 128 : (i + 1) * 128] = m
            top[h, rows], zsum[h, rows], ysum[h, rows], _ = merge(
                m, d, n, [(m1[h, half], d1[h, half], n1[h, half], 1)]
            )


def second_split_kernel(r1, after, l1, send):
    core, _ = place()
    l1[part(core, 64), :] = r1[128:192]
    l1[part(1 - core, 64), :] = coarse(r1[:128])
    send[:64] = coarse(l1[...])
    send[64:] = r1[192:]


def forward_kernel(r2, after, send):
    send[...] = r2[...]


def third_kernel(q3, r2, got2, r3, got3, top, zsum, ysum, w3, e3, m3, top_out, z_out, y_out):
    core, chip = place()
    is0 = core == 0
    w3[:64] = r2[...]
    w3[64:128] = got2[...]
    w3[128:192] = jnp.where(lax.rem(core + chip, 2) == 1, r3[...], got3[...])
    w3[192:] = jnp.zeros((64, FULL), BF)
    low2, high2 = chip >= 2, chip <= 29
    even = lax.rem(chip, 2) == 0
    cross_bad = penalty(jnp.where(even, chip <= 28, chip >= 3))
    lane = lax.broadcasted_iota(jnp.int32, (1, 256), 1)
    own_bad = penalty(jnp.where(is0, high2, low2))
    sib_bad = penalty(jnp.where(is0, low2, high2))
    bias = jnp.where(
        lane < 64, own_bad, jnp.where(lane < 128, sib_bad, jnp.where(lane < 192, cross_bad, NEG))
    )
    results = soft([(q3[:, head(h)], w3[:, head(h)], w3[:, head(HEADS + h)], bias) for h in range(HEADS)])
    for h in range(HEADS):
        e3[h], m3[h], d, n = results[h]
        for c in range(2):
            r, a = slice(c * 128, (c + 1) * 128), slice(c * 16, (c + 1) * 16)
            top_out[h, r], z_out[h, r], y_out[h, r], _ = merge(
                top[h, r], zsum[h, r], ysum[h, r], [(m3[h, a], d[a], n[a], 3)]
            )


def outer_kernel(q0, q1, r1, l1, top, zsum, ysum, top_out, z_out, y_out, e0, e1, m0, m1, d1, n1):
    core, chip = place()
    is0 = core == 0
    bad = penalty(jnp.where(is0, chip >= 1, chip <= 30))
    left, right = half_masks()
    bias = jnp.where(is0, left, right) + bad
    outer = part(core, 128)
    units = []
    for h in range(HEADS):
        kl, vl = head(h), head(HEADS + h)
        units.append((q1[:, kl], l1[:, kl], l1[:, vl], bias))
        units.append((q0[outer, kl], r1[:128, kl], r1[:128, vl], bad))
    results = soft(units)
    for h in range(HEADS):
        e1[h], m1[h], d1[h], n1[h] = results[2 * h]
        e0[h], m, d, n = results[2 * h + 1]
        m0[h] = m
        for number in (core, 1 - core):
            rows, half = part(number, 128), part(number, 64)
            pieces = [(m1[h, half], d1[h, half], n1[h, half], 1)]
            if number is core:
                pieces.append((m, d, n, 0))
            top_out[h, rows], z_out[h, rows], y_out[h, rows], _ = merge(
                top[h, rows], zsum[h, rows], ysum[h, rows], pieces
            )


def second_kernel(q2, r1, got, top, zsum, ysum, win, e2, m2, top_out, z_out, y_out):
    core, chip = place()
    is0 = core == 0
    win[:64] = r1[192:]
    win[64:192] = got[...]
    win[192:] = jnp.zeros((64, FULL), BF)
    lane = lax.broadcasted_iota(jnp.int32, (1, 256), 1)
    left_ok, right_ok = chip >= 1, chip <= 30
    own_bad = penalty(jnp.where(is0, left_ok, right_ok))
    sib_bad = penalty(jnp.where(is0, right_ok, left_ok))
    bias = jnp.where(lane < 64, own_bad, jnp.where(lane < 192, sib_bad, NEG))
    results = soft([(q2[:, head(h)], win[:, head(h)], win[:, head(HEADS + h)], bias) for h in range(HEADS)])
    for h in range(HEADS):
        e2[h], m2[h], d, n = results[h]
        for c in range(2):
            r, a = slice(c * 128, (c + 1) * 128), slice(c * 32, (c + 1) * 32)
            top_out[h, r], z_out[h, r], y_out[h, r], _ = merge(
                top[h, r], zsum[h, r], ysum[h, r], [(m2[h, a], d[a], n[a], 2)]
            )


def far_kernel(
    q2, q3, g_ref, top, zsum, ysum, w2, e2, m2, w3, e3, m3,
    att, inv_out, delta_out, dq2, dq3, own2, own3, cross3, send,
):
    core, chip = place()
    holder = lax.rem(core + chip, 2) == 1
    units = []
    for h in range(HEADS):
        kl, vl = head(h), head(HEADS + h)
        grads = ([], [])
        drifts = ([], [])
        for c in range(2):
            r = slice(c * 128, (c + 1) * 128)
            a, b = slice(c * 32, (c + 1) * 32), slice(c * 16, (c + 1) * 16)
            best = top[h, r]
            inv = 1.0 / zsum[h, r]
            y = ysum[h, r] * inv
            att[r, kl] = y.astype(BF)
            g = g_ref[r, kl].astype(F32)
            delta = lanes128(jnp.sum(g * y, axis=1, keepdims=True))
            inv_out[h, r] = inv
            delta_out[h, r] = delta
            for i, (m, rows) in enumerate(((m2, a), (m3, b))):
                share = jnp.exp2(expand(m[h, rows], i + 2) - best) * (2.0 ** (i + 2) * inv)
                grads[i].append(fold(share * g, i + 2))
                drifts[i].append(fold(share * delta, i + 2))
        for i, (q, w, e) in enumerate(((q2, w2, e2[h]), (q3, w3, e3[h]))):
            grad = jnp.concatenate(grads[i], axis=0).astype(BF)
            units.append((q[:, kl], w[:, kl], w[:, vl], e, grad, jnp.concatenate(drifts[i], axis=0)))
    results = backward(units)
    for h in range(HEADS):
        for i in range(2):
            dq, dk, dv = results[2 * h + i]
            (dq2, dq3)[i][h] = dq
            for lanes, value in ((head(h), dk), (head(HEADS + h), dv)):
                if i == 0:
                    own2[:, lanes] = value[:64]
                    send[:128, lanes] = value[64:192].astype(BF)
                else:
                    own3[:, lanes] = value[:64]
                    send[128:192, lanes] = value[64:128].astype(BF)
                    cross3[:, lanes] = jnp.where(holder, value[128:160], value[160:192])
                    send[192:, lanes] = jnp.where(holder, value[160:192], value[128:160]).astype(BF)


def coarse_grad(m, best, inv, g, delta):
    grads, drifts = [], []
    for c in range(2):
        r, half = slice(c * 128, (c + 1) * 128), slice(c * 64, (c + 1) * 64)
        share = jnp.exp2(expand(m[half]) - best[r]) * (2.0 * inv[r])
        grads.append(fold(share * g[r].astype(F32), 1))
        drifts.append(fold(share * delta[r], 1))
    return jnp.concatenate(grads, axis=0).astype(BF), jnp.concatenate(drifts, axis=0)


def outer_back_kernel(
    q0, q1, g_ref, r1, l1, e0, e1, m0, m1, best, inv_ref, delta_ref,
    dq0, dq1, d0, d1,
):
    core, _ = place()
    outer = part(core, 128)
    units = []
    for h in range(HEADS):
        kl, vl = head(h), head(HEADS + h)
        share = jnp.exp2(m0[h] - best[h, outer]) * inv_ref[h, outer]
        grad = (share * g_ref[outer, kl].astype(F32)).astype(BF)
        drift = share * delta_ref[h, outer]
        units.append((q0[outer, kl], r1[:128, kl], r1[:128, vl], e0[h], grad, drift))
        grad, drift = coarse_grad(m1[h], best[h], inv_ref[h], g_ref[:, kl], delta_ref[h])
        units.append((q1[:, kl], l1[:, kl], l1[:, vl], e1[h], grad, drift))
    results = backward(units)
    for h in range(HEADS):
        kl, vl = head(h), head(HEADS + h)
        dq0[h], d0[:, kl], d0[:, vl] = results[2 * h]
        dq1[h], d1[:, kl], d1[:, vl] = results[2 * h + 1]


def join_kernel(own2, own3, cross3, d0, d1, got, msg1, msg2, msg3):
    core, _ = place()
    is0 = core == 0
    for j in range(2 * HEADS):
        lanes = head(j)
        msg1[192:, lanes] = (own2[:, lanes] + got[64:128, lanes].astype(F32)).astype(BF)
        first = d1[:, lanes] + expand(0.5 * got[:64, lanes].astype(F32))
        low, high = first[:64], first[64:]
        msg1[128:192, lanes] = jnp.where(is0, low, high).astype(BF)
        msg1[:128, lanes] = (d0[:, lanes] + expand(0.5 * jnp.where(is0, high, low))).astype(BF)
        msg2[:, lanes] = (own3[:, lanes] + got[128:192, lanes].astype(F32)).astype(BF)
        msg3[:, lanes] = (cross3[:, lanes] + got[192:, lanes].astype(F32)).astype(BF)


def rest_kernel(
    q0, q1, g_ref, win, s1, e0, e1, m0, m1, best, inv_ref, delta_ref, dqo0, dqo1, dq2, dq3, att_ref, after,
    att, dq_out, acc, send,
    t0,
):
    core, _ = place()
    is0 = core == 0
    matrix = order_matrix(back=True)
    att[...] = reorder(matrix, att_ref[...])
    for h in range(HEADS):
        kl, vl = head(h), head(HEADS + h)
        grad, drift = coarse_grad(m1[h], best[h], inv_ref[h], g_ref[:, kl], delta_ref[h])
        units = [(q1[:, kl], s1[:, kl], s1[:, vl], e1[h], grad, drift)]
        for i, (number, keys) in enumerate(((1 - core, 384), (core, 256))):
            rows, kept = part(number, 128), slice(i * 128, (i + 1) * 128)
            share = jnp.exp2(m0[h, kept] - best[h, rows]) * inv_ref[h, rows]
            grad = (share * g_ref[rows, kl].astype(F32)).astype(BF)
            drift = share * delta_ref[h, rows]
            units.append((q0[rows, kl], win[:keys, kl], win[:keys, vl], e0[h, kept, :keys], grad, drift))
        (dq, dk, dv), (dq_in, dk_in, dv_in), (dq_out0, dk_out, dv_out) = backward(units)
        t0[h, part(1 - core, 128)] = dq_in
        t0[h, part(core, 128)] = dq_out0 + dqo0[h]
        acc[:, kl] = dk_in[:256] + dk_out
        acc[:, vl] = dv_in[:256] + dv_out
        dq = dq + dqo1[h] + expand(0.5 * (dq2[h] + expand(0.5 * dq3[h])))
        dq_out[:, kl] = reorder(matrix, (t0[h] + expand(0.5 * dq)).astype(BF))
        for lanes, value, fine in ((kl, dk, dk_in), (vl, dv, dv_in)):
            low, high = value[:64], value[64:]
            send[:128, lanes] = (fine[256:] + expand(0.5 * jnp.where(is0, low, high))).astype(BF)
            send[128:, lanes] = jnp.where(is0, high, low).astype(BF)


def add_kernel(own, r1, r2, r3, acc, send):
    core, _ = place()
    is0 = core == 0
    for j in range(2 * HEADS):
        lanes = head(j)
        sib3 = r2[32:, lanes].astype(F32)
        send[:, lanes] = (r1[192:, lanes].astype(F32) + expand(0.5 * sib3)).astype(BF)
        own3 = r2[:32, lanes].astype(F32) + r3[:, lanes].astype(F32)
        first = expand(0.25 * own3, 2) + placed(r1[128:192, lanes].astype(F32), ~is0, 64)
        acc[:, lanes] = own[:, lanes] + expand(0.5 * first) + placed(r1[:128, lanes].astype(F32), is0, 128)


def final_kernel(acc, near, got, dk, dv):
    core, _ = place()
    is0 = core == 0
    matrix = order_matrix(back=True)
    for j in range(2 * HEADS):
        lanes = head(j)
        first = expand(0.5 * got[:, lanes].astype(F32)) + placed(near[128:, lanes].astype(F32), is0, 64)
        total = acc[:, lanes] + expand(0.5 * first) + placed(near[:128, lanes].astype(F32), ~is0, 128)
        (dk if j < HEADS else dv)[:, head(j % HEADS)] = reorder(matrix, total.astype(BF))


SPACES = {"v": pltpu.VMEM, "a": pl.ANY}


def call(kernel, outs, scratch=(), flops=0, specs=None):
    extra = {"in_specs": [pl.BlockSpec(memory_space=SPACES[s]) for s in specs]} if specs else {}
    if flops:
        extra["cost_estimate"] = pl.CostEstimate(flops=flops, bytes_accessed=1 << 20, transcendentals=0)
    return pl.pallas_call(
        kernel,
        out_shape=[jax.ShapeDtypeStruct(shape, dtype) for shape, dtype in outs],
        out_specs=[pl.BlockSpec(memory_space=pltpu.VMEM)] * len(outs),
        scratch_shapes=[s if not isinstance(s, tuple) else pltpu.VMEM(*s) for s in scratch],
        compiler_params=pltpu.CompilerParams(vmem_limit_bytes=VMEM_LIMIT),
        **extra,
    )


def per_device(query, key_rows, value_rows, out_grad):
    count = lax.axis_size("seq")
    sibling = [(i, i + 1) for i in range(0, count, 2)]
    next1 = [(i, i + 1) for i in range(1, count - 1, 2)]
    next2 = [(i, i + 5) for i in range(0, count - 5, 2)]
    forward = [(i, i + 1) for i in range(1, count, 4)]
    next3 = [(i, i + 6) for i in range(count - 6) if (i // 2) % 2 == 0]

    def swap(value, pairs):
        return lax.ppermute(value, "seq", pairs + [(b, a) for a, b in pairs])

    def rows(n, dtype=BF):
        return ((n, FULL), dtype)

    def heads(n, dtype=F32, lanes=HEAD):
        return ((HEADS, n, lanes), dtype)

    stat = heads(256)
    out = ((ROWS, D), BF)
    key_sib = swap(key_rows, sibling)
    value_sib = swap(value_rows, sibling)
    kv, l1, l3 = call(pre_kernel, [rows(256), rows(128), rows(32)])(
        jnp.concatenate([key_rows, value_rows], axis=1)
    )
    near, s1, msg1, msg2 = call(pack_kernel, [rows(128), rows(128), rows(256), rows(64)])(
        kv, l1, l3, key_sib, value_sib
    )
    r2 = swap(msg2, next2)
    r1 = swap(msg1, next1)
    q0, g0, q1, q2, q3, win, e0, e1, m0, m1, top, zsum, ysum = call(
        local_kernel,
        [out, out, ((128, D), BF), ((64, D), BF), ((32, D), BF), rows(384)]
        + [heads(256, BF, 384), heads(128, BF), stat, heads(128), stat, stat, stat],
        [heads(128), heads(128)],
        flops=1 << 33,
    )(query, out_grad, kv, near, s1)
    (send,) = call(forward_kernel, [rows(64)], specs="va")(r2, top)
    r3 = swap(send, forward)
    got2 = swap(send, sibling)
    got3 = swap(r3, sibling)
    w3, e3, m3, top, zsum, ysum = call(
        third_kernel,
        [rows(256), heads(32, BF, 256), heads(32), stat, stat, stat],
        flops=1 << 28,
    )(q3, r2, got2, r3, got3, top, zsum, ysum)
    outer1, send = call(second_split_kernel, [rows(128), rows(128)], specs="va")(r1, top)
    got2 = swap(send, sibling)
    top, zsum, ysum, eo0, eo1, mo0, mo1 = call(
        outer_kernel,
        [stat] * 3 + [heads(128, BF), heads(128, BF), heads(128), heads(128)],
        [heads(128), heads(128)],
        flops=1 << 30,
    )(q0, q1, r1, outer1, top, zsum, ysum)
    w2, e2, m2, top, zsum, ysum = call(
        second_kernel,
        [rows(256), heads(64, BF, 256), heads(64), stat, stat, stat],
        flops=1 << 28,
    )(q2, r1, got2, top, zsum, ysum)
    att, inv, delta, dq2, dq3, own2, own3, cross3, send = call(
        far_kernel,
        [out, stat, stat, heads(64), heads(32), rows(64, F32), rows(64, F32), rows(32, F32), rows(224)],
    )(q2, q3, g0, top, zsum, ysum, w2, e2, m2, w3, e3, m3)
    got = swap(send, sibling)
    dqo0, dqo1, d0, d1 = call(
        outer_back_kernel, [heads(128), heads(128), rows(128, F32), rows(128, F32)], flops=1 << 30
    )(q0, q1, g0, r1, outer1, eo0, eo1, mo0, mo1, top, inv, delta)
    msg1, msg2, msg3 = call(join_kernel, [rows(256), rows(64), rows(32)])(own2, own3, cross3, d0, d1, got)
    r1 = swap(msg1, next1)
    r2 = swap(msg2, next2)
    r3 = swap(msg3, next3)
    attended, query_grad, acc, send = call(
        rest_kernel,
        [out, out, rows(256, F32), rows(192)],
        [stat],
        flops=1 << 31,
        specs="v" * 17 + "a",
    )(q0, q1, g0, win, s1, e0, e1, m0, m1, top, inv, delta, dqo0, dqo1, dq2, dq3, att, msg1)
    near = swap(send, sibling)
    acc, send = call(add_kernel, [rows(256, F32), rows(64)], flops=1 << 34)(acc, r1, r2, r3)
    got = swap(send, sibling)
    key_grad, value_grad = call(final_kernel, [out, out])(acc, near, got)
    return attended, query_grad, key_grad, value_grad


def solution(mesh):
    spec = P(("batch", "seq"), None)
    return jax.shard_map(
        per_device, mesh=mesh, in_specs=(spec,) * 4, out_specs=(spec,) * 4, check_vma=False
    )
```

```python
import jax
import jax.numpy as jnp
from jax import lax
from jax.experimental import pallas as pl
from jax.experimental.pallas import tpu as pltpu
from jax.sharding import PartitionSpec as P

HEADS = 4
HEAD = 128
D = HEADS * HEAD
ROWS = 256
FULL = 2 * D
SCALE = HEAD**-0.5
LOG2E = 1.4426950408889634
EXP_SCALE = SCALE * LOG2E
NEG = -1e30
VMEM_LIMIT = 40 * 1024 * 1024
BF = jnp.bfloat16
F32 = jnp.float32

RUN = 16


def place():
    index = lax.axis_index("seq")
    return lax.rem(index, 2), lax.div(index, 2)


def part(number, size):
    return pl.ds(pl.multiple_of(number * size, size), size)


def head(h):
    return slice(h * HEAD, (h + 1) * HEAD)


def order_matrix(back=False):
    a = lax.broadcasted_iota(jnp.int32, (128, 128), 0)
    b = lax.broadcasted_iota(jnp.int32, (128, 128), 1)
    row, token = (b, a) if back else (a, b)
    hit = row == (token & 7) * RUN + lax.shift_right_logical(token, 3)
    return jnp.where(hit, 1.0, 0.0).astype(BF)


def reorder(matrix, x):
    blocks = [jnp.dot(matrix, x[i : i + 128], preferred_element_type=F32) for i in range(0, x.shape[0], 128)]
    return jnp.concatenate(blocks, axis=0).astype(BF)


def coarse(x):
    rows, lanes = x.shape
    y = x.astype(F32).reshape(rows // (2 * RUN), 2, RUN, lanes)
    return ((y[:, 0] + y[:, 1]) * 0.5).reshape(rows // 2, lanes).astype(BF)


def expand(x, level=1):
    rows, lanes = x.shape
    step = 2**level
    y = jnp.broadcast_to(x.reshape(rows // RUN, 1, RUN, lanes), (rows // RUN, step, RUN, lanes))
    return y.reshape(rows * step, lanes)


def fold(x, level):
    rows, lanes = x.shape
    step = 2**level
    y = x.reshape(rows // (step * RUN), step, RUN, lanes)
    total = y[:, 0]
    for s in range(1, step):
        total = total + y[:, s]
    return total.reshape(rows // step, lanes)


def nt(a, b):
    return lax.dot_general(a, b, (((1,), (1,)), ((), ())), preferred_element_type=F32)


def tn(a, b):
    return lax.dot_general(a, b, (((0,), (0,)), ((), ())), preferred_element_type=F32)


def nn(a, b):
    return jnp.dot(a, b, preferred_element_type=F32)


def lanes128(value):
    return jnp.broadcast_to(value, (value.shape[0], HEAD))


def wide(value, lanes):
    pieces = [value[:, : min(HEAD, lanes - i)] for i in range(0, lanes, HEAD)]
    return pieces[0] if len(pieces) == 1 else jnp.concatenate(pieces, axis=1)


def penalty(ok):
    return jnp.where(ok, 0.0, NEG).astype(F32)


def half_masks():
    row = lax.broadcasted_iota(jnp.int32, (128, 128), 0) >= 64
    key = lax.broadcasted_iota(jnp.int32, (128, 128), 1) >= 64
    left = jnp.where(jnp.logical_and(~row, key), NEG, 0.0).astype(F32)
    right = jnp.where(jnp.logical_and(row, ~key), NEG, 0.0).astype(F32)
    return left, right


def soft(units):
    scores = [nt(q, k) if bias is None else nt(q, k) + bias for q, k, _, bias in units]
    peaks = [jnp.max(s, axis=1, keepdims=True) for s in scores]
    weights = [jnp.exp2((s - peak) * EXP_SCALE) for s, peak in zip(scores, peaks)]
    rounded = [e.astype(BF) for e in weights]
    mixes = [nn(eb, v) for eb, (_, _, v, _) in zip(rounded, units)]
    sums = [jnp.sum(e, axis=1, keepdims=True) for e in weights]
    return [
        (eb, lanes128(peak * EXP_SCALE), lanes128(den), mix)
        for eb, peak, den, mix in zip(rounded, peaks, sums, mixes)
    ]


def backward(units):
    inners = [nt(grad, v) for _, _, v, _, grad, _ in units]
    dvs = [tn(eb, grad) for _, _, _, eb, grad, _ in units]
    dscores = [
        (eb.astype(F32) * (inner - wide(drift, eb.shape[1]))).astype(BF)
        for inner, (_, _, _, eb, _, drift) in zip(inners, units)
    ]
    dqs = [nn(dscore, k) * SCALE for dscore, (_, k, _, _, _, _) in zip(dscores, units)]
    dks = [tn(dscore, q) * SCALE for dscore, (q, _, _, _, _, _) in zip(dscores, units)]
    return list(zip(dqs, dks, dvs))


def merge(top, z, y, pieces):
    best = top
    peaks = [expand(m, level) if level else m for m, _, _, level in pieces]
    for m in peaks:
        best = jnp.maximum(best, m)
    f = jnp.exp2(top - best)
    z, y = f * z, f * y
    factors = []
    for m, (_, d, n, level) in zip(peaks, pieces):
        f = jnp.exp2(m - best)
        if level:
            f = f * 2.0**level
            d, n = expand(d, level), expand(n, level)
        factors.append(f)
        z = z + f * d
        y = y + f * n
    return best, z, y, factors


def placed(value, first, rows):
    zeros = jnp.zeros((rows, value.shape[1]), F32)
    return jnp.concatenate([jnp.where(first, value, zeros), jnp.where(first, zeros, value)], axis=0)


def pre_kernel(raw, kv, l1, l3):
    matrix = order_matrix()
    for i in range(2):
        lanes = slice(i * D, (i + 1) * D)
        fine = reorder(matrix, raw[:, lanes])
        kv[:, lanes] = fine
        fine = coarse(fine)
        l1[:, lanes] = fine
        l3[:, lanes] = coarse(coarse(fine))


def pack_kernel(kv, l1, l3, ks, vs, near, s1, msg1, msg2):
    core, _ = place()
    matrix = order_matrix()
    for i, raw in enumerate((ks, vs)):
        lanes = slice(i * D, (i + 1) * D)
        fine = reorder(matrix, raw[...])
        near[:, lanes] = jnp.where(core == 0, fine[:128], fine[128:])
        first = coarse(fine)
        s1[:, lanes] = first
        second = coarse(first)
        msg1[192:, lanes] = second
        msg2[32:, lanes] = coarse(second)
    msg1[:128] = kv[part(core, 128), :]
    msg1[128:192] = l1[part(1 - core, 64), :]
    msg2[:32] = l3[...]


def local_kernel(q_ref, g_ref, kv, near, s1, q0, g0, q1, q2, q3, win, e0, e1, m0, m1, top, zsum, ysum, d1, n1):
    core, _ = place()
    matrix = order_matrix()
    q0[...] = reorder(matrix, q_ref[...])
    g0[...] = reorder(matrix, g_ref[...])
    q1[...] = coarse(q0[...])
    q2[...] = coarse(q1[...])
    q3[...] = coarse(q2[...])
    win[:256] = kv[...]
    win[256:] = near[...]
    left, right = half_masks()
    bias = jnp.where(core == 0, right, left)
    for h in range(HEADS):
        kl, vl = head(h), head(HEADS + h)
        blocks = ((1 - core, 384), (core, 256))
        units = [(q1[:, kl], s1[:, kl], s1[:, vl], bias)]
        units += [(q0[part(n, 128), kl], win[:keys, kl], win[:keys, vl], None) for n, keys in blocks]
        first, *fine = soft(units)
        e1[h], m1[h], d1[h], n1[h] = first
        for i, (number, keys) in enumerate(blocks):
            rows, half = part(number, 128), part(number, 64)
            e, m, d, n = fine[i]
            e0[h, i * 128 : (i + 1) * 128, :keys] = e
            m0[h, i * 128 : (i + 1) * 128] = m
            top[h, rows], zsum[h, rows], ysum[h, rows], _ = merge(
                m, d, n, [(m1[h, half], d1[h, half], n1[h, half], 1)]
            )


def second_split_kernel(r1, after, l1, send):
    core, _ = place()
    l1[part(core, 64), :] = r1[128:192]
    l1[part(1 - core, 64), :] = coarse(r1[:128])
    send[:64] = coarse(l1[...])
    send[64:] = r1[192:]


def third_split_kernel(r2, r3, after, send):
    send[:64] = r2[...]
    send[64:] = r3[...]


def outer_kernel(q0, q1, r1, l1, top, zsum, ysum, top_out, z_out, y_out, e0, e1, m0, m1, d1, n1):
    core, chip = place()
    is0 = core == 0
    bad = penalty(jnp.where(is0, chip >= 1, chip <= 30))
    left, right = half_masks()
    bias = jnp.where(is0, left, right) + bad
    outer = part(core, 128)
    units = []
    for h in range(HEADS):
        kl, vl = head(h), head(HEADS + h)
        units.append((q1[:, kl], l1[:, kl], l1[:, vl], bias))
        units.append((q0[outer, kl], r1[:128, kl], r1[:128, vl], bad))
    results = soft(units)
    for h in range(HEADS):
        e1[h], m1[h], d1[h], n1[h] = results[2 * h]
        e0[h], m, d, n = results[2 * h + 1]
        m0[h] = m
        for number in (core, 1 - core):
            rows, half = part(number, 128), part(number, 64)
            pieces = [(m1[h, half], d1[h, half], n1[h, half], 1)]
            if number is core:
                pieces.append((m, d, n, 0))
            top_out[h, rows], z_out[h, rows], y_out[h, rows], _ = merge(
                top[h, rows], zsum[h, rows], ysum[h, rows], pieces
            )


def far_kernel(
    q2, q3, g_ref, top, zsum, ysum, r1, got2, r2, r3, got3,
    att, best_out, inv_out, delta_out, dq2, dq3, own2, own3, cross3, send,
    w2, w3,
):
    core, chip = place()
    is0 = core == 0
    holder = lax.rem(core + chip, 2) == 1
    w2[:128] = got2[...]
    w2[128:] = r1[192:]
    w3[:64] = r2[...]
    w3[64:128] = got3[:64]
    w3[128:] = jnp.where(holder, r3[...], got3[64:])
    left_ok, right_ok = chip >= 1, chip <= 30
    low2, high2 = chip >= 2, chip <= 29
    even = lax.rem(chip, 2) == 0
    lane = lax.broadcasted_iota(jnp.int32, (1, 192), 1)
    own_bad = penalty(jnp.where(is0, left_ok, right_ok))
    sib_bad = penalty(jnp.where(is0, right_ok, left_ok))
    bias2 = jnp.where(lane < 128, sib_bad, own_bad)
    cross_bad = penalty(jnp.where(even, chip <= 28, chip >= 3))
    own_bad = penalty(jnp.where(is0, high2, low2))
    sib_bad = penalty(jnp.where(is0, low2, high2))
    bias3 = jnp.where(lane < 64, own_bad, jnp.where(lane < 128, sib_bad, cross_bad))
    units = []
    for h in range(HEADS):
        kl, vl = head(h), head(HEADS + h)
        units.append((q2[:, kl], w2[:, kl], w2[:, vl], bias2))
        units.append((q3[:, kl], w3[:, kl], w3[:, vl], bias3))
    results = soft(units)
    units = []
    for h in range(HEADS):
        kl, vl = head(h), head(HEADS + h)
        (e2, m2, d2, n2), (e3, m3, d3, n3) = results[2 * h : 2 * h + 2]
        grads = ([], [])
        drifts = ([], [])
        for c in range(2):
            r = slice(c * 128, (c + 1) * 128)
            a, b = slice(c * 32, (c + 1) * 32), slice(c * 16, (c + 1) * 16)
            pieces = [(m2[a], d2[a], n2[a], 2), (m3[b], d3[b], n3[b], 3)]
            best, z, y, factors = merge(top[h, r], zsum[h, r], ysum[h, r], pieces)
            inv = 1.0 / z
            y = y * inv
            att[r, kl] = y.astype(BF)
            g = g_ref[r, kl].astype(F32)
            delta = lanes128(jnp.sum(g * y, axis=1, keepdims=True))
            best_out[h, r] = best
            inv_out[h, r] = inv
            delta_out[h, r] = delta
            for i in range(2):
                share = factors[i] * inv
                grads[i].append(fold(share * g, i + 2))
                drifts[i].append(fold(share * delta, i + 2))
        for i, (q, w, e) in enumerate(((q2, w2, e2), (q3, w3, e3))):
            grad = jnp.concatenate(grads[i], axis=0).astype(BF)
            units.append((q[:, kl], w[:, kl], w[:, vl], e, grad, jnp.concatenate(drifts[i], axis=0)))
    results = backward(units)
    for h in range(HEADS):
        for i in range(2):
            dq, dk, dv = results[2 * h + i]
            (dq2, dq3)[i][h] = dq
            for lanes, value in ((head(h), dk), (head(HEADS + h), dv)):
                if i == 0:
                    send[:128, lanes] = value[:128].astype(BF)
                    own2[:, lanes] = value[128:]
                else:
                    own3[:, lanes] = value[:64]
                    send[128:192, lanes] = value[64:128].astype(BF)
                    cross3[:, lanes] = jnp.where(holder, value[128:160], value[160:])
                    send[192:, lanes] = jnp.where(holder, value[160:], value[128:160]).astype(BF)


def coarse_grad(m, best, inv, g, delta):
    grads, drifts = [], []
    for c in range(2):
        r, half = slice(c * 128, (c + 1) * 128), slice(c * 64, (c + 1) * 64)
        share = jnp.exp2(expand(m[half]) - best[r]) * (2.0 * inv[r])
        grads.append(fold(share * g[r].astype(F32), 1))
        drifts.append(fold(share * delta[r], 1))
    return jnp.concatenate(grads, axis=0).astype(BF), jnp.concatenate(drifts, axis=0)


def outer_back_kernel(
    q0, q1, g_ref, r1, l1, e0, e1, m0, m1, best, inv_ref, delta_ref,
    dq0, dq1, d0, d1,
):
    core, _ = place()
    outer = part(core, 128)
    units = []
    for h in range(HEADS):
        kl, vl = head(h), head(HEADS + h)
        share = jnp.exp2(m0[h] - best[h, outer]) * inv_ref[h, outer]
        grad = (share * g_ref[outer, kl].astype(F32)).astype(BF)
        drift = share * delta_ref[h, outer]
        units.append((q0[outer, kl], r1[:128, kl], r1[:128, vl], e0[h], grad, drift))
        grad, drift = coarse_grad(m1[h], best[h], inv_ref[h], g_ref[:, kl], delta_ref[h])
        units.append((q1[:, kl], l1[:, kl], l1[:, vl], e1[h], grad, drift))
    results = backward(units)
    for h in range(HEADS):
        kl, vl = head(h), head(HEADS + h)
        dq0[h], d0[:, kl], d0[:, vl] = results[2 * h]
        dq1[h], d1[:, kl], d1[:, vl] = results[2 * h + 1]


def join_kernel(own2, own3, cross3, d0, d1, got, msg1, msg2, msg3):
    core, _ = place()
    is0 = core == 0
    for j in range(2 * HEADS):
        lanes = head(j)
        msg1[192:, lanes] = (own2[:, lanes] + got[64:128, lanes].astype(F32)).astype(BF)
        first = d1[:, lanes] + expand(0.5 * got[:64, lanes].astype(F32))
        low, high = first[:64], first[64:]
        msg1[128:192, lanes] = jnp.where(is0, low, high).astype(BF)
        msg1[:128, lanes] = (d0[:, lanes] + expand(0.5 * jnp.where(is0, high, low))).astype(BF)
        msg2[:, lanes] = (own3[:, lanes] + got[128:192, lanes].astype(F32)).astype(BF)
        msg3[:, lanes] = (cross3[:, lanes] + got[192:, lanes].astype(F32)).astype(BF)


def rest_kernel(
    q0, q1, g_ref, win, s1, e0, e1, m0, m1, best, inv_ref, delta_ref, dqo0, dqo1, dq2, dq3, att_ref, after,
    att, dq_out, acc, send,
    t0,
):
    core, _ = place()
    is0 = core == 0
    matrix = order_matrix(back=True)
    att[...] = reorder(matrix, att_ref[...])
    for h in range(HEADS):
        kl, vl = head(h), head(HEADS + h)
        grad, drift = coarse_grad(m1[h], best[h], inv_ref[h], g_ref[:, kl], delta_ref[h])
        units = [(q1[:, kl], s1[:, kl], s1[:, vl], e1[h], grad, drift)]
        for i, (number, keys) in enumerate(((1 - core, 384), (core, 256))):
            rows, kept = part(number, 128), slice(i * 128, (i + 1) * 128)
            share = jnp.exp2(m0[h, kept] - best[h, rows]) * inv_ref[h, rows]
            grad = (share * g_ref[rows, kl].astype(F32)).astype(BF)
            drift = share * delta_ref[h, rows]
            units.append((q0[rows, kl], win[:keys, kl], win[:keys, vl], e0[h, kept, :keys], grad, drift))
        (dq, dk, dv), (dq_in, dk_in, dv_in), (dq_out0, dk_out, dv_out) = backward(units)
        t0[h, part(1 - core, 128)] = dq_in
        t0[h, part(core, 128)] = dq_out0 + dqo0[h]
        acc[:, kl] = dk_in[:256] + dk_out
        acc[:, vl] = dv_in[:256] + dv_out
        dq = dq + dqo1[h] + expand(0.5 * (dq2[h] + expand(0.5 * dq3[h])))
        dq_out[:, kl] = reorder(matrix, (t0[h] + expand(0.5 * dq)).astype(BF))
        for lanes, value, fine in ((kl, dk, dk_in), (vl, dv, dv_in)):
            low, high = value[:64], value[64:]
            send[:128, lanes] = (fine[256:] + expand(0.5 * jnp.where(is0, low, high))).astype(BF)
            send[128:, lanes] = jnp.where(is0, high, low).astype(BF)


def add_kernel(own, r1, r2, r3, acc, send):
    core, _ = place()
    is0 = core == 0
    for j in range(2 * HEADS):
        lanes = head(j)
        sib3 = r2[32:, lanes].astype(F32)
        send[:, lanes] = (r1[192:, lanes].astype(F32) + expand(0.5 * sib3)).astype(BF)
        own3 = r2[:32, lanes].astype(F32) + r3[:, lanes].astype(F32)
        first = expand(0.25 * own3, 2) + placed(r1[128:192, lanes].astype(F32), ~is0, 64)
        acc[:, lanes] = own[:, lanes] + expand(0.5 * first) + placed(r1[:128, lanes].astype(F32), is0, 128)


def final_kernel(acc, near, got, dk, dv, done, sems):
    core, _ = place()
    is0 = core == 0
    matrix = order_matrix(back=True)
    copies = []
    for j in range(2 * HEADS):
        lanes = head(j)
        first = expand(0.5 * got[:, lanes].astype(F32)) + placed(near[128:, lanes].astype(F32), is0, 64)
        total = acc[:, lanes] + expand(0.5 * first) + placed(near[:128, lanes].astype(F32), ~is0, 128)
        done[:, lanes] = reorder(matrix, total.astype(BF))
        target = (dk if j < HEADS else dv).at[:, head(j % HEADS)]
        copies.append(pltpu.make_async_copy(done.at[:, lanes], target, sems.at[j]))
        copies[-1].start()
    for copy in copies:
        copy.wait()


SPACES = {"v": pltpu.VMEM, "a": pl.ANY}


def call(kernel, outs, scratch=(), flops=0, specs=None, results=pltpu.VMEM):
    extra = {"in_specs": [pl.BlockSpec(memory_space=SPACES[s]) for s in specs]} if specs else {}
    if flops:
        extra["cost_estimate"] = pl.CostEstimate(flops=flops, bytes_accessed=1 << 20, transcendentals=0)
    return pl.pallas_call(
        kernel,
        out_shape=[jax.ShapeDtypeStruct(shape, dtype) for shape, dtype in outs],
        out_specs=[pl.BlockSpec(memory_space=results)] * len(outs),
        scratch_shapes=[s if not isinstance(s, tuple) else pltpu.VMEM(*s) for s in scratch],
        compiler_params=pltpu.CompilerParams(vmem_limit_bytes=VMEM_LIMIT),
        **extra,
    )


def per_device(query, key_rows, value_rows, out_grad):
    count = lax.axis_size("seq")
    sibling = [(i, i + 1) for i in range(0, count, 2)]
    next1 = [(i, i + 1) for i in range(1, count - 1, 2)]
    next2 = [(i, i + 5) for i in range(0, count - 5, 2)]
    forward = [(i, i + 1) for i in range(1, count, 4)]
    next3 = [(i, i + 6) for i in range(count - 6) if (i // 2) % 2 == 0]

    def swap(value, pairs):
        return lax.ppermute(value, "seq", pairs + [(b, a) for a, b in pairs])

    def rows(n, dtype=BF):
        return ((n, FULL), dtype)

    def heads(n, dtype=F32, lanes=HEAD):
        return ((HEADS, n, lanes), dtype)

    stat = heads(256)
    out = ((ROWS, D), BF)
    key_sib = swap(key_rows, sibling)
    value_sib = swap(value_rows, sibling)
    kv, l1, l3 = call(pre_kernel, [rows(256), rows(128), rows(32)])(
        jnp.concatenate([key_rows, value_rows], axis=1)
    )
    near, s1, msg1, msg2 = call(pack_kernel, [rows(128), rows(128), rows(256), rows(64)])(
        kv, l1, l3, key_sib, value_sib
    )
    r2 = swap(msg2, next2)
    r1 = swap(msg1, next1)
    r3 = swap(r2, forward)
    q0, g0, q1, q2, q3, win, e0, e1, m0, m1, top, zsum, ysum = call(
        local_kernel,
        [out, out, ((128, D), BF), ((64, D), BF), ((32, D), BF), rows(384)]
        + [heads(256, BF, 384), heads(128, BF), stat, heads(128), stat, stat, stat],
        [heads(128), heads(128)],
        flops=1 << 33,
    )(query, out_grad, kv, near, s1)
    (send,) = call(third_split_kernel, [rows(128)], specs="vva")(r2, r3, top)
    got3 = swap(send, sibling)
    outer1, send = call(second_split_kernel, [rows(128), rows(128)], specs="va")(r1, send)
    got2 = swap(send, sibling)
    top, zsum, ysum, eo0, eo1, mo0, mo1 = call(
        outer_kernel,
        [stat] * 3 + [heads(128, BF), heads(128, BF), heads(128), heads(128)],
        [heads(128), heads(128)],
        flops=1 << 30,
    )(q0, q1, r1, outer1, top, zsum, ysum)
    att, best, inv, delta, dq2, dq3, own2, own3, cross3, send = call(
        far_kernel,
        [out, stat, stat, stat, heads(64), heads(32), rows(64, F32), rows(64, F32), rows(32, F32), rows(224)],
        [rows(192), rows(192)],
    )(q2, q3, g0, top, zsum, ysum, r1, got2, r2, r3, got3)
    got = swap(send, sibling)
    dqo0, dqo1, d0, d1 = call(
        outer_back_kernel, [heads(128), heads(128), rows(128, F32), rows(128, F32)], flops=1 << 30
    )(q0, q1, g0, r1, outer1, eo0, eo1, mo0, mo1, best, inv, delta)
    msg1, msg2, msg3 = call(join_kernel, [rows(256), rows(64), rows(32)])(own2, own3, cross3, d0, d1, got)
    r1 = swap(msg1, next1)
    r2 = swap(msg2, next2)
    r3 = swap(msg3, next3)
    attended, query_grad, acc, send = call(
        rest_kernel,
        [out, out, rows(256, F32), rows(192)],
        [stat],
        flops=1 << 31,
        specs="v" * 17 + "a",
    )(q0, q1, g0, win, s1, e0, e1, m0, m1, best, inv, delta, dqo0, dqo1, dq2, dq3, att, msg1)
    near = swap(send, sibling)
    acc, send = call(add_kernel, [rows(256, F32), rows(64)], flops=1 << 34)(acc, r1, r2, r3)
    got = swap(send, sibling)
    key_grad, value_grad = call(
        final_kernel, [out, out], [rows(256), pltpu.SemaphoreType.DMA((2 * HEADS,))], results=pl.ANY
    )(acc, near, got)
    return attended, query_grad, key_grad, value_grad


def solution(mesh):
    spec = P(("batch", "seq"), None)
    return jax.shard_map(
        per_device, mesh=mesh, in_specs=(spec,) * 4, out_specs=(spec,) * 4, check_vma=False
    )
```

```python
import jax
import jax.numpy as jnp
from jax import lax
from jax.experimental import pallas as pl
from jax.experimental.pallas import tpu as pltpu
from jax.sharding import PartitionSpec as P

HEADS = 4
HEAD = 128
D = HEADS * HEAD
ROWS = 256
FULL = 2 * D
SCALE = HEAD**-0.5
LOG2E = 1.4426950408889634
EXP_SCALE = SCALE * LOG2E
NEG = -1e30
VMEM_LIMIT = 40 * 1024 * 1024
BF = jnp.bfloat16
F32 = jnp.float32

RUN = 16


def place():
    index = lax.axis_index("seq")
    return lax.rem(index, 2), lax.div(index, 2)


def part(number, size):
    return pl.ds(pl.multiple_of(number * size, size), size)


def head(h):
    return slice(h * HEAD, (h + 1) * HEAD)


def order_matrix(back=False):
    a = lax.broadcasted_iota(jnp.int32, (128, 128), 0)
    b = lax.broadcasted_iota(jnp.int32, (128, 128), 1)
    row, token = (b, a) if back else (a, b)
    hit = row == (token & 7) * RUN + lax.shift_right_logical(token, 3)
    return jnp.where(hit, 1.0, 0.0).astype(BF)


def reorder(matrix, x):
    blocks = [jnp.dot(matrix, x[i : i + 128], preferred_element_type=F32) for i in range(0, x.shape[0], 128)]
    return jnp.concatenate(blocks, axis=0).astype(BF)


def coarse(x):
    rows, lanes = x.shape
    y = x.astype(F32).reshape(rows // (2 * RUN), 2, RUN, lanes)
    return ((y[:, 0] + y[:, 1]) * 0.5).reshape(rows // 2, lanes).astype(BF)


def expand(x, level=1):
    rows, lanes = x.shape
    step = 2**level
    y = jnp.broadcast_to(x.reshape(rows // RUN, 1, RUN, lanes), (rows // RUN, step, RUN, lanes))
    return y.reshape(rows * step, lanes)


def fold(x, level):
    rows, lanes = x.shape
    step = 2**level
    y = x.reshape(rows // (step * RUN), step, RUN, lanes)
    total = y[:, 0]
    for s in range(1, step):
        total = total + y[:, s]
    return total.reshape(rows // step, lanes)


def nt(a, b):
    return lax.dot_general(a, b, (((1,), (1,)), ((), ())), preferred_element_type=F32)


def tn(a, b):
    return lax.dot_general(a, b, (((0,), (0,)), ((), ())), preferred_element_type=F32)


def nn(a, b):
    return jnp.dot(a, b, preferred_element_type=F32)


def lanes128(value):
    return jnp.broadcast_to(value, (value.shape[0], HEAD))


def wide(value, lanes):
    pieces = [value[:, : min(HEAD, lanes - i)] for i in range(0, lanes, HEAD)]
    return pieces[0] if len(pieces) == 1 else jnp.concatenate(pieces, axis=1)


def penalty(ok):
    return jnp.where(ok, 0.0, NEG).astype(F32)


def half_masks():
    row = lax.broadcasted_iota(jnp.int32, (128, 128), 0) >= 64
    key = lax.broadcasted_iota(jnp.int32, (128, 128), 1) >= 64
    left = jnp.where(jnp.logical_and(~row, key), NEG, 0.0).astype(F32)
    right = jnp.where(jnp.logical_and(row, ~key), NEG, 0.0).astype(F32)
    return left, right


def soft(units):
    scores = [nt(q, k) if bias is None else nt(q, k) + bias for q, k, _, bias in units]
    peaks = [jnp.max(s, axis=1, keepdims=True) for s in scores]
    weights = [jnp.exp2((s - peak) * EXP_SCALE) for s, peak in zip(scores, peaks)]
    rounded = [e.astype(BF) for e in weights]
    mixes = [nn(eb, v) for eb, (_, _, v, _) in zip(rounded, units)]
    sums = [jnp.sum(e, axis=1, keepdims=True) for e in weights]
    return [
        (eb, lanes128(peak * EXP_SCALE), lanes128(den), mix)
        for eb, peak, den, mix in zip(rounded, peaks, sums, mixes)
    ]


def backward(units):
    inners = [nt(grad, v) for _, _, v, _, grad, _ in units]
    dvs = [tn(eb, grad) for _, _, _, eb, grad, _ in units]
    dscores = [
        (eb.astype(F32) * (inner - wide(drift, eb.shape[1]))).astype(BF)
        for inner, (_, _, _, eb, _, drift) in zip(inners, units)
    ]
    dqs = [nn(dscore, k) * SCALE for dscore, (_, k, _, _, _, _) in zip(dscores, units)]
    dks = [tn(dscore, q) * SCALE for dscore, (q, _, _, _, _, _) in zip(dscores, units)]
    return list(zip(dqs, dks, dvs))


def merge(top, z, y, pieces):
    best = top
    peaks = [expand(m, level) if level else m for m, _, _, level in pieces]
    for m in peaks:
        best = jnp.maximum(best, m)
    f = jnp.exp2(top - best)
    z, y = f * z, f * y
    factors = []
    for m, (_, d, n, level) in zip(peaks, pieces):
        f = jnp.exp2(m - best)
        if level:
            f = f * 2.0**level
            d, n = expand(d, level), expand(n, level)
        factors.append(f)
        z = z + f * d
        y = y + f * n
    return best, z, y, factors


def placed(value, first, rows):
    zeros = jnp.zeros((rows, value.shape[1]), F32)
    return jnp.concatenate([jnp.where(first, value, zeros), jnp.where(first, zeros, value)], axis=0)


def pre_kernel(raw, kv, l1, l3):
    matrix = order_matrix()
    for i in range(2):
        lanes = slice(i * D, (i + 1) * D)
        fine = reorder(matrix, raw[:, lanes])
        kv[:, lanes] = fine
        fine = coarse(fine)
        l1[:, lanes] = fine
        l3[:, lanes] = coarse(coarse(fine))


def pack_kernel(kv, l1, l3, ks, vs, near, s1, msg1, msg2):
    core, _ = place()
    matrix = order_matrix()
    for i, raw in enumerate((ks, vs)):
        lanes = slice(i * D, (i + 1) * D)
        fine = reorder(matrix, raw[...])
        near[:, lanes] = jnp.where(core == 0, fine[:128], fine[128:])
        first = coarse(fine)
        s1[:, lanes] = first
        second = coarse(first)
        msg1[192:, lanes] = second
        msg2[32:, lanes] = coarse(second)
    msg1[:128] = kv[part(core, 128), :]
    msg1[128:192] = l1[part(1 - core, 64), :]
    msg2[:32] = l3[...]


def local_kernel(q_ref, g_ref, kv, near, s1, q0, g0, q1, q2, q3, win, e0, e1, m0, m1, top, zsum, ysum, d1, n1):
    core, _ = place()
    matrix = order_matrix()
    q0[...] = reorder(matrix, q_ref[...])
    g0[...] = reorder(matrix, g_ref[...])
    q1[...] = coarse(q0[...])
    q2[...] = coarse(q1[...])
    q3[...] = coarse(q2[...])
    win[:256] = kv[...]
    win[256:] = near[...]
    left, right = half_masks()
    bias = jnp.where(core == 0, right, left)
    for h in range(HEADS):
        kl, vl = head(h), head(HEADS + h)
        blocks = ((1 - core, 384), (core, 256))
        units = [(q1[:, kl], s1[:, kl], s1[:, vl], bias)]
        units += [(q0[part(n, 128), kl], win[:keys, kl], win[:keys, vl], None) for n, keys in blocks]
        first, *fine = soft(units)
        e1[h], m1[h], d1[h], n1[h] = first
        for i, (number, keys) in enumerate(blocks):
            rows, half = part(number, 128), part(number, 64)
            e, m, d, n = fine[i]
            e0[h, i * 128 : (i + 1) * 128, :keys] = e
            m0[h, i * 128 : (i + 1) * 128] = m
            top[h, rows], zsum[h, rows], ysum[h, rows], _ = merge(
                m, d, n, [(m1[h, half], d1[h, half], n1[h, half], 1)]
            )


def second_split_kernel(r1, after, l1, send):
    core, _ = place()
    l1[part(core, 64), :] = r1[128:192]
    l1[part(1 - core, 64), :] = coarse(r1[:128])
    send[:64] = coarse(l1[...])
    send[64:] = r1[192:]


def third_split_kernel(r2, r3, after, send):
    send[:64] = r2[...]
    send[64:] = r3[...]


def outer_kernel(q0, q1, r1, l1, top, zsum, ysum, top_out, z_out, y_out, e0, e1, m0, m1, d1, n1):
    core, chip = place()
    is0 = core == 0
    bad = penalty(jnp.where(is0, chip >= 1, chip <= 30))
    left, right = half_masks()
    bias = jnp.where(is0, left, right) + bad
    outer = part(core, 128)
    units = []
    for h in range(HEADS):
        kl, vl = head(h), head(HEADS + h)
        units.append((q1[:, kl], l1[:, kl], l1[:, vl], bias))
        units.append((q0[outer, kl], r1[:128, kl], r1[:128, vl], bad))
    results = soft(units)
    for h in range(HEADS):
        e1[h], m1[h], d1[h], n1[h] = results[2 * h]
        e0[h], m, d, n = results[2 * h + 1]
        m0[h] = m
        for number in (core, 1 - core):
            rows, half = part(number, 128), part(number, 64)
            pieces = [(m1[h, half], d1[h, half], n1[h, half], 1)]
            if number is core:
                pieces.append((m, d, n, 0))
            top_out[h, rows], z_out[h, rows], y_out[h, rows], _ = merge(
                top[h, rows], zsum[h, rows], ysum[h, rows], pieces
            )


def far_kernel(
    q2, q3, g_ref, top, zsum, ysum, r1, got2, r2, r3, got3,
    att, best_out, inv_out, delta_out, dq2, dq3, own2, own3, cross3, send,
    w2, w3,
):
    core, chip = place()
    is0 = core == 0
    holder = lax.rem(core + chip, 2) == 1
    w2[:128] = got2[...]
    w2[128:] = r1[192:]
    w3[:64] = r2[...]
    w3[64:128] = got3[:64]
    w3[128:] = jnp.where(holder, r3[...], got3[64:])
    left_ok, right_ok = chip >= 1, chip <= 30
    low2, high2 = chip >= 2, chip <= 29
    even = lax.rem(chip, 2) == 0
    lane = lax.broadcasted_iota(jnp.int32, (1, 192), 1)
    own_bad = penalty(jnp.where(is0, left_ok, right_ok))
    sib_bad = penalty(jnp.where(is0, right_ok, left_ok))
    bias2 = jnp.where(lane < 128, sib_bad, own_bad)
    cross_bad = penalty(jnp.where(even, chip <= 28, chip >= 3))
    own_bad = penalty(jnp.where(is0, high2, low2))
    sib_bad = penalty(jnp.where(is0, low2, high2))
    bias3 = jnp.where(lane < 64, own_bad, jnp.where(lane < 128, sib_bad, cross_bad))
    units = []
    for h in range(HEADS):
        kl, vl = head(h), head(HEADS + h)
        units.append((q2[:, kl], w2[:, kl], w2[:, vl], bias2))
        units.append((q3[:, kl], w3[:, kl], w3[:, vl], bias3))
    results = soft(units)
    units = []
    for h in range(HEADS):
        kl, vl = head(h), head(HEADS + h)
        (e2, m2, d2, n2), (e3, m3, d3, n3) = results[2 * h : 2 * h + 2]
        grads = ([], [])
        drifts = ([], [])
        for c in range(2):
            r = slice(c * 128, (c + 1) * 128)
            a, b = slice(c * 32, (c + 1) * 32), slice(c * 16, (c + 1) * 16)
            pieces = [(m2[a], d2[a], n2[a], 2), (m3[b], d3[b], n3[b], 3)]
            best, z, y, factors = merge(top[h, r], zsum[h, r], ysum[h, r], pieces)
            inv = 1.0 / z
            y = y * inv
            att[r, kl] = y.astype(BF)
            g = g_ref[r, kl].astype(F32)
            delta = lanes128(jnp.sum(g * y, axis=1, keepdims=True))
            best_out[h, r] = best
            inv_out[h, r] = inv
            delta_out[h, r] = delta
            for i in range(2):
                share = factors[i] * inv
                grads[i].append(fold(share * g, i + 2))
                drifts[i].append(fold(share * delta, i + 2))
        for i, (q, w, e) in enumerate(((q2, w2, e2), (q3, w3, e3))):
            grad = jnp.concatenate(grads[i], axis=0).astype(BF)
            units.append((q[:, kl], w[:, kl], w[:, vl], e, grad, jnp.concatenate(drifts[i], axis=0)))
    results = backward(units)
    for h in range(HEADS):
        for i in range(2):
            dq, dk, dv = results[2 * h + i]
            (dq2, dq3)[i][h] = dq
            for lanes, value in ((head(h), dk), (head(HEADS + h), dv)):
                if i == 0:
                    send[:128, lanes] = value[:128].astype(BF)
                    own2[:, lanes] = value[128:]
                else:
                    own3[:, lanes] = value[:64]
                    send[128:192, lanes] = value[64:128].astype(BF)
                    cross3[:, lanes] = jnp.where(holder, value[128:160], value[160:])
                    send[192:, lanes] = jnp.where(holder, value[160:], value[128:160]).astype(BF)


def coarse_grad(m, best, inv, g, delta):
    grads, drifts = [], []
    for c in range(2):
        r, half = slice(c * 128, (c + 1) * 128), slice(c * 64, (c + 1) * 64)
        share = jnp.exp2(expand(m[half]) - best[r]) * (2.0 * inv[r])
        grads.append(fold(share * g[r].astype(F32), 1))
        drifts.append(fold(share * delta[r], 1))
    return jnp.concatenate(grads, axis=0).astype(BF), jnp.concatenate(drifts, axis=0)


def outer_back_kernel(
    q0, q1, g_ref, r1, l1, e0, e1, m0, m1, best, inv_ref, delta_ref,
    dq0, dq1, d0, d1,
):
    core, _ = place()
    outer = part(core, 128)
    units = []
    for h in range(HEADS):
        kl, vl = head(h), head(HEADS + h)
        share = jnp.exp2(m0[h] - best[h, outer]) * inv_ref[h, outer]
        grad = (share * g_ref[outer, kl].astype(F32)).astype(BF)
        drift = share * delta_ref[h, outer]
        units.append((q0[outer, kl], r1[:128, kl], r1[:128, vl], e0[h], grad, drift))
        grad, drift = coarse_grad(m1[h], best[h], inv_ref[h], g_ref[:, kl], delta_ref[h])
        units.append((q1[:, kl], l1[:, kl], l1[:, vl], e1[h], grad, drift))
    results = backward(units)
    for h in range(HEADS):
        kl, vl = head(h), head(HEADS + h)
        dq0[h], d0[:, kl], d0[:, vl] = results[2 * h]
        dq1[h], d1[:, kl], d1[:, vl] = results[2 * h + 1]


def join_kernel(own2, own3, cross3, d0, d1, got, msg1, msg2, msg3):
    core, _ = place()
    is0 = core == 0
    for j in range(2 * HEADS):
        lanes = head(j)
        msg1[192:, lanes] = (own2[:, lanes] + got[64:128, lanes].astype(F32)).astype(BF)
        first = d1[:, lanes] + expand(0.5 * got[:64, lanes].astype(F32))
        low, high = first[:64], first[64:]
        msg1[128:192, lanes] = jnp.where(is0, low, high).astype(BF)
        msg1[:128, lanes] = (d0[:, lanes] + expand(0.5 * jnp.where(is0, high, low))).astype(BF)
        msg2[:, lanes] = (own3[:, lanes] + got[128:192, lanes].astype(F32)).astype(BF)
        msg3[:, lanes] = (cross3[:, lanes] + got[192:, lanes].astype(F32)).astype(BF)


def rest_kernel(
    q0, q1, g_ref, win, s1, e0, e1, m0, m1, best, inv_ref, delta_ref, dqo0, dqo1, dq2, dq3, att_ref, after,
    att, dq_out, acc, send,
    t0,
):
    core, _ = place()
    is0 = core == 0
    matrix = order_matrix(back=True)
    att[...] = reorder(matrix, att_ref[...])
    for h in range(HEADS):
        kl, vl = head(h), head(HEADS + h)
        grad, drift = coarse_grad(m1[h], best[h], inv_ref[h], g_ref[:, kl], delta_ref[h])
        units = [(q1[:, kl], s1[:, kl], s1[:, vl], e1[h], grad, drift)]
        for i, (number, keys) in enumerate(((1 - core, 384), (core, 256))):
            rows, kept = part(number, 128), slice(i * 128, (i + 1) * 128)
            share = jnp.exp2(m0[h, kept] - best[h, rows]) * inv_ref[h, rows]
            grad = (share * g_ref[rows, kl].astype(F32)).astype(BF)
            drift = share * delta_ref[h, rows]
            units.append((q0[rows, kl], win[:keys, kl], win[:keys, vl], e0[h, kept, :keys], grad, drift))
        (dq, dk, dv), (dq_in, dk_in, dv_in), (dq_out0, dk_out, dv_out) = backward(units)
        t0[h, part(1 - core, 128)] = dq_in
        t0[h, part(core, 128)] = dq_out0 + dqo0[h]
        acc[:, kl] = dk_in[:256] + dk_out
        acc[:, vl] = dv_in[:256] + dv_out
        dq = dq + dqo1[h] + expand(0.5 * (dq2[h] + expand(0.5 * dq3[h])))
        dq_out[:, kl] = reorder(matrix, (t0[h] + expand(0.5 * dq)).astype(BF))
        for lanes, value, fine in ((kl, dk, dk_in), (vl, dv, dv_in)):
            low, high = value[:64], value[64:]
            send[:128, lanes] = (fine[256:] + expand(0.5 * jnp.where(is0, low, high))).astype(BF)
            send[128:, lanes] = jnp.where(is0, high, low).astype(BF)


def send_kernel(r1, r2, send):
    send[...] = (r1[192:].astype(F32) + expand(0.5 * r2[32:].astype(F32))).astype(BF)


def add_kernel(own, r1, r2, r3, after, acc):
    core, _ = place()
    is0 = core == 0
    for j in range(2 * HEADS):
        lanes = head(j)
        own3 = r2[:32, lanes].astype(F32) + r3[:, lanes].astype(F32)
        first = expand(0.25 * own3, 2) + placed(r1[128:192, lanes].astype(F32), ~is0, 64)
        acc[:, lanes] = own[:, lanes] + expand(0.5 * first) + placed(r1[:128, lanes].astype(F32), is0, 128)


def final_kernel(acc, near, got, dk, dv, done, sems):
    core, _ = place()
    is0 = core == 0
    matrix = order_matrix(back=True)
    copies = []
    for j in range(2 * HEADS):
        lanes = head(j)
        first = expand(0.5 * got[:, lanes].astype(F32)) + placed(near[128:, lanes].astype(F32), is0, 64)
        total = acc[:, lanes] + expand(0.5 * first) + placed(near[:128, lanes].astype(F32), ~is0, 128)
        done[:, lanes] = reorder(matrix, total.astype(BF))
        target = (dk if j < HEADS else dv).at[:, head(j % HEADS)]
        copies.append(pltpu.make_async_copy(done.at[:, lanes], target, sems.at[j]))
        copies[-1].start()
    for copy in copies:
        copy.wait()


SPACES = {"v": pltpu.VMEM, "a": pl.ANY}


def call(kernel, outs, scratch=(), flops=0, specs=None, results=pltpu.VMEM):
    extra = {"in_specs": [pl.BlockSpec(memory_space=SPACES[s]) for s in specs]} if specs else {}
    if flops:
        extra["cost_estimate"] = pl.CostEstimate(flops=flops, bytes_accessed=1 << 20, transcendentals=0)
    return pl.pallas_call(
        kernel,
        out_shape=[jax.ShapeDtypeStruct(shape, dtype) for shape, dtype in outs],
        out_specs=[pl.BlockSpec(memory_space=results)] * len(outs),
        scratch_shapes=[s if not isinstance(s, tuple) else pltpu.VMEM(*s) for s in scratch],
        compiler_params=pltpu.CompilerParams(vmem_limit_bytes=VMEM_LIMIT),
        **extra,
    )


def per_device(query, key_rows, value_rows, out_grad):
    count = lax.axis_size("seq")
    sibling = [(i, i + 1) for i in range(0, count, 2)]
    next1 = [(i, i + 1) for i in range(1, count - 1, 2)]
    next2 = [(i, i + 5) for i in range(0, count - 5, 2)]
    forward = [(i, i + 1) for i in range(1, count, 4)]
    next3 = [(i, i + 6) for i in range(count - 6) if (i // 2) % 2 == 0]

    def swap(value, pairs):
        return lax.ppermute(value, "seq", pairs + [(b, a) for a, b in pairs])

    def rows(n, dtype=BF):
        return ((n, FULL), dtype)

    def heads(n, dtype=F32, lanes=HEAD):
        return ((HEADS, n, lanes), dtype)

    stat = heads(256)
    out = ((ROWS, D), BF)
    key_sib = swap(key_rows, sibling)
    value_sib = swap(value_rows, sibling)
    kv, l1, l3 = call(pre_kernel, [rows(256), rows(128), rows(32)])(
        jnp.concatenate([key_rows, value_rows], axis=1)
    )
    near, s1, msg1, msg2 = call(pack_kernel, [rows(128), rows(128), rows(256), rows(64)])(
        kv, l1, l3, key_sib, value_sib
    )
    r2 = swap(msg2, next2)
    r1 = swap(msg1, next1)
    r3 = swap(r2, forward)
    q0, g0, q1, q2, q3, win, e0, e1, m0, m1, top, zsum, ysum = call(
        local_kernel,
        [out, out, ((128, D), BF), ((64, D), BF), ((32, D), BF), rows(384)]
        + [heads(256, BF, 384), heads(128, BF), stat, heads(128), stat, stat, stat],
        [heads(128), heads(128)],
        flops=1 << 33,
    )(query, out_grad, kv, near, s1)
    (send,) = call(third_split_kernel, [rows(128)], specs="vva")(r2, r3, top)
    got3 = swap(send, sibling)
    outer1, send = call(second_split_kernel, [rows(128), rows(128)], specs="va")(r1, send)
    got2 = swap(send, sibling)
    top, zsum, ysum, eo0, eo1, mo0, mo1 = call(
        outer_kernel,
        [stat] * 3 + [heads(128, BF), heads(128, BF), heads(128), heads(128)],
        [heads(128), heads(128)],
        flops=1 << 30,
    )(q0, q1, r1, outer1, top, zsum, ysum)
    att, best, inv, delta, dq2, dq3, own2, own3, cross3, send = call(
        far_kernel,
        [out, stat, stat, stat, heads(64), heads(32), rows(64, F32), rows(64, F32), rows(32, F32), rows(224)],
        [rows(192), rows(192)],
    )(q2, q3, g0, top, zsum, ysum, r1, got2, r2, r3, got3)
    got = swap(send, sibling)
    dqo0, dqo1, d0, d1 = call(
        outer_back_kernel, [heads(128), heads(128), rows(128, F32), rows(128, F32)], flops=1 << 30
    )(q0, q1, g0, r1, outer1, eo0, eo1, mo0, mo1, best, inv, delta)
    msg1, msg2, msg3 = call(join_kernel, [rows(256), rows(64), rows(32)])(own2, own3, cross3, d0, d1, got)
    r1 = swap(msg1, next1)
    r2 = swap(msg2, next2)
    r3 = swap(msg3, next3)
    attended, query_grad, acc, send = call(
        rest_kernel,
        [out, out, rows(256, F32), rows(192)],
        [stat],
        flops=1 << 29,
        specs="v" * 17 + "a",
    )(q0, q1, g0, win, s1, e0, e1, m0, m1, best, inv, delta, dqo0, dqo1, dq2, dq3, att, msg1)
    near = swap(send, sibling)
    (send,) = call(send_kernel, [rows(64)], flops=1 << 34)(r1, r2)
    got = swap(send, sibling)
    (acc,) = call(add_kernel, [rows(256, F32)], flops=1 << 34, specs="vvvva")(acc, r1, r2, r3, send)
    key_grad, value_grad = call(
        final_kernel, [out, out], [rows(256), pltpu.SemaphoreType.DMA((2 * HEADS,))], results=pl.ANY
    )(acc, near, got)
    return attended, query_grad, key_grad, value_grad


def solution(mesh):
    spec = P(("batch", "seq"), None)
    return jax.shard_map(
        per_device, mesh=mesh, in_specs=(spec,) * 4, out_specs=(spec,) * 4, check_vma=False
    )
```

```python
import jax
import jax.numpy as jnp
from jax import lax
from jax.experimental import pallas as pl
from jax.experimental.pallas import tpu as pltpu
from jax.sharding import PartitionSpec as P

HEADS = 4
HEAD = 128
D = HEADS * HEAD
ROWS = 256
FULL = 2 * D
SCALE = HEAD**-0.5
LOG2E = 1.4426950408889634
EXP_SCALE = SCALE * LOG2E
NEG = -1e30
VMEM_LIMIT = 40 * 1024 * 1024
BF = jnp.bfloat16
F32 = jnp.float32

RUN = 16


def place():
    index = lax.axis_index("seq")
    return lax.rem(index, 2), lax.div(index, 2)


def part(number, size):
    return pl.ds(pl.multiple_of(number * size, size), size)


def head(h):
    return slice(h * HEAD, (h + 1) * HEAD)


def order_matrix(back=False):
    a = lax.broadcasted_iota(jnp.int32, (128, 128), 0)
    b = lax.broadcasted_iota(jnp.int32, (128, 128), 1)
    row, token = (b, a) if back else (a, b)
    hit = row == (token & 7) * RUN + lax.shift_right_logical(token, 3)
    return jnp.where(hit, 1.0, 0.0).astype(BF)


def reorder(matrix, x):
    blocks = [jnp.dot(matrix, x[i : i + 128], preferred_element_type=F32) for i in range(0, x.shape[0], 128)]
    return jnp.concatenate(blocks, axis=0).astype(BF)


def coarse(x):
    rows, lanes = x.shape
    y = x.astype(F32).reshape(rows // (2 * RUN), 2, RUN, lanes)
    return ((y[:, 0] + y[:, 1]) * 0.5).reshape(rows // 2, lanes).astype(BF)


def expand(x, level=1):
    rows, lanes = x.shape
    step = 2**level
    y = jnp.broadcast_to(x.reshape(rows // RUN, 1, RUN, lanes), (rows // RUN, step, RUN, lanes))
    return y.reshape(rows * step, lanes)


def fold(x, level):
    rows, lanes = x.shape
    step = 2**level
    y = x.reshape(rows // (step * RUN), step, RUN, lanes)
    total = y[:, 0]
    for s in range(1, step):
        total = total + y[:, s]
    return total.reshape(rows // step, lanes)


def nt(a, b):
    return lax.dot_general(a, b, (((1,), (1,)), ((), ())), preferred_element_type=F32)


def tn(a, b):
    return lax.dot_general(a, b, (((0,), (0,)), ((), ())), preferred_element_type=F32)


def nn(a, b):
    return jnp.dot(a, b, preferred_element_type=F32)


def lanes128(value):
    return jnp.broadcast_to(value, (value.shape[0], HEAD))


def wide(value, lanes):
    pieces = [value[:, : min(HEAD, lanes - i)] for i in range(0, lanes, HEAD)]
    return pieces[0] if len(pieces) == 1 else jnp.concatenate(pieces, axis=1)


def penalty(ok):
    return jnp.where(ok, 0.0, NEG).astype(F32)


def half_masks():
    row = lax.broadcasted_iota(jnp.int32, (128, 128), 0) >= 64
    key = lax.broadcasted_iota(jnp.int32, (128, 128), 1) >= 64
    left = jnp.where(jnp.logical_and(~row, key), NEG, 0.0).astype(F32)
    right = jnp.where(jnp.logical_and(row, ~key), NEG, 0.0).astype(F32)
    return left, right


def soft(units):
    scores = [nt(q, k) if bias is None else nt(q, k) + bias for q, k, _, bias in units]
    peaks = [jnp.max(s, axis=1, keepdims=True) for s in scores]
    weights = [jnp.exp2((s - peak) * EXP_SCALE) for s, peak in zip(scores, peaks)]
    rounded = [e.astype(BF) for e in weights]
    mixes = [nn(eb, v) for eb, (_, _, v, _) in zip(rounded, units)]
    sums = [jnp.sum(e, axis=1, keepdims=True) for e in weights]
    return [
        (eb, lanes128(peak * EXP_SCALE), lanes128(den), mix)
        for eb, peak, den, mix in zip(rounded, peaks, sums, mixes)
    ]


def backward(units):
    inners = [nt(grad, v) for _, _, v, _, grad, _ in units]
    dvs = [tn(eb, grad) for _, _, _, eb, grad, _ in units]
    dscores = [
        (eb.astype(F32) * (inner - wide(drift, eb.shape[1]))).astype(BF)
        for inner, (_, _, _, eb, _, drift) in zip(inners, units)
    ]
    dqs = [nn(dscore, k) * SCALE for dscore, (_, k, _, _, _, _) in zip(dscores, units)]
    dks = [tn(dscore, q) * SCALE for dscore, (q, _, _, _, _, _) in zip(dscores, units)]
    return list(zip(dqs, dks, dvs))


def merge(top, z, y, pieces):
    best = top
    peaks = [expand(m, level) if level else m for m, _, _, level in pieces]
    for m in peaks:
        best = jnp.maximum(best, m)
    f = jnp.exp2(top - best)
    z, y = f * z, f * y
    factors = []
    for m, (_, d, n, level) in zip(peaks, pieces):
        f = jnp.exp2(m - best)
        if level:
            f = f * 2.0**level
            d, n = expand(d, level), expand(n, level)
        factors.append(f)
        z = z + f * d
        y = y + f * n
    return best, z, y, factors


def placed(value, first, rows):
    zeros = jnp.zeros((rows, value.shape[1]), F32)
    return jnp.concatenate([jnp.where(first, value, zeros), jnp.where(first, zeros, value)], axis=0)


def pre_kernel(raw, kv, l1, l3):
    matrix = order_matrix()
    for i in range(2):
        lanes = slice(i * D, (i + 1) * D)
        fine = reorder(matrix, raw[:, lanes])
        kv[:, lanes] = fine
        fine = coarse(fine)
        l1[:, lanes] = fine
        l3[:, lanes] = coarse(coarse(fine))


def pack_kernel(kv, l1, l3, ks, vs, near, s1, msg1, msg2):
    core, _ = place()
    matrix = order_matrix()
    for i, raw in enumerate((ks, vs)):
        lanes = slice(i * D, (i + 1) * D)
        fine = reorder(matrix, raw[...])
        near[:, lanes] = jnp.where(core == 0, fine[:128], fine[128:])
        first = coarse(fine)
        s1[:, lanes] = first
        second = coarse(first)
        msg1[192:, lanes] = second
        msg2[32:, lanes] = coarse(second)
    msg1[:128] = kv[part(core, 128), :]
    msg1[128:192] = l1[part(1 - core, 64), :]
    msg2[:32] = l3[...]


def local_kernel(q_ref, g_ref, kv, near, s1, q0, g0, q1, q2, q3, win, e0, e1, m0, m1, top, zsum, ysum, d1, n1):
    core, _ = place()
    matrix = order_matrix()
    q0[...] = reorder(matrix, q_ref[...])
    g0[...] = reorder(matrix, g_ref[...])
    q1[...] = coarse(q0[...])
    q2[...] = coarse(q1[...])
    q3[...] = coarse(q2[...])
    win[:256] = kv[...]
    win[256:] = near[...]
    left, right = half_masks()
    bias = jnp.where(core == 0, right, left)
    for h in range(HEADS):
        kl, vl = head(h), head(HEADS + h)
        blocks = ((1 - core, 384), (core, 256))
        units = [(q1[:, kl], s1[:, kl], s1[:, vl], bias)]
        units += [(q0[part(n, 128), kl], win[:keys, kl], win[:keys, vl], None) for n, keys in blocks]
        first, *fine = soft(units)
        e1[h], m1[h], d1[h], n1[h] = first
        for i, (number, keys) in enumerate(blocks):
            rows, half = part(number, 128), part(number, 64)
            e, m, d, n = fine[i]
            e0[h, i * 128 : (i + 1) * 128, :keys] = e
            m0[h, i * 128 : (i + 1) * 128] = m
            top[h, rows], zsum[h, rows], ysum[h, rows], _ = merge(
                m, d, n, [(m1[h, half], d1[h, half], n1[h, half], 1)]
            )


def second_split_kernel(r1, after, l1, send):
    core, _ = place()
    l1[part(core, 64), :] = r1[128:192]
    l1[part(1 - core, 64), :] = coarse(r1[:128])
    send[:64] = coarse(l1[...])
    send[64:] = r1[192:]


def third_split_kernel(r2, r3, after, send):
    send[:64] = r2[...]
    send[64:] = r3[...]


def outer_kernel(q0, q1, r1, l1, top, zsum, ysum, top_out, z_out, y_out, e0, e1, m0, m1, d1, n1):
    core, chip = place()
    is0 = core == 0
    bad = penalty(jnp.where(is0, chip >= 1, chip <= 30))
    left, right = half_masks()
    bias = jnp.where(is0, left, right) + bad
    outer = part(core, 128)
    units = []
    for h in range(HEADS):
        kl, vl = head(h), head(HEADS + h)
        units.append((q1[:, kl], l1[:, kl], l1[:, vl], bias))
        units.append((q0[outer, kl], r1[:128, kl], r1[:128, vl], bad))
    results = soft(units)
    for h in range(HEADS):
        e1[h], m1[h], d1[h], n1[h] = results[2 * h]
        e0[h], m, d, n = results[2 * h + 1]
        m0[h] = m
        for number in (core, 1 - core):
            rows, half = part(number, 128), part(number, 64)
            pieces = [(m1[h, half], d1[h, half], n1[h, half], 1)]
            if number is core:
                pieces.append((m, d, n, 0))
            top_out[h, rows], z_out[h, rows], y_out[h, rows], _ = merge(
                top[h, rows], zsum[h, rows], ysum[h, rows], pieces
            )


def third_kernel(q3, r2, r3, got, top, zsum, ysum, w3, e3, m3, top_out, z_out, y_out):
    core, chip = place()
    is0 = core == 0
    holder = lax.rem(core + chip, 2) == 1
    w3[:64] = r2[...]
    w3[64:128] = got[:64]
    w3[128:] = jnp.where(holder, r3[...], got[64:])
    low2, high2 = chip >= 2, chip <= 29
    even = lax.rem(chip, 2) == 0
    lane = lax.broadcasted_iota(jnp.int32, (1, 192), 1)
    cross_bad = penalty(jnp.where(even, chip <= 28, chip >= 3))
    own_bad = penalty(jnp.where(is0, high2, low2))
    sib_bad = penalty(jnp.where(is0, low2, high2))
    bias = jnp.where(lane < 64, own_bad, jnp.where(lane < 128, sib_bad, cross_bad))
    results = soft([(q3[:, head(h)], w3[:, head(h)], w3[:, head(HEADS + h)], bias) for h in range(HEADS)])
    for h in range(HEADS):
        e3[h], m3[h], d, n = results[h]
        for c in range(2):
            r, b = slice(c * 128, (c + 1) * 128), slice(c * 16, (c + 1) * 16)
            top_out[h, r], z_out[h, r], y_out[h, r], _ = merge(
                top[h, r], zsum[h, r], ysum[h, r], [(m3[h, b], d[b], n[b], 3)]
            )


def far_kernel(
    q2, q3, g_ref, top, zsum, ysum, r1, got2, w3, e3, m3,
    att, best_out, inv_out, delta_out, dq2, dq3, own2, own3, cross3, send2, send3,
    w2,
):
    core, chip = place()
    is0 = core == 0
    holder = lax.rem(core + chip, 2) == 1
    w2[:128] = got2[...]
    w2[128:] = r1[192:]
    left_ok, right_ok = chip >= 1, chip <= 30
    lane = lax.broadcasted_iota(jnp.int32, (1, 192), 1)
    own_bad = penalty(jnp.where(is0, left_ok, right_ok))
    sib_bad = penalty(jnp.where(is0, right_ok, left_ok))
    bias = jnp.where(lane < 128, sib_bad, own_bad)
    units = [(q2[:, head(h)], w2[:, head(h)], w2[:, head(HEADS + h)], bias) for h in range(HEADS)]
    results = soft(units)
    units = []
    for h in range(HEADS):
        kl, vl = head(h), head(HEADS + h)
        e2, m2, d2, n2 = results[h]
        grads = ([], [])
        drifts = ([], [])
        for c in range(2):
            r = slice(c * 128, (c + 1) * 128)
            a, b = slice(c * 32, (c + 1) * 32), slice(c * 16, (c + 1) * 16)
            best, z, y, factors = merge(top[h, r], zsum[h, r], ysum[h, r], [(m2[a], d2[a], n2[a], 2)])
            factors.append(8.0 * jnp.exp2(expand(m3[h, b], 3) - best))
            inv = 1.0 / z
            y = y * inv
            att[r, kl] = y.astype(BF)
            g = g_ref[r, kl].astype(F32)
            delta = lanes128(jnp.sum(g * y, axis=1, keepdims=True))
            best_out[h, r] = best
            inv_out[h, r] = inv
            delta_out[h, r] = delta
            for i in range(2):
                share = factors[i] * inv
                grads[i].append(fold(share * g, i + 2))
                drifts[i].append(fold(share * delta, i + 2))
        for i, (q, w, e) in enumerate(((q2, w2, e2), (q3, w3, e3[h]))):
            grad = jnp.concatenate(grads[i], axis=0).astype(BF)
            units.append((q[:, kl], w[:, kl], w[:, vl], e, grad, jnp.concatenate(drifts[i], axis=0)))
    results = backward(units)
    for h in range(HEADS):
        for i in range(2):
            dq, dk, dv = results[2 * h + i]
            (dq2, dq3)[i][h] = dq
            for lanes, value in ((head(h), dk), (head(HEADS + h), dv)):
                if i == 0:
                    send2[:, lanes] = value[:128].astype(BF)
                    own2[:, lanes] = value[128:]
                else:
                    own3[:, lanes] = value[:64]
                    send3[:64, lanes] = value[64:128].astype(BF)
                    cross3[:, lanes] = jnp.where(holder, value[128:160], value[160:])
                    send3[64:, lanes] = jnp.where(holder, value[160:], value[128:160]).astype(BF)


def coarse_grad(m, best, inv, g, delta):
    grads, drifts = [], []
    for c in range(2):
        r, half = slice(c * 128, (c + 1) * 128), slice(c * 64, (c + 1) * 64)
        share = jnp.exp2(expand(m[half]) - best[r]) * (2.0 * inv[r])
        grads.append(fold(share * g[r].astype(F32), 1))
        drifts.append(fold(share * delta[r], 1))
    return jnp.concatenate(grads, axis=0).astype(BF), jnp.concatenate(drifts, axis=0)


def outer_back_kernel(
    q0, q1, g_ref, r1, l1, e0, e1, m0, m1, best, inv_ref, delta_ref,
    dq0, dq1, d0, d1,
):
    core, _ = place()
    outer = part(core, 128)
    units = []
    for h in range(HEADS):
        kl, vl = head(h), head(HEADS + h)
        share = jnp.exp2(m0[h] - best[h, outer]) * inv_ref[h, outer]
        grad = (share * g_ref[outer, kl].astype(F32)).astype(BF)
        drift = share * delta_ref[h, outer]
        units.append((q0[outer, kl], r1[:128, kl], r1[:128, vl], e0[h], grad, drift))
        grad, drift = coarse_grad(m1[h], best[h], inv_ref[h], g_ref[:, kl], delta_ref[h])
        units.append((q1[:, kl], l1[:, kl], l1[:, vl], e1[h], grad, drift))
    results = backward(units)
    for h in range(HEADS):
        kl, vl = head(h), head(HEADS + h)
        dq0[h], d0[:, kl], d0[:, vl] = results[2 * h]
        dq1[h], d1[:, kl], d1[:, vl] = results[2 * h + 1]


def join_kernel(own2, d0, d1, got, msg1):
    core, _ = place()
    is0 = core == 0
    for j in range(2 * HEADS):
        lanes = head(j)
        msg1[192:, lanes] = (own2[:, lanes] + got[64:, lanes].astype(F32)).astype(BF)
        first = d1[:, lanes] + expand(0.5 * got[:64, lanes].astype(F32))
        low, high = first[:64], first[64:]
        msg1[128:192, lanes] = jnp.where(is0, low, high).astype(BF)
        msg1[:128, lanes] = (d0[:, lanes] + expand(0.5 * jnp.where(is0, high, low))).astype(BF)


def third_join_kernel(own3, cross3, got, msg2, msg3):
    msg2[...] = (own3[...] + got[:64].astype(F32)).astype(BF)
    msg3[...] = (cross3[...] + got[64:].astype(F32)).astype(BF)


def rest_kernel(
    q0, q1, g_ref, win, s1, e0, e1, m0, m1, best, inv_ref, delta_ref, dqo0, dqo1, dq2, dq3, att_ref, after,
    att, dq_out, acc, send,
    t0,
):
    core, _ = place()
    is0 = core == 0
    matrix = order_matrix(back=True)
    att[...] = reorder(matrix, att_ref[...])
    for h in range(HEADS):
        kl, vl = head(h), head(HEADS + h)
        grad, drift = coarse_grad(m1[h], best[h], inv_ref[h], g_ref[:, kl], delta_ref[h])
        units = [(q1[:, kl], s1[:, kl], s1[:, vl], e1[h], grad, drift)]
        for i, (number, keys) in enumerate(((1 - core, 384), (core, 256))):
            rows, kept = part(number, 128), slice(i * 128, (i + 1) * 128)
            share = jnp.exp2(m0[h, kept] - best[h, rows]) * inv_ref[h, rows]
            grad = (share * g_ref[rows, kl].astype(F32)).astype(BF)
            drift = share * delta_ref[h, rows]
            units.append((q0[rows, kl], win[:keys, kl], win[:keys, vl], e0[h, kept, :keys], grad, drift))
        (dq, dk, dv), (dq_in, dk_in, dv_in), (dq_out0, dk_out, dv_out) = backward(units)
        t0[h, part(1 - core, 128)] = dq_in
        t0[h, part(core, 128)] = dq_out0 + dqo0[h]
        acc[:, kl] = dk_in[:256] + dk_out
        acc[:, vl] = dv_in[:256] + dv_out
        dq = dq + dqo1[h] + expand(0.5 * (dq2[h] + expand(0.5 * dq3[h])))
        dq_out[:, kl] = reorder(matrix, (t0[h] + expand(0.5 * dq)).astype(BF))
        for lanes, value, fine in ((kl, dk, dk_in), (vl, dv, dv_in)):
            low, high = value[:64], value[64:]
            send[:128, lanes] = (fine[256:] + expand(0.5 * jnp.where(is0, low, high))).astype(BF)
            send[128:, lanes] = jnp.where(is0, high, low).astype(BF)


def send_kernel(r1, r2, send):
    send[...] = (r1[192:].astype(F32) + expand(0.5 * r2[32:].astype(F32))).astype(BF)


def add_kernel(own, r1, r2, after, acc):
    core, _ = place()
    is0 = core == 0
    for j in range(2 * HEADS):
        lanes = head(j)
        first = expand(0.25 * r2[:32, lanes].astype(F32), 2) + placed(r1[128:192, lanes].astype(F32), ~is0, 64)
        acc[:, lanes] = own[:, lanes] + expand(0.5 * first) + placed(r1[:128, lanes].astype(F32), is0, 128)


def cross_kernel(r3, after, second):
    second[...] = expand(0.5 * r3[...].astype(F32))


def final_kernel(acc, near, got, cross, dk, dv, done, sems):
    core, _ = place()
    is0 = core == 0
    matrix = order_matrix(back=True)
    copies = []
    for j in range(2 * HEADS):
        lanes = head(j)
        second = got[:, lanes].astype(F32) + cross[:, lanes]
        first = expand(0.5 * second) + placed(near[128:, lanes].astype(F32), is0, 64)
        total = acc[:, lanes] + expand(0.5 * first) + placed(near[:128, lanes].astype(F32), ~is0, 128)
        done[:, lanes] = reorder(matrix, total.astype(BF))
        target = (dk if j < HEADS else dv).at[:, head(j % HEADS)]
        copies.append(pltpu.make_async_copy(done.at[:, lanes], target, sems.at[j]))
        copies[-1].start()
    for copy in copies:
        copy.wait()


SPACES = {"v": pltpu.VMEM, "a": pl.ANY}


def call(kernel, outs, scratch=(), flops=0, specs=None, results=pltpu.VMEM):
    extra = {"in_specs": [pl.BlockSpec(memory_space=SPACES[s]) for s in specs]} if specs else {}
    if flops:
        extra["cost_estimate"] = pl.CostEstimate(flops=flops, bytes_accessed=1 << 20, transcendentals=0)
    return pl.pallas_call(
        kernel,
        out_shape=[jax.ShapeDtypeStruct(shape, dtype) for shape, dtype in outs],
        out_specs=[pl.BlockSpec(memory_space=results)] * len(outs),
        scratch_shapes=[s if not isinstance(s, tuple) else pltpu.VMEM(*s) for s in scratch],
        compiler_params=pltpu.CompilerParams(vmem_limit_bytes=VMEM_LIMIT),
        **extra,
    )


def per_device(query, key_rows, value_rows, out_grad):
    count = lax.axis_size("seq")
    sibling = [(i, i + 1) for i in range(0, count, 2)]
    next1 = [(i, i + 1) for i in range(1, count - 1, 2)]
    next2 = [(i, i + 5) for i in range(0, count - 5, 2)]
    forward = [(i, i + 1) for i in range(1, count, 4)]
    next3 = [(i, i + 6) for i in range(count - 6) if (i // 2) % 2 == 0]

    def swap(value, pairs):
        return lax.ppermute(value, "seq", pairs + [(b, a) for a, b in pairs])

    def rows(n, dtype=BF):
        return ((n, FULL), dtype)

    def heads(n, dtype=F32, lanes=HEAD):
        return ((HEADS, n, lanes), dtype)

    stat = heads(256)
    out = ((ROWS, D), BF)
    key_sib = swap(key_rows, sibling)
    value_sib = swap(value_rows, sibling)
    kv, l1, l3 = call(pre_kernel, [rows(256), rows(128), rows(32)])(
        jnp.concatenate([key_rows, value_rows], axis=1)
    )
    near, s1, msg1, msg2 = call(pack_kernel, [rows(128), rows(128), rows(256), rows(64)])(
        kv, l1, l3, key_sib, value_sib
    )
    r2 = swap(msg2, next2)
    r1 = swap(msg1, next1)
    r3 = swap(r2, forward)
    q0, g0, q1, q2, q3, win, e0, e1, m0, m1, top, zsum, ysum = call(
        local_kernel,
        [out, out, ((128, D), BF), ((64, D), BF), ((32, D), BF), rows(384)]
        + [heads(256, BF, 384), heads(128, BF), stat, heads(128), stat, stat, stat],
        [heads(128), heads(128)],
        flops=1 << 33,
    )(query, out_grad, kv, near, s1)
    (send,) = call(third_split_kernel, [rows(128)], specs="vva")(r2, r3, top)
    got3 = swap(send, sibling)
    outer1, send = call(second_split_kernel, [rows(128), rows(128)], specs="va")(r1, send)
    got2 = swap(send, sibling)
    top, zsum, ysum, eo0, eo1, mo0, mo1 = call(
        outer_kernel,
        [stat] * 3 + [heads(128, BF), heads(128, BF), heads(128), heads(128)],
        [heads(128), heads(128)],
        flops=1 << 30,
    )(q0, q1, r1, outer1, top, zsum, ysum)
    w3, e3, m3, top, zsum, ysum = call(
        third_kernel, [rows(192), heads(32, BF, 192), heads(32), stat, stat, stat], flops=1 << 28
    )(q3, r2, r3, got3, top, zsum, ysum)
    att, best, inv, delta, dq2, dq3, own2, own3, cross3, send2, send3 = call(
        far_kernel,
        [out, stat, stat, stat, heads(64), heads(32), rows(64, F32), rows(64, F32), rows(32, F32), rows(128), rows(96)],
        [rows(192)],
    )(q2, q3, g0, top, zsum, ysum, r1, got2, w3, e3, m3)
    got2 = swap(send2, sibling)
    got3 = swap(send3, sibling)
    dqo0, dqo1, d0, d1 = call(
        outer_back_kernel, [heads(128), heads(128), rows(128, F32), rows(128, F32)], flops=1 << 30
    )(q0, q1, g0, r1, outer1, eo0, eo1, mo0, mo1, best, inv, delta)
    (msg1,) = call(join_kernel, [rows(256)])(own2, d0, d1, got2)
    msg2, msg3 = call(third_join_kernel, [rows(64), rows(32)], flops=1 << 33)(own3, cross3, got3)
    r1 = swap(msg1, next1)
    r2 = swap(msg2, next2)
    r3 = swap(msg3, next3)
    attended, query_grad, acc, send = call(
        rest_kernel,
        [out, out, rows(256, F32), rows(192)],
        [stat],
        flops=1 << 29,
        specs="v" * 17 + "a",
    )(q0, q1, g0, win, s1, e0, e1, m0, m1, best, inv, delta, dqo0, dqo1, dq2, dq3, att, msg1)
    near = swap(send, sibling)
    (send,) = call(send_kernel, [rows(64)], flops=1 << 34)(r1, r2)
    got = swap(send, sibling)
    (acc,) = call(add_kernel, [rows(256, F32)], specs="vvva")(acc, r1, r2, send)
    (cross,) = call(cross_kernel, [rows(64, F32)], flops=1 << 34, specs="va")(r3, acc)
    key_grad, value_grad = call(
        final_kernel, [out, out], [rows(256), pltpu.SemaphoreType.DMA((2 * HEADS,))], results=pl.ANY
    )(acc, near, got, cross)
    return attended, query_grad, key_grad, value_grad


def solution(mesh):
    spec = P(("batch", "seq"), None)
    return jax.shard_map(
        per_device, mesh=mesh, in_specs=(spec,) * 4, out_specs=(spec,) * 4, check_vma=False
    )
```

```python
import jax
import jax.numpy as jnp
from jax import lax
from jax.experimental import pallas as pl
from jax.experimental.pallas import tpu as pltpu
from jax.sharding import PartitionSpec as P

HEADS = 4
HEAD = 128
D = HEADS * HEAD
ROWS = 256
FULL = 2 * D
SCALE = HEAD**-0.5
LOG2E = 1.4426950408889634
EXP_SCALE = SCALE * LOG2E
NEG = -1e30
VMEM_LIMIT = 40 * 1024 * 1024
BF = jnp.bfloat16
F32 = jnp.float32

RUN = 16


def place():
    index = lax.axis_index("seq")
    return lax.rem(index, 2), lax.div(index, 2)


def part(number, size):
    return pl.ds(pl.multiple_of(number * size, size), size)


def head(h):
    return slice(h * HEAD, (h + 1) * HEAD)


def order_matrix(back=False):
    a = lax.broadcasted_iota(jnp.int32, (128, 128), 0)
    b = lax.broadcasted_iota(jnp.int32, (128, 128), 1)
    row, token = (b, a) if back else (a, b)
    hit = row == (token & 7) * RUN + lax.shift_right_logical(token, 3)
    return jnp.where(hit, 1.0, 0.0).astype(BF)


def reorder(matrix, x):
    blocks = [jnp.dot(matrix, x[i : i + 128], preferred_element_type=F32) for i in range(0, x.shape[0], 128)]
    return jnp.concatenate(blocks, axis=0).astype(BF)


def coarse(x):
    rows, lanes = x.shape
    y = x.astype(F32).reshape(rows // (2 * RUN), 2, RUN, lanes)
    return ((y[:, 0] + y[:, 1]) * 0.5).reshape(rows // 2, lanes).astype(BF)


def expand(x, level=1):
    rows, lanes = x.shape
    step = 2**level
    y = jnp.broadcast_to(x.reshape(rows // RUN, 1, RUN, lanes), (rows // RUN, step, RUN, lanes))
    return y.reshape(rows * step, lanes)


def fold(x, level):
    rows, lanes = x.shape
    step = 2**level
    y = x.reshape(rows // (step * RUN), step, RUN, lanes)
    total = y[:, 0]
    for s in range(1, step):
        total = total + y[:, s]
    return total.reshape(rows // step, lanes)


def nt(a, b):
    return lax.dot_general(a, b, (((1,), (1,)), ((), ())), preferred_element_type=F32)


def tn(a, b):
    return lax.dot_general(a, b, (((0,), (0,)), ((), ())), preferred_element_type=F32)


def nn(a, b):
    return jnp.dot(a, b, preferred_element_type=F32)


def lanes128(value):
    return jnp.broadcast_to(value, (value.shape[0], HEAD))


def wide(value, lanes):
    pieces = [value[:, : min(HEAD, lanes - i)] for i in range(0, lanes, HEAD)]
    return pieces[0] if len(pieces) == 1 else jnp.concatenate(pieces, axis=1)


def penalty(ok):
    return jnp.where(ok, 0.0, NEG).astype(F32)


def half_masks():
    row = lax.broadcasted_iota(jnp.int32, (128, 128), 0) >= 64
    key = lax.broadcasted_iota(jnp.int32, (128, 128), 1) >= 64
    left = jnp.where(jnp.logical_and(~row, key), NEG, 0.0).astype(F32)
    right = jnp.where(jnp.logical_and(row, ~key), NEG, 0.0).astype(F32)
    return left, right


def soft(units):
    scores = [nt(q, k) if bias is None else nt(q, k) + bias for q, k, _, bias in units]
    peaks = [jnp.max(s, axis=1, keepdims=True) for s in scores]
    weights = [jnp.exp2((s - peak) * EXP_SCALE) for s, peak in zip(scores, peaks)]
    rounded = [e.astype(BF) for e in weights]
    mixes = [nn(eb, v) for eb, (_, _, v, _) in zip(rounded, units)]
    sums = [jnp.sum(e, axis=1, keepdims=True) for e in weights]
    return [
        (eb, lanes128(peak * EXP_SCALE), lanes128(den), mix)
        for eb, peak, den, mix in zip(rounded, peaks, sums, mixes)
    ]


def backward(units):
    inners = [nt(grad, v) for _, _, v, _, grad, _ in units]
    dvs = [tn(eb, grad) for _, _, _, eb, grad, _ in units]
    dscores = [
        (eb.astype(F32) * (inner - wide(drift, eb.shape[1]))).astype(BF)
        for inner, (_, _, _, eb, _, drift) in zip(inners, units)
    ]
    dqs = [nn(dscore, k) * SCALE for dscore, (_, k, _, _, _, _) in zip(dscores, units)]
    dks = [tn(dscore, q) * SCALE for dscore, (q, _, _, _, _, _) in zip(dscores, units)]
    return list(zip(dqs, dks, dvs))


def merge(top, z, y, pieces):
    best = top
    peaks = [expand(m, level) if level else m for m, _, _, level in pieces]
    for m in peaks:
        best = jnp.maximum(best, m)
    f = jnp.exp2(top - best)
    z, y = f * z, f * y
    factors = []
    for m, (_, d, n, level) in zip(peaks, pieces):
        f = jnp.exp2(m - best)
        if level:
            f = f * 2.0**level
            d, n = expand(d, level), expand(n, level)
        factors.append(f)
        z = z + f * d
        y = y + f * n
    return best, z, y, factors


def placed(value, first, rows):
    zeros = jnp.zeros((rows, value.shape[1]), F32)
    return jnp.concatenate([jnp.where(first, value, zeros), jnp.where(first, zeros, value)], axis=0)


def pre_kernel(raw, kv, l1, l3):
    matrix = order_matrix()
    for i in range(2):
        lanes = slice(i * D, (i + 1) * D)
        fine = reorder(matrix, raw[:, lanes])
        kv[:, lanes] = fine
        fine = coarse(fine)
        l1[:, lanes] = fine
        l3[:, lanes] = coarse(coarse(fine))


def pack_kernel(kv, l1, l3, ks, vs, near, s1, msg1, msg2):
    core, _ = place()
    matrix = order_matrix()
    for i, raw in enumerate((ks, vs)):
        lanes = slice(i * D, (i + 1) * D)
        fine = reorder(matrix, raw[...])
        near[:, lanes] = jnp.where(core == 0, fine[:128], fine[128:])
        first = coarse(fine)
        s1[:, lanes] = first
        second = coarse(first)
        msg1[192:, lanes] = second
        msg2[32:, lanes] = coarse(second)
    msg1[:128] = kv[part(core, 128), :]
    msg1[128:192] = l1[part(1 - core, 64), :]
    msg2[:32] = l3[...]


def local_kernel(q_ref, g_ref, kv, near, s1, q0, g0, q1, q2, q3, win, e0, e1, m0, m1, top, zsum, ysum, d1, n1):
    core, _ = place()
    matrix = order_matrix()
    q0[...] = reorder(matrix, q_ref[...])
    g0[...] = reorder(matrix, g_ref[...])
    q1[...] = coarse(q0[...])
    q2[...] = coarse(q1[...])
    q3[...] = coarse(q2[...])
    win[:256] = kv[...]
    win[256:] = near[...]
    left, right = half_masks()
    bias = jnp.where(core == 0, right, left)
    for h in range(HEADS):
        kl, vl = head(h), head(HEADS + h)
        blocks = ((1 - core, 384), (core, 256))
        units = [(q1[:, kl], s1[:, kl], s1[:, vl], bias)]
        units += [(q0[part(n, 128), kl], win[:keys, kl], win[:keys, vl], None) for n, keys in blocks]
        first, *fine = soft(units)
        e1[h], m1[h], d1[h], n1[h] = first
        for i, (number, keys) in enumerate(blocks):
            rows, half = part(number, 128), part(number, 64)
            e, m, d, n = fine[i]
            e0[h, i * 128 : (i + 1) * 128, :keys] = e
            m0[h, i * 128 : (i + 1) * 128] = m
            top[h, rows], zsum[h, rows], ysum[h, rows], _ = merge(
                m, d, n, [(m1[h, half], d1[h, half], n1[h, half], 1)]
            )


def second_split_kernel(r1, after, l1, send):
    core, _ = place()
    l1[part(core, 64), :] = r1[128:192]
    l1[part(1 - core, 64), :] = coarse(r1[:128])
    send[:64] = coarse(l1[...])
    send[64:] = r1[192:]


def third_split_kernel(r2, r3, after, send):
    send[:64] = r2[...]
    send[64:] = r3[...]


def outer_kernel(q0, q1, r1, l1, top, zsum, ysum, top_out, z_out, y_out, e0, e1, m0, m1, d1, n1):
    core, chip = place()
    is0 = core == 0
    bad = penalty(jnp.where(is0, chip >= 1, chip <= 30))
    left, right = half_masks()
    bias = jnp.where(is0, left, right) + bad
    outer = part(core, 128)
    units = []
    for h in range(HEADS):
        kl, vl = head(h), head(HEADS + h)
        units.append((q1[:, kl], l1[:, kl], l1[:, vl], bias))
        units.append((q0[outer, kl], r1[:128, kl], r1[:128, vl], bad))
    results = soft(units)
    for h in range(HEADS):
        e1[h], m1[h], d1[h], n1[h] = results[2 * h]
        e0[h], m, d, n = results[2 * h + 1]
        m0[h] = m
        for number in (core, 1 - core):
            rows, half = part(number, 128), part(number, 64)
            pieces = [(m1[h, half], d1[h, half], n1[h, half], 1)]
            if number is core:
                pieces.append((m, d, n, 0))
            top_out[h, rows], z_out[h, rows], y_out[h, rows], _ = merge(
                top[h, rows], zsum[h, rows], ysum[h, rows], pieces
            )


def third_kernel(q3, r2, r3, got, top, zsum, ysum, w3, e3, m3, top_out, z_out, y_out):
    core, chip = place()
    is0 = core == 0
    holder = lax.rem(core + chip, 2) == 1
    w3[:64] = r2[...]
    w3[64:128] = got[:64]
    w3[128:] = jnp.where(holder, r3[...], got[64:])
    low2, high2 = chip >= 2, chip <= 29
    even = lax.rem(chip, 2) == 0
    lane = lax.broadcasted_iota(jnp.int32, (1, 192), 1)
    cross_bad = penalty(jnp.where(even, chip <= 28, chip >= 3))
    own_bad = penalty(jnp.where(is0, high2, low2))
    sib_bad = penalty(jnp.where(is0, low2, high2))
    bias = jnp.where(lane < 64, own_bad, jnp.where(lane < 128, sib_bad, cross_bad))
    results = soft([(q3[:, head(h)], w3[:, head(h)], w3[:, head(HEADS + h)], bias) for h in range(HEADS)])
    for h in range(HEADS):
        e3[h], m3[h], d, n = results[h]
        for c in range(2):
            r, b = slice(c * 128, (c + 1) * 128), slice(c * 16, (c + 1) * 16)
            top_out[h, r], z_out[h, r], y_out[h, r], _ = merge(
                top[h, r], zsum[h, r], ysum[h, r], [(m3[h, b], d[b], n[b], 3)]
            )


def far_kernel(
    q2, g_ref, top, zsum, ysum, r1, got2, m3,
    att, best_out, inv_out, delta_out, grad3, drift3, dq2, own2, send,
    w2,
):
    core, chip = place()
    is0 = core == 0
    w2[:128] = got2[...]
    w2[128:] = r1[192:]
    left_ok, right_ok = chip >= 1, chip <= 30
    lane = lax.broadcasted_iota(jnp.int32, (1, 192), 1)
    own_bad = penalty(jnp.where(is0, left_ok, right_ok))
    sib_bad = penalty(jnp.where(is0, right_ok, left_ok))
    bias = jnp.where(lane < 128, sib_bad, own_bad)
    units = [(q2[:, head(h)], w2[:, head(h)], w2[:, head(HEADS + h)], bias) for h in range(HEADS)]
    results = soft(units)
    units = []
    for h in range(HEADS):
        kl, vl = head(h), head(HEADS + h)
        e2, m2, d2, n2 = results[h]
        grads = ([], [])
        drifts = ([], [])
        for c in range(2):
            r = slice(c * 128, (c + 1) * 128)
            a, b = slice(c * 32, (c + 1) * 32), slice(c * 16, (c + 1) * 16)
            best, z, y, factors = merge(top[h, r], zsum[h, r], ysum[h, r], [(m2[a], d2[a], n2[a], 2)])
            factors.append(8.0 * jnp.exp2(expand(m3[h, b], 3) - best))
            inv = 1.0 / z
            y = y * inv
            att[r, kl] = y.astype(BF)
            g = g_ref[r, kl].astype(F32)
            delta = lanes128(jnp.sum(g * y, axis=1, keepdims=True))
            best_out[h, r] = best
            inv_out[h, r] = inv
            delta_out[h, r] = delta
            for i in range(2):
                share = factors[i] * inv
                grads[i].append(fold(share * g, i + 2))
                drifts[i].append(fold(share * delta, i + 2))
        grad = jnp.concatenate(grads[0], axis=0).astype(BF)
        units.append((q2[:, kl], w2[:, kl], w2[:, vl], e2, grad, jnp.concatenate(drifts[0], axis=0)))
        grad3[h] = jnp.concatenate(grads[1], axis=0).astype(BF)
        drift3[h] = jnp.concatenate(drifts[1], axis=0)
    for h, (dq, dk, dv) in enumerate(backward(units)):
        dq2[h] = dq
        for lanes, value in ((head(h), dk), (head(HEADS + h), dv)):
            send[:, lanes] = value[:128].astype(BF)
            own2[:, lanes] = value[128:]


def third_back_kernel(q3, w3, e3, grad, drift, dq3, own3, cross3, send):
    core, chip = place()
    holder = lax.rem(core + chip, 2) == 1
    units = []
    for h in range(HEADS):
        units.append((q3[:, head(h)], w3[:, head(h)], w3[:, head(HEADS + h)], e3[h], grad[h], drift[h]))
    for h, (dq, dk, dv) in enumerate(backward(units)):
        dq3[h] = dq
        for lanes, value in ((head(h), dk), (head(HEADS + h), dv)):
            own3[:, lanes] = value[:64]
            send[:64, lanes] = value[64:128].astype(BF)
            cross3[:, lanes] = jnp.where(holder, value[128:160], value[160:])
            send[64:, lanes] = jnp.where(holder, value[160:], value[128:160]).astype(BF)


def coarse_grad(m, best, inv, g, delta):
    grads, drifts = [], []
    for c in range(2):
        r, half = slice(c * 128, (c + 1) * 128), slice(c * 64, (c + 1) * 64)
        share = jnp.exp2(expand(m[half]) - best[r]) * (2.0 * inv[r])
        grads.append(fold(share * g[r].astype(F32), 1))
        drifts.append(fold(share * delta[r], 1))
    return jnp.concatenate(grads, axis=0).astype(BF), jnp.concatenate(drifts, axis=0)


def outer_back_kernel(
    q0, q1, g_ref, r1, l1, e0, e1, m0, m1, best, inv_ref, delta_ref,
    dq0, dq1, d0, d1,
):
    core, _ = place()
    outer = part(core, 128)
    units = []
    for h in range(HEADS):
        kl, vl = head(h), head(HEADS + h)
        share = jnp.exp2(m0[h] - best[h, outer]) * inv_ref[h, outer]
        grad = (share * g_ref[outer, kl].astype(F32)).astype(BF)
        drift = share * delta_ref[h, outer]
        units.append((q0[outer, kl], r1[:128, kl], r1[:128, vl], e0[h], grad, drift))
        grad, drift = coarse_grad(m1[h], best[h], inv_ref[h], g_ref[:, kl], delta_ref[h])
        units.append((q1[:, kl], l1[:, kl], l1[:, vl], e1[h], grad, drift))
    results = backward(units)
    for h in range(HEADS):
        kl, vl = head(h), head(HEADS + h)
        dq0[h], d0[:, kl], d0[:, vl] = results[2 * h]
        dq1[h], d1[:, kl], d1[:, vl] = results[2 * h + 1]


def join_kernel(own2, d0, d1, got, msg1):
    core, _ = place()
    is0 = core == 0
    for j in range(2 * HEADS):
        lanes = head(j)
        msg1[192:, lanes] = (own2[:, lanes] + got[64:, lanes].astype(F32)).astype(BF)
        first = d1[:, lanes] + expand(0.5 * got[:64, lanes].astype(F32))
        low, high = first[:64], first[64:]
        msg1[128:192, lanes] = jnp.where(is0, low, high).astype(BF)
        msg1[:128, lanes] = (d0[:, lanes] + expand(0.5 * jnp.where(is0, high, low))).astype(BF)


def third_join_kernel(own3, cross3, got, msg2, msg3):
    msg2[...] = (own3[...] + got[:64].astype(F32)).astype(BF)
    msg3[...] = (cross3[...] + got[64:].astype(F32)).astype(BF)


def rest_kernel(
    q0, q1, g_ref, win, s1, e0, e1, m0, m1, best, inv_ref, delta_ref, dqo0, dqo1, dq2, dq3, att_ref, after,
    att, dq_out, acc, send,
    t0,
):
    core, _ = place()
    is0 = core == 0
    matrix = order_matrix(back=True)
    att[...] = reorder(matrix, att_ref[...])
    for h in range(HEADS):
        kl, vl = head(h), head(HEADS + h)
        grad, drift = coarse_grad(m1[h], best[h], inv_ref[h], g_ref[:, kl], delta_ref[h])
        units = [(q1[:, kl], s1[:, kl], s1[:, vl], e1[h], grad, drift)]
        for i, (number, keys) in enumerate(((1 - core, 384), (core, 256))):
            rows, kept = part(number, 128), slice(i * 128, (i + 1) * 128)
            share = jnp.exp2(m0[h, kept] - best[h, rows]) * inv_ref[h, rows]
            grad = (share * g_ref[rows, kl].astype(F32)).astype(BF)
            drift = share * delta_ref[h, rows]
            units.append((q0[rows, kl], win[:keys, kl], win[:keys, vl], e0[h, kept, :keys], grad, drift))
        (dq, dk, dv), (dq_in, dk_in, dv_in), (dq_out0, dk_out, dv_out) = backward(units)
        t0[h, part(1 - core, 128)] = dq_in
        t0[h, part(core, 128)] = dq_out0 + dqo0[h]
        acc[:, kl] = dk_in[:256] + dk_out
        acc[:, vl] = dv_in[:256] + dv_out
        dq = dq + dqo1[h] + expand(0.5 * (dq2[h] + expand(0.5 * dq3[h])))
        dq_out[:, kl] = reorder(matrix, (t0[h] + expand(0.5 * dq)).astype(BF))
        for lanes, value, fine in ((kl, dk, dk_in), (vl, dv, dv_in)):
            low, high = value[:64], value[64:]
            send[:128, lanes] = (fine[256:] + expand(0.5 * jnp.where(is0, low, high))).astype(BF)
            send[128:, lanes] = jnp.where(is0, high, low).astype(BF)


def send_kernel(r1, r2, send):
    send[...] = (r1[192:].astype(F32) + expand(0.5 * r2[32:].astype(F32))).astype(BF)


def add_kernel(own, r1, r2, after, acc):
    core, _ = place()
    is0 = core == 0
    for j in range(2 * HEADS):
        lanes = head(j)
        first = expand(0.25 * r2[:32, lanes].astype(F32), 2) + placed(r1[128:192, lanes].astype(F32), ~is0, 64)
        acc[:, lanes] = own[:, lanes] + expand(0.5 * first) + placed(r1[:128, lanes].astype(F32), is0, 128)


def cross_kernel(r3, after, second):
    second[...] = expand(0.5 * r3[...].astype(F32))


def final_kernel(acc, near, got, cross, dk, dv, done, sems):
    core, _ = place()
    is0 = core == 0
    matrix = order_matrix(back=True)
    copies = []
    for j in range(2 * HEADS):
        lanes = head(j)
        second = got[:, lanes].astype(F32) + cross[:, lanes]
        first = expand(0.5 * second) + placed(near[128:, lanes].astype(F32), is0, 64)
        total = acc[:, lanes] + expand(0.5 * first) + placed(near[:128, lanes].astype(F32), ~is0, 128)
        done[:, lanes] = reorder(matrix, total.astype(BF))
        target = (dk if j < HEADS else dv).at[:, head(j % HEADS)]
        copies.append(pltpu.make_async_copy(done.at[:, lanes], target, sems.at[j]))
        copies[-1].start()
    for copy in copies:
        copy.wait()


SPACES = {"v": pltpu.VMEM, "a": pl.ANY}


def call(kernel, outs, scratch=(), flops=0, specs=None, results=pltpu.VMEM):
    extra = {"in_specs": [pl.BlockSpec(memory_space=SPACES[s]) for s in specs]} if specs else {}
    if flops:
        extra["cost_estimate"] = pl.CostEstimate(flops=flops, bytes_accessed=1 << 20, transcendentals=0)
    return pl.pallas_call(
        kernel,
        out_shape=[jax.ShapeDtypeStruct(shape, dtype) for shape, dtype in outs],
        out_specs=[pl.BlockSpec(memory_space=results)] * len(outs),
        scratch_shapes=[s if not isinstance(s, tuple) else pltpu.VMEM(*s) for s in scratch],
        compiler_params=pltpu.CompilerParams(vmem_limit_bytes=VMEM_LIMIT),
        **extra,
    )


def per_device(query, key_rows, value_rows, out_grad):
    count = lax.axis_size("seq")
    sibling = [(i, i + 1) for i in range(0, count, 2)]
    next1 = [(i, i + 1) for i in range(1, count - 1, 2)]
    next2 = [(i, i + 5) for i in range(0, count - 5, 2)]
    forward = [(i, i + 1) for i in range(1, count, 4)]
    next3 = [(i, i + 6) for i in range(count - 6) if (i // 2) % 2 == 0]

    def swap(value, pairs):
        return lax.ppermute(value, "seq", pairs + [(b, a) for a, b in pairs])

    def rows(n, dtype=BF):
        return ((n, FULL), dtype)

    def heads(n, dtype=F32, lanes=HEAD):
        return ((HEADS, n, lanes), dtype)

    stat = heads(256)
    out = ((ROWS, D), BF)
    key_sib = swap(key_rows, sibling)
    value_sib = swap(value_rows, sibling)
    kv, l1, l3 = call(pre_kernel, [rows(256), rows(128), rows(32)])(
        jnp.concatenate([key_rows, value_rows], axis=1)
    )
    near, s1, msg1, msg2 = call(pack_kernel, [rows(128), rows(128), rows(256), rows(64)])(
        kv, l1, l3, key_sib, value_sib
    )
    r2 = swap(msg2, next2)
    r1 = swap(msg1, next1)
    r3 = swap(r2, forward)
    q0, g0, q1, q2, q3, win, e0, e1, m0, m1, top, zsum, ysum = call(
        local_kernel,
        [out, out, ((128, D), BF), ((64, D), BF), ((32, D), BF), rows(384)]
        + [heads(256, BF, 384), heads(128, BF), stat, heads(128), stat, stat, stat],
        [heads(128), heads(128)],
        flops=1 << 33,
    )(query, out_grad, kv, near, s1)
    (send,) = call(third_split_kernel, [rows(128)], specs="vva")(r2, r3, top)
    got3 = swap(send, sibling)
    outer1, send = call(second_split_kernel, [rows(128), rows(128)], specs="va")(r1, send)
    got2 = swap(send, sibling)
    top, zsum, ysum, eo0, eo1, mo0, mo1 = call(
        outer_kernel,
        [stat] * 3 + [heads(128, BF), heads(128, BF), heads(128), heads(128)],
        [heads(128), heads(128)],
        flops=1 << 30,
    )(q0, q1, r1, outer1, top, zsum, ysum)
    w3, e3, m3, top, zsum, ysum = call(
        third_kernel, [rows(192), heads(32, BF, 192), heads(32), stat, stat, stat], flops=1 << 28
    )(q3, r2, r3, got3, top, zsum, ysum)
    att, best, inv, delta, grad3, drift3, dq2, own2, send = call(
        far_kernel,
        [out, stat, stat, stat, heads(32, BF), heads(32), heads(64), rows(64, F32), rows(128)],
        [rows(192)],
    )(q2, g0, top, zsum, ysum, r1, got2, m3)
    got2 = swap(send, sibling)
    dq3, own3, cross3, send = call(
        third_back_kernel, [heads(32), rows(64, F32), rows(32, F32), rows(96)], flops=1 << 28
    )(q3, w3, e3, grad3, drift3)
    got3 = swap(send, sibling)
    dqo0, dqo1, d0, d1 = call(
        outer_back_kernel, [heads(128), heads(128), rows(128, F32), rows(128, F32)], flops=1 << 30
    )(q0, q1, g0, r1, outer1, eo0, eo1, mo0, mo1, best, inv, delta)
    (msg1,) = call(join_kernel, [rows(256)])(own2, d0, d1, got2)
    msg2, msg3 = call(third_join_kernel, [rows(64), rows(32)], flops=1 << 33)(own3, cross3, got3)
    r1 = swap(msg1, next1)
    r2 = swap(msg2, next2)
    r3 = swap(msg3, next3)
    attended, query_grad, acc, send = call(
        rest_kernel,
        [out, out, rows(256, F32), rows(192)],
        [stat],
        flops=1 << 29,
        specs="v" * 17 + "a",
    )(q0, q1, g0, win, s1, e0, e1, m0, m1, best, inv, delta, dqo0, dqo1, dq2, dq3, att, msg1)
    near = swap(send, sibling)
    (send,) = call(send_kernel, [rows(64)], flops=1 << 34)(r1, r2)
    got = swap(send, sibling)
    (acc,) = call(add_kernel, [rows(256, F32)], specs="vvva")(acc, r1, r2, send)
    (cross,) = call(cross_kernel, [rows(64, F32)], flops=1 << 34, specs="va")(r3, acc)
    key_grad, value_grad = call(
        final_kernel, [out, out], [rows(256), pltpu.SemaphoreType.DMA((2 * HEADS,))], results=pl.ANY
    )(acc, near, got, cross)
    return attended, query_grad, key_grad, value_grad


def solution(mesh):
    spec = P(("batch", "seq"), None)
    return jax.shard_map(
        per_device, mesh=mesh, in_specs=(spec,) * 4, out_specs=(spec,) * 4, check_vma=False
    )
```

```python
import jax
import jax.numpy as jnp
from jax import lax
from jax.experimental import pallas as pl
from jax.experimental.pallas import tpu as pltpu
from jax.sharding import PartitionSpec as P

HEADS = 4
HEAD = 128
D = HEADS * HEAD
ROWS = 256
FULL = 2 * D
SCALE = HEAD**-0.5
LOG2E = 1.4426950408889634
EXP_SCALE = SCALE * LOG2E
NEG = -1e30
VMEM_LIMIT = 40 * 1024 * 1024
BF = jnp.bfloat16
F32 = jnp.float32

RUN = 16


def place():
    index = lax.axis_index("seq")
    return lax.rem(index, 2), lax.div(index, 2)


def part(number, size):
    return pl.ds(pl.multiple_of(number * size, size), size)


def head(h):
    return slice(h * HEAD, (h + 1) * HEAD)


def order_matrix(back=False):
    a = lax.broadcasted_iota(jnp.int32, (128, 128), 0)
    b = lax.broadcasted_iota(jnp.int32, (128, 128), 1)
    row, token = (b, a) if back else (a, b)
    hit = row == (token & 7) * RUN + lax.shift_right_logical(token, 3)
    return jnp.where(hit, 1.0, 0.0).astype(BF)


def reorder(matrix, x):
    blocks = [jnp.dot(matrix, x[i : i + 128], preferred_element_type=F32) for i in range(0, x.shape[0], 128)]
    return jnp.concatenate(blocks, axis=0).astype(BF)


def coarse(x):
    rows, lanes = x.shape
    y = x.astype(F32).reshape(rows // (2 * RUN), 2, RUN, lanes)
    return ((y[:, 0] + y[:, 1]) * 0.5).reshape(rows // 2, lanes).astype(BF)


def expand(x, level=1):
    rows, lanes = x.shape
    step = 2**level
    y = jnp.broadcast_to(x.reshape(rows // RUN, 1, RUN, lanes), (rows // RUN, step, RUN, lanes))
    return y.reshape(rows * step, lanes)


def fold(x, level):
    rows, lanes = x.shape
    step = 2**level
    y = x.reshape(rows // (step * RUN), step, RUN, lanes)
    total = y[:, 0]
    for s in range(1, step):
        total = total + y[:, s]
    return total.reshape(rows // step, lanes)


def nt(a, b):
    return lax.dot_general(a, b, (((1,), (1,)), ((), ())), preferred_element_type=F32)


def tn(a, b):
    return lax.dot_general(a, b, (((0,), (0,)), ((), ())), preferred_element_type=F32)


def nn(a, b):
    return jnp.dot(a, b, preferred_element_type=F32)


def lanes128(value):
    return jnp.broadcast_to(value, (value.shape[0], HEAD))


def wide(value, lanes):
    pieces = [value[:, : min(HEAD, lanes - i)] for i in range(0, lanes, HEAD)]
    return pieces[0] if len(pieces) == 1 else jnp.concatenate(pieces, axis=1)


def penalty(ok):
    return jnp.where(ok, 0.0, NEG).astype(F32)


def half_masks():
    row = lax.broadcasted_iota(jnp.int32, (128, 128), 0) >= 64
    key = lax.broadcasted_iota(jnp.int32, (128, 128), 1) >= 64
    left = jnp.where(jnp.logical_and(~row, key), NEG, 0.0).astype(F32)
    right = jnp.where(jnp.logical_and(row, ~key), NEG, 0.0).astype(F32)
    return left, right


def soft(units):
    scores = [nt(q, k) if bias is None else nt(q, k) + bias for q, k, _, bias in units]
    peaks = [jnp.max(s, axis=1, keepdims=True) for s in scores]
    weights = [jnp.exp2((s - peak) * EXP_SCALE) for s, peak in zip(scores, peaks)]
    rounded = [e.astype(BF) for e in weights]
    mixes = [nn(eb, v) for eb, (_, _, v, _) in zip(rounded, units)]
    sums = [jnp.sum(e, axis=1, keepdims=True) for e in weights]
    return [
        (e, lanes128(peak * EXP_SCALE), lanes128(den), mix)
        for e, peak, den, mix in zip(weights, peaks, sums, mixes)
    ]


def backward(units):
    inners = [nt(grad, v) for _, _, v, _, grad, _ in units]
    dvs = [tn(e.astype(BF), grad) for _, _, _, e, grad, _ in units]
    dscores = [
        (e * (inner - wide(drift, e.shape[1]))).astype(BF)
        for inner, (_, _, _, e, _, drift) in zip(inners, units)
    ]
    dqs = [nn(dscore, k) * SCALE for dscore, (_, k, _, _, _, _) in zip(dscores, units)]
    dks = [tn(dscore, q) * SCALE for dscore, (q, _, _, _, _, _) in zip(dscores, units)]
    return list(zip(dqs, dks, dvs))


def merge(top, z, y, pieces):
    best = top
    peaks = [expand(m, level) if level else m for m, _, _, level in pieces]
    for m in peaks:
        best = jnp.maximum(best, m)
    f = jnp.exp2(top - best)
    z, y = f * z, f * y
    factors = []
    for m, (_, d, n, level) in zip(peaks, pieces):
        f = jnp.exp2(m - best)
        if level:
            f = f * 2.0**level
            d, n = expand(d, level), expand(n, level)
        factors.append(f)
        z = z + f * d
        y = y + f * n
    return best, z, y, factors


def placed(value, first, rows):
    zeros = jnp.zeros((rows, value.shape[1]), F32)
    return jnp.concatenate([jnp.where(first, value, zeros), jnp.where(first, zeros, value)], axis=0)


def pre_kernel(raw, kv, l1, l3):
    matrix = order_matrix()
    for i in range(2):
        lanes = slice(i * D, (i + 1) * D)
        fine = reorder(matrix, raw[:, lanes])
        kv[:, lanes] = fine
        fine = coarse(fine)
        l1[:, lanes] = fine
        l3[:, lanes] = coarse(coarse(fine))


def pack_kernel(kv, l1, l3, ks, vs, near, s1, msg1, msg2):
    core, _ = place()
    matrix = order_matrix()
    for i, raw in enumerate((ks, vs)):
        lanes = slice(i * D, (i + 1) * D)
        fine = reorder(matrix, raw[...])
        near[:, lanes] = jnp.where(core == 0, fine[:128], fine[128:])
        first = coarse(fine)
        s1[:, lanes] = first
        second = coarse(first)
        msg1[192:, lanes] = second
        msg2[32:, lanes] = coarse(second)
    msg1[:128] = kv[part(core, 128), :]
    msg1[128:192] = l1[part(1 - core, 64), :]
    msg2[:32] = l3[...]


def local_kernel(q_ref, g_ref, kv, near, s1, q0, g0, q1, q2, q3, win, e0, e1, m0, m1, top, zsum, ysum, d1, n1):
    core, _ = place()
    matrix = order_matrix()
    q0[...] = reorder(matrix, q_ref[...])
    g0[...] = reorder(matrix, g_ref[...])
    q1[...] = coarse(q0[...])
    q2[...] = coarse(q1[...])
    q3[...] = coarse(q2[...])
    win[:256] = kv[...]
    win[256:] = near[...]
    left, right = half_masks()
    bias = jnp.where(core == 0, right, left)
    for h in range(HEADS):
        kl, vl = head(h), head(HEADS + h)
        blocks = ((1 - core, 384), (core, 256))
        units = [(q1[:, kl], s1[:, kl], s1[:, vl], bias)]
        units += [(q0[part(n, 128), kl], win[:keys, kl], win[:keys, vl], None) for n, keys in blocks]
        first, *fine = soft(units)
        e1[h], m1[h], d1[h], n1[h] = first
        for i, (number, keys) in enumerate(blocks):
            rows, half = part(number, 128), part(number, 64)
            e, m, d, n = fine[i]
            e0[h, i * 128 : (i + 1) * 128, :keys] = e
            m0[h, i * 128 : (i + 1) * 128] = m
            top[h, rows], zsum[h, rows], ysum[h, rows], _ = merge(
                m, d, n, [(m1[h, half], d1[h, half], n1[h, half], 1)]
            )


def second_split_kernel(r1, after, l1, send):
    core, _ = place()
    l1[part(core, 64), :] = r1[128:192]
    l1[part(1 - core, 64), :] = coarse(r1[:128])
    send[:64] = coarse(l1[...])
    send[64:] = r1[192:]


def third_split_kernel(r2, r3, after, send):
    send[:64] = r2[...]
    send[64:] = r3[...]


def outer_kernel(q0, q1, r1, l1, top, zsum, ysum, top_out, z_out, y_out, e0, e1, m0, m1, d1, n1):
    core, chip = place()
    is0 = core == 0
    bad = penalty(jnp.where(is0, chip >= 1, chip <= 30))
    left, right = half_masks()
    bias = jnp.where(is0, left, right) + bad
    outer = part(core, 128)
    units = []
    for h in range(HEADS):
        kl, vl = head(h), head(HEADS + h)
        units.append((q1[:, kl], l1[:, kl], l1[:, vl], bias))
        units.append((q0[outer, kl], r1[:128, kl], r1[:128, vl], bad))
    results = soft(units)
    for h in range(HEADS):
        e1[h], m1[h], d1[h], n1[h] = results[2 * h]
        e0[h], m, d, n = results[2 * h + 1]
        m0[h] = m
        for number in (core, 1 - core):
            rows, half = part(number, 128), part(number, 64)
            pieces = [(m1[h, half], d1[h, half], n1[h, half], 1)]
            if number is core:
                pieces.append((m, d, n, 0))
            top_out[h, rows], z_out[h, rows], y_out[h, rows], _ = merge(
                top[h, rows], zsum[h, rows], ysum[h, rows], pieces
            )


def third_kernel(q3, r2, r3, got, top, zsum, ysum, w3, e3, m3, top_out, z_out, y_out):
    core, chip = place()
    is0 = core == 0
    holder = lax.rem(core + chip, 2) == 1
    w3[:64] = r2[...]
    w3[64:128] = got[:64]
    w3[128:] = jnp.where(holder, r3[...], got[64:])
    low2, high2 = chip >= 2, chip <= 29
    even = lax.rem(chip, 2) == 0
    lane = lax.broadcasted_iota(jnp.int32, (1, 192), 1)
    cross_bad = penalty(jnp.where(even, chip <= 28, chip >= 3))
    own_bad = penalty(jnp.where(is0, high2, low2))
    sib_bad = penalty(jnp.where(is0, low2, high2))
    bias = jnp.where(lane < 64, own_bad, jnp.where(lane < 128, sib_bad, cross_bad))
    results = soft([(q3[:, head(h)], w3[:, head(h)], w3[:, head(HEADS + h)], bias) for h in range(HEADS)])
    for h in range(HEADS):
        e3[h], m3[h], d, n = results[h]
        for c in range(2):
            r, b = slice(c * 128, (c + 1) * 128), slice(c * 16, (c + 1) * 16)
            top_out[h, r], z_out[h, r], y_out[h, r], _ = merge(
                top[h, r], zsum[h, r], ysum[h, r], [(m3[h, b], d[b], n[b], 3)]
            )


def far_kernel(
    q2, g_ref, top, zsum, ysum, r1, got2, m3,
    att, best_out, inv_out, delta_out, grad3, drift3, dq2, own2, send,
    w2,
):
    core, chip = place()
    is0 = core == 0
    w2[:128] = got2[...]
    w2[128:] = r1[192:]
    left_ok, right_ok = chip >= 1, chip <= 30
    lane = lax.broadcasted_iota(jnp.int32, (1, 192), 1)
    own_bad = penalty(jnp.where(is0, left_ok, right_ok))
    sib_bad = penalty(jnp.where(is0, right_ok, left_ok))
    bias = jnp.where(lane < 128, sib_bad, own_bad)
    units = [(q2[:, head(h)], w2[:, head(h)], w2[:, head(HEADS + h)], bias) for h in range(HEADS)]
    results = soft(units)
    units = []
    for h in range(HEADS):
        kl, vl = head(h), head(HEADS + h)
        e2, m2, d2, n2 = results[h]
        grads = ([], [])
        drifts = ([], [])
        for c in range(2):
            r = slice(c * 128, (c + 1) * 128)
            a, b = slice(c * 32, (c + 1) * 32), slice(c * 16, (c + 1) * 16)
            best, z, y, factors = merge(top[h, r], zsum[h, r], ysum[h, r], [(m2[a], d2[a], n2[a], 2)])
            factors.append(8.0 * jnp.exp2(expand(m3[h, b], 3) - best))
            inv = 1.0 / z
            y = y * inv
            att[r, kl] = y.astype(BF)
            g = g_ref[r, kl].astype(F32)
            delta = lanes128(jnp.sum(g * y, axis=1, keepdims=True))
            best_out[h, r] = best
            inv_out[h, r] = inv
            delta_out[h, r] = delta
            for i in range(2):
                share = factors[i] * inv
                grads[i].append(fold(share * g, i + 2))
                drifts[i].append(fold(share * delta, i + 2))
        grad = jnp.concatenate(grads[0], axis=0).astype(BF)
        units.append((q2[:, kl], w2[:, kl], w2[:, vl], e2, grad, jnp.concatenate(drifts[0], axis=0)))
        grad3[h] = jnp.concatenate(grads[1], axis=0).astype(BF)
        drift3[h] = jnp.concatenate(drifts[1], axis=0)
    for h, (dq, dk, dv) in enumerate(backward(units)):
        dq2[h] = dq
        for lanes, value in ((head(h), dk), (head(HEADS + h), dv)):
            send[:, lanes] = value[:128].astype(BF)
            own2[:, lanes] = value[128:]


def third_back_kernel(q3, w3, e3, grad, drift, dq3, own3, cross3, send):
    core, chip = place()
    holder = lax.rem(core + chip, 2) == 1
    units = []
    for h in range(HEADS):
        units.append((q3[:, head(h)], w3[:, head(h)], w3[:, head(HEADS + h)], e3[h], grad[h], drift[h]))
    for h, (dq, dk, dv) in enumerate(backward(units)):
        dq3[h] = dq
        for lanes, value in ((head(h), dk), (head(HEADS + h), dv)):
            own3[:, lanes] = value[:64]
            send[:64, lanes] = value[64:128].astype(BF)
            cross3[:, lanes] = jnp.where(holder, value[128:160], value[160:])
            send[64:, lanes] = jnp.where(holder, value[160:], value[128:160]).astype(BF)


def coarse_grad(m, best, inv, g, delta):
    grads, drifts = [], []
    for c in range(2):
        r, half = slice(c * 128, (c + 1) * 128), slice(c * 64, (c + 1) * 64)
        share = jnp.exp2(expand(m[half]) - best[r]) * (2.0 * inv[r])
        grads.append(fold(share * g[r].astype(F32), 1))
        drifts.append(fold(share * delta[r], 1))
    return jnp.concatenate(grads, axis=0).astype(BF), jnp.concatenate(drifts, axis=0)


def outer_back_kernel(
    q0, q1, g_ref, r1, l1, e0, e1, m0, m1, best, inv_ref, delta_ref,
    dq0, dq1, d0, d1,
):
    core, _ = place()
    outer = part(core, 128)
    units = []
    for h in range(HEADS):
        kl, vl = head(h), head(HEADS + h)
        share = jnp.exp2(m0[h] - best[h, outer]) * inv_ref[h, outer]
        grad = (share * g_ref[outer, kl].astype(F32)).astype(BF)
        drift = share * delta_ref[h, outer]
        units.append((q0[outer, kl], r1[:128, kl], r1[:128, vl], e0[h], grad, drift))
        grad, drift = coarse_grad(m1[h], best[h], inv_ref[h], g_ref[:, kl], delta_ref[h])
        units.append((q1[:, kl], l1[:, kl], l1[:, vl], e1[h], grad, drift))
    results = backward(units)
    for h in range(HEADS):
        kl, vl = head(h), head(HEADS + h)
        dq0[h], d0[:, kl], d0[:, vl] = results[2 * h]
        dq1[h], d1[:, kl], d1[:, vl] = results[2 * h + 1]


def join_kernel(own2, d0, d1, got, msg1):
    core, _ = place()
    is0 = core == 0
    for j in range(2 * HEADS):
        lanes = head(j)
        msg1[192:, lanes] = (own2[:, lanes] + got[64:, lanes].astype(F32)).astype(BF)
        first = d1[:, lanes] + expand(0.5 * got[:64, lanes].astype(F32))
        low, high = first[:64], first[64:]
        msg1[128:192, lanes] = jnp.where(is0, low, high).astype(BF)
        msg1[:128, lanes] = (d0[:, lanes] + expand(0.5 * jnp.where(is0, high, low))).astype(BF)


def third_join_kernel(own3, cross3, got, msg2, msg3):
    msg2[...] = (own3[...] + got[:64].astype(F32)).astype(BF)
    msg3[...] = (cross3[...] + got[64:].astype(F32)).astype(BF)


def rest_kernel(
    q0, q1, g_ref, win, s1, e0, e1, m0, m1, best, inv_ref, delta_ref, dqo0, dqo1, dq2, dq3, att_ref, after,
    att, dq_out, acc, send,
    t0,
):
    core, _ = place()
    is0 = core == 0
    matrix = order_matrix(back=True)
    att[...] = reorder(matrix, att_ref[...])
    for h in range(HEADS):
        kl, vl = head(h), head(HEADS + h)
        grad, drift = coarse_grad(m1[h], best[h], inv_ref[h], g_ref[:, kl], delta_ref[h])
        units = [(q1[:, kl], s1[:, kl], s1[:, vl], e1[h], grad, drift)]
        for i, (number, keys) in enumerate(((1 - core, 384), (core, 256))):
            rows, kept = part(number, 128), slice(i * 128, (i + 1) * 128)
            share = jnp.exp2(m0[h, kept] - best[h, rows]) * inv_ref[h, rows]
            grad = (share * g_ref[rows, kl].astype(F32)).astype(BF)
            drift = share * delta_ref[h, rows]
            units.append((q0[rows, kl], win[:keys, kl], win[:keys, vl], e0[h, kept, :keys], grad, drift))
        (dq, dk, dv), (dq_in, dk_in, dv_in), (dq_out0, dk_out, dv_out) = backward(units)
        t0[h, part(1 - core, 128)] = dq_in
        t0[h, part(core, 128)] = dq_out0 + dqo0[h]
        acc[:, kl] = dk_in[:256] + dk_out
        acc[:, vl] = dv_in[:256] + dv_out
        dq = dq + dqo1[h] + expand(0.5 * (dq2[h] + expand(0.5 * dq3[h])))
        dq_out[:, kl] = reorder(matrix, (t0[h] + expand(0.5 * dq)).astype(BF))
        for lanes, value, fine in ((kl, dk, dk_in), (vl, dv, dv_in)):
            low, high = value[:64], value[64:]
            send[:128, lanes] = (fine[256:] + expand(0.5 * jnp.where(is0, low, high))).astype(BF)
            send[128:, lanes] = jnp.where(is0, high, low).astype(BF)


def send_kernel(r1, r2, send):
    send[...] = (r1[192:].astype(F32) + expand(0.5 * r2[32:].astype(F32))).astype(BF)


def add_kernel(own, r1, r2, after, acc):
    core, _ = place()
    is0 = core == 0
    for j in range(2 * HEADS):
        lanes = head(j)
        first = expand(0.25 * r2[:32, lanes].astype(F32), 2) + placed(r1[128:192, lanes].astype(F32), ~is0, 64)
        acc[:, lanes] = own[:, lanes] + expand(0.5 * first) + placed(r1[:128, lanes].astype(F32), is0, 128)


def cross_kernel(r3, after, second):
    second[...] = expand(0.5 * r3[...].astype(F32))


def final_kernel(acc, near, got, cross, dk, dv, done, sems):
    core, _ = place()
    is0 = core == 0
    matrix = order_matrix(back=True)
    copies = []
    for j in range(2 * HEADS):
        lanes = head(j)
        second = got[:, lanes].astype(F32) + cross[:, lanes]
        first = expand(0.5 * second) + placed(near[128:, lanes].astype(F32), is0, 64)
        total = acc[:, lanes] + expand(0.5 * first) + placed(near[:128, lanes].astype(F32), ~is0, 128)
        done[:, lanes] = reorder(matrix, total.astype(BF))
        target = (dk if j < HEADS else dv).at[:, head(j % HEADS)]
        copies.append(pltpu.make_async_copy(done.at[:, lanes], target, sems.at[j]))
        copies[-1].start()
    for copy in copies:
        copy.wait()


SPACES = {"v": pltpu.VMEM, "a": pl.ANY}


def call(kernel, outs, scratch=(), flops=0, specs=None, results=pltpu.VMEM):
    extra = {"in_specs": [pl.BlockSpec(memory_space=SPACES[s]) for s in specs]} if specs else {}
    if flops:
        extra["cost_estimate"] = pl.CostEstimate(flops=flops, bytes_accessed=1 << 20, transcendentals=0)
    return pl.pallas_call(
        kernel,
        out_shape=[jax.ShapeDtypeStruct(shape, dtype) for shape, dtype in outs],
        out_specs=[pl.BlockSpec(memory_space=results)] * len(outs),
        scratch_shapes=[s if not isinstance(s, tuple) else pltpu.VMEM(*s) for s in scratch],
        compiler_params=pltpu.CompilerParams(vmem_limit_bytes=VMEM_LIMIT),
        **extra,
    )


def per_device(query, key_rows, value_rows, out_grad):
    count = lax.axis_size("seq")
    sibling = [(i, i + 1) for i in range(0, count, 2)]
    next1 = [(i, i + 1) for i in range(1, count - 1, 2)]
    next2 = [(i, i + 5) for i in range(0, count - 5, 2)]
    forward = [(i, i + 1) for i in range(1, count, 4)]
    next3 = [(i, i + 6) for i in range(count - 6) if (i // 2) % 2 == 0]

    def swap(value, pairs):
        return lax.ppermute(value, "seq", pairs + [(b, a) for a, b in pairs])

    def rows(n, dtype=BF):
        return ((n, FULL), dtype)

    def heads(n, dtype=F32, lanes=HEAD):
        return ((HEADS, n, lanes), dtype)

    stat = heads(256)
    out = ((ROWS, D), BF)
    key_sib = swap(key_rows, sibling)
    value_sib = swap(value_rows, sibling)
    kv, l1, l3 = call(pre_kernel, [rows(256), rows(128), rows(32)])(
        jnp.concatenate([key_rows, value_rows], axis=1)
    )
    near, s1, msg1, msg2 = call(pack_kernel, [rows(128), rows(128), rows(256), rows(64)])(
        kv, l1, l3, key_sib, value_sib
    )
    r2 = swap(msg2, next2)
    r1 = swap(msg1, next1)
    r3 = swap(r2, forward)
    q0, g0, q1, q2, q3, win, e0, e1, m0, m1, top, zsum, ysum = call(
        local_kernel,
        [out, out, ((128, D), BF), ((64, D), BF), ((32, D), BF), rows(384)]
        + [heads(256, F32, 384), heads(128), stat, heads(128), stat, stat, stat],
        [heads(128), heads(128)],
        flops=1 << 33,
    )(query, out_grad, kv, near, s1)
    (send,) = call(third_split_kernel, [rows(128)], specs="vva")(r2, r3, top)
    got3 = swap(send, sibling)
    outer1, send = call(second_split_kernel, [rows(128), rows(128)], specs="va")(r1, send)
    got2 = swap(send, sibling)
    top, zsum, ysum, eo0, eo1, mo0, mo1 = call(
        outer_kernel,
        [stat] * 3 + [heads(128), heads(128), heads(128), heads(128)],
        [heads(128), heads(128)],
        flops=1 << 30,
    )(q0, q1, r1, outer1, top, zsum, ysum)
    w3, e3, m3, top, zsum, ysum = call(
        third_kernel, [rows(192), heads(32, F32, 192), heads(32), stat, stat, stat], flops=1 << 28
    )(q3, r2, r3, got3, top, zsum, ysum)
    att, best, inv, delta, grad3, drift3, dq2, own2, send = call(
        far_kernel,
        [out, stat, stat, stat, heads(32, BF), heads(32), heads(64), rows(64, F32), rows(128)],
        [rows(192)],
    )(q2, g0, top, zsum, ysum, r1, got2, m3)
    got2 = swap(send, sibling)
    dq3, own3, cross3, send = call(
        third_back_kernel, [heads(32), rows(64, F32), rows(32, F32), rows(96)], flops=1 << 28
    )(q3, w3, e3, grad3, drift3)
    got3 = swap(send, sibling)
    dqo0, dqo1, d0, d1 = call(
        outer_back_kernel, [heads(128), heads(128), rows(128, F32), rows(128, F32)], flops=1 << 30
    )(q0, q1, g0, r1, outer1, eo0, eo1, mo0, mo1, best, inv, delta)
    (msg1,) = call(join_kernel, [rows(256)])(own2, d0, d1, got2)
    msg2, msg3 = call(third_join_kernel, [rows(64), rows(32)], flops=1 << 33)(own3, cross3, got3)
    r1 = swap(msg1, next1)
    r2 = swap(msg2, next2)
    r3 = swap(msg3, next3)
    attended, query_grad, acc, send = call(
        rest_kernel,
        [out, out, rows(256, F32), rows(192)],
        [stat],
        flops=1 << 29,
        specs="v" * 17 + "a",
    )(q0, q1, g0, win, s1, e0, e1, m0, m1, best, inv, delta, dqo0, dqo1, dq2, dq3, att, msg1)
    near = swap(send, sibling)
    (send,) = call(send_kernel, [rows(64)], flops=1 << 34)(r1, r2)
    got = swap(send, sibling)
    (acc,) = call(add_kernel, [rows(256, F32)], specs="vvva")(acc, r1, r2, send)
    (cross,) = call(cross_kernel, [rows(64, F32)], flops=1 << 34, specs="va")(r3, acc)
    key_grad, value_grad = call(
        final_kernel, [out, out], [rows(256), pltpu.SemaphoreType.DMA((2 * HEADS,))], results=pl.ANY
    )(acc, near, got, cross)
    return attended, query_grad, key_grad, value_grad


def solution(mesh):
    spec = P(("batch", "seq"), None)
    return jax.shard_map(
        per_device, mesh=mesh, in_specs=(spec,) * 4, out_specs=(spec,) * 4, check_vma=False
    )
```

```python
import jax
import jax.numpy as jnp
from jax import lax
from jax.experimental import pallas as pl
from jax.experimental.pallas import tpu as pltpu
from jax.sharding import PartitionSpec as P

HEADS = 4
HEAD = 128
D = HEADS * HEAD
ROWS = 256
FULL = 2 * D
SCALE = HEAD**-0.5
LOG2E = 1.4426950408889634
EXP_SCALE = SCALE * LOG2E
NEG = -1e30
VMEM_LIMIT = 40 * 1024 * 1024
BF = jnp.bfloat16
F32 = jnp.float32

RUN = 16


def place():
    index = lax.axis_index("seq")
    return lax.rem(index, 2), lax.div(index, 2)


def part(number, size):
    return pl.ds(pl.multiple_of(number * size, size), size)


def head(h):
    return slice(h * HEAD, (h + 1) * HEAD)


def order_matrix(back=False):
    a = lax.broadcasted_iota(jnp.int32, (128, 128), 0)
    b = lax.broadcasted_iota(jnp.int32, (128, 128), 1)
    row, token = (b, a) if back else (a, b)
    hit = row == (token & 7) * RUN + lax.shift_right_logical(token, 3)
    return jnp.where(hit, 1.0, 0.0).astype(BF)


def reorder(matrix, x):
    blocks = [jnp.dot(matrix, x[i : i + 128], preferred_element_type=F32) for i in range(0, x.shape[0], 128)]
    return jnp.concatenate(blocks, axis=0).astype(BF)


def coarse(x):
    rows, lanes = x.shape
    y = x.astype(F32).reshape(rows // (2 * RUN), 2, RUN, lanes)
    return ((y[:, 0] + y[:, 1]) * 0.5).reshape(rows // 2, lanes).astype(BF)


def expand(x, level=1):
    rows, lanes = x.shape
    step = 2**level
    y = jnp.broadcast_to(x.reshape(rows // RUN, 1, RUN, lanes), (rows // RUN, step, RUN, lanes))
    return y.reshape(rows * step, lanes)


def fold(x, level):
    rows, lanes = x.shape
    step = 2**level
    y = x.reshape(rows // (step * RUN), step, RUN, lanes)
    total = y[:, 0]
    for s in range(1, step):
        total = total + y[:, s]
    return total.reshape(rows // step, lanes)


def nt(a, b):
    return lax.dot_general(a, b, (((1,), (1,)), ((), ())), preferred_element_type=F32)


def tn(a, b):
    return lax.dot_general(a, b, (((0,), (0,)), ((), ())), preferred_element_type=F32)


def nn(a, b):
    return jnp.dot(a, b, preferred_element_type=F32)


def lanes128(value):
    return jnp.broadcast_to(value, (value.shape[0], HEAD))


def wide(value, lanes):
    pieces = [value[:, : min(HEAD, lanes - i)] for i in range(0, lanes, HEAD)]
    return pieces[0] if len(pieces) == 1 else jnp.concatenate(pieces, axis=1)


def penalty(ok):
    return jnp.where(ok, 0.0, NEG).astype(F32)


def half_masks():
    row = lax.broadcasted_iota(jnp.int32, (128, 128), 0) >= 64
    key = lax.broadcasted_iota(jnp.int32, (128, 128), 1) >= 64
    left = jnp.where(jnp.logical_and(~row, key), NEG, 0.0).astype(F32)
    right = jnp.where(jnp.logical_and(row, ~key), NEG, 0.0).astype(F32)
    return left, right


def soft(units):
    scores = [nt(q, k) if bias is None else nt(q, k) + bias for q, k, _, bias in units]
    peaks = [jnp.max(s, axis=1, keepdims=True) for s in scores]
    weights = [jnp.exp2((s - peak) * EXP_SCALE) for s, peak in zip(scores, peaks)]
    rounded = [e.astype(BF) for e in weights]
    mixes = [nn(eb, v) for eb, (_, _, v, _) in zip(rounded, units)]
    sums = [jnp.sum(e, axis=1, keepdims=True) for e in weights]
    return [
        (e, lanes128(peak * EXP_SCALE), lanes128(den), mix)
        for e, peak, den, mix in zip(weights, peaks, sums, mixes)
    ]


def backward(units):
    inners = [nt(grad, v) for _, _, v, _, grad, _ in units]
    dvs = [tn(e.astype(BF), grad) for _, _, _, e, grad, _ in units]
    dscores = [
        (e * (inner - wide(drift, e.shape[1]))).astype(BF)
        for inner, (_, _, _, e, _, drift) in zip(inners, units)
    ]
    dqs = [nn(dscore, k) * SCALE for dscore, (_, k, _, _, _, _) in zip(dscores, units)]
    dks = [tn(dscore, q) * SCALE for dscore, (q, _, _, _, _, _) in zip(dscores, units)]
    return list(zip(dqs, dks, dvs))


def merge(top, z, y, pieces):
    best = top
    peaks = [expand(m, level) if level else m for m, _, _, level in pieces]
    for m in peaks:
        best = jnp.maximum(best, m)
    f = jnp.exp2(top - best)
    z, y = f * z, f * y
    factors = []
    for m, (_, d, n, level) in zip(peaks, pieces):
        f = jnp.exp2(m - best)
        if level:
            f = f * 2.0**level
            d, n = expand(d, level), expand(n, level)
        factors.append(f)
        z = z + f * d
        y = y + f * n
    return best, z, y, factors


def placed(value, first, rows):
    zeros = jnp.zeros((rows, value.shape[1]), F32)
    return jnp.concatenate([jnp.where(first, value, zeros), jnp.where(first, zeros, value)], axis=0)


def pre_kernel(raw, kv, l1, l3):
    matrix = order_matrix()
    for i in range(2):
        lanes = slice(i * D, (i + 1) * D)
        fine = reorder(matrix, raw[:, lanes])
        kv[:, lanes] = fine
        fine = coarse(fine)
        l1[:, lanes] = fine
        l3[:, lanes] = coarse(coarse(fine))


def pack_kernel(kv, l1, l3, ks, vs, near, s1, msg1, msg2):
    core, _ = place()
    matrix = order_matrix()
    for i, raw in enumerate((ks, vs)):
        lanes = slice(i * D, (i + 1) * D)
        fine = reorder(matrix, raw[...])
        near[:, lanes] = jnp.where(core == 0, fine[:128], fine[128:])
        first = coarse(fine)
        s1[:, lanes] = first
        second = coarse(first)
        msg1[192:, lanes] = second
        msg2[32:, lanes] = coarse(second)
    msg1[:128] = kv[part(core, 128), :]
    msg1[128:192] = l1[part(1 - core, 64), :]
    msg2[:32] = l3[...]


def local_kernel(q_ref, g_ref, kv, near, s1, q0, g0, q1, q2, q3, win, e0, e1, m0, m1, top, zsum, ysum, d1, n1):
    core, _ = place()
    matrix = order_matrix()
    q0[...] = reorder(matrix, q_ref[...])
    g0[...] = reorder(matrix, g_ref[...])
    q1[...] = coarse(q0[...])
    q2[...] = coarse(q1[...])
    q3[...] = coarse(q2[...])
    win[:256] = kv[...]
    win[256:] = near[...]
    left, right = half_masks()
    bias = jnp.where(core == 0, right, left)
    for h in range(HEADS):
        kl, vl = head(h), head(HEADS + h)
        blocks = ((1 - core, 384), (core, 256))
        units = [(q1[:, kl], s1[:, kl], s1[:, vl], bias)]
        units += [(q0[part(n, 128), kl], win[:keys, kl], win[:keys, vl], None) for n, keys in blocks]
        first, *fine = soft(units)
        e1[h], m1[h], d1[h], n1[h] = first
        for i, (number, keys) in enumerate(blocks):
            rows, half = part(number, 128), part(number, 64)
            e, m, d, n = fine[i]
            e0[h, i * 128 : (i + 1) * 128, :keys] = e
            m0[h, i * 128 : (i + 1) * 128] = m
            top[h, rows], zsum[h, rows], ysum[h, rows], _ = merge(
                m, d, n, [(m1[h, half], d1[h, half], n1[h, half], 1)]
            )


def second_split_kernel(r1, after, l1, send):
    core, _ = place()
    l1[part(core, 64), :] = r1[128:192]
    l1[part(1 - core, 64), :] = coarse(r1[:128])
    send[:64] = coarse(l1[...])
    send[64:] = r1[192:]


def third_split_kernel(r2, r3, after, send):
    send[:64] = r2[...]
    send[64:] = r3[...]


def outer_kernel(q0, q1, r1, l1, top, zsum, ysum, top_out, z_out, y_out, e0, e1, m0, m1, d1, n1):
    core, chip = place()
    is0 = core == 0
    bad = penalty(jnp.where(is0, chip >= 1, chip <= 30))
    left, right = half_masks()
    bias = jnp.where(is0, left, right) + bad
    outer = part(core, 128)
    units = []
    for h in range(HEADS):
        kl, vl = head(h), head(HEADS + h)
        units.append((q1[:, kl], l1[:, kl], l1[:, vl], bias))
        units.append((q0[outer, kl], r1[:128, kl], r1[:128, vl], bad))
    results = soft(units)
    for h in range(HEADS):
        e1[h], m1[h], d1[h], n1[h] = results[2 * h]
        e0[h], m, d, n = results[2 * h + 1]
        m0[h] = m
        for number in (core, 1 - core):
            rows, half = part(number, 128), part(number, 64)
            pieces = [(m1[h, half], d1[h, half], n1[h, half], 1)]
            if number is core:
                pieces.append((m, d, n, 0))
            top_out[h, rows], z_out[h, rows], y_out[h, rows], _ = merge(
                top[h, rows], zsum[h, rows], ysum[h, rows], pieces
            )


def third_kernel(q3, r2, r3, got, top, zsum, ysum, w3, e3, m3, top_out, z_out, y_out):
    core, chip = place()
    is0 = core == 0
    holder = lax.rem(core + chip, 2) == 1
    w3[:64] = r2[...]
    w3[64:128] = got[:64]
    w3[128:] = jnp.where(holder, r3[...], got[64:])
    low2, high2 = chip >= 2, chip <= 29
    even = lax.rem(chip, 2) == 0
    lane = lax.broadcasted_iota(jnp.int32, (1, 192), 1)
    cross_bad = penalty(jnp.where(even, chip <= 28, chip >= 3))
    own_bad = penalty(jnp.where(is0, high2, low2))
    sib_bad = penalty(jnp.where(is0, low2, high2))
    bias = jnp.where(lane < 64, own_bad, jnp.where(lane < 128, sib_bad, cross_bad))
    results = soft([(q3[:, head(h)], w3[:, head(h)], w3[:, head(HEADS + h)], bias) for h in range(HEADS)])
    for h in range(HEADS):
        e3[h], m3[h], d, n = results[h]
        for c in range(2):
            r, b = slice(c * 128, (c + 1) * 128), slice(c * 16, (c + 1) * 16)
            top_out[h, r], z_out[h, r], y_out[h, r], _ = merge(
                top[h, r], zsum[h, r], ysum[h, r], [(m3[h, b], d[b], n[b], 3)]
            )


def far_kernel(
    q2, g_ref, top, zsum, ysum, r1, got2, m3,
    att, best_out, inv_out, delta_out, grad3, drift3, dq2, own2, send,
    w2,
):
    core, chip = place()
    is0 = core == 0
    w2[:128] = got2[...]
    w2[128:] = r1[192:]
    left_ok, right_ok = chip >= 1, chip <= 30
    lane = lax.broadcasted_iota(jnp.int32, (1, 192), 1)
    own_bad = penalty(jnp.where(is0, left_ok, right_ok))
    sib_bad = penalty(jnp.where(is0, right_ok, left_ok))
    bias = jnp.where(lane < 128, sib_bad, own_bad)
    units = [(q2[:, head(h)], w2[:, head(h)], w2[:, head(HEADS + h)], bias) for h in range(HEADS)]
    results = soft(units)
    units = []
    for h in range(HEADS):
        kl, vl = head(h), head(HEADS + h)
        e2, m2, d2, n2 = results[h]
        grads = ([], [])
        drifts = ([], [])
        for c in range(2):
            r = slice(c * 128, (c + 1) * 128)
            a, b = slice(c * 32, (c + 1) * 32), slice(c * 16, (c + 1) * 16)
            best, z, y, factors = merge(top[h, r], zsum[h, r], ysum[h, r], [(m2[a], d2[a], n2[a], 2)])
            factors.append(8.0 * jnp.exp2(expand(m3[h, b], 3) - best))
            inv = 1.0 / z
            y = y * inv
            att[r, kl] = y.astype(BF)
            g = g_ref[r, kl].astype(F32)
            delta = lanes128(jnp.sum(g * y, axis=1, keepdims=True))
            best_out[h, r] = best
            inv_out[h, r] = inv
            delta_out[h, r] = delta
            for i in range(2):
                share = factors[i] * inv
                grads[i].append(fold(share * g, i + 2))
                drifts[i].append(fold(share * delta, i + 2))
        grad = jnp.concatenate(grads[0], axis=0).astype(BF)
        units.append((q2[:, kl], w2[:, kl], w2[:, vl], e2, grad, jnp.concatenate(drifts[0], axis=0)))
        grad3[h] = jnp.concatenate(grads[1], axis=0).astype(BF)
        drift3[h] = jnp.concatenate(drifts[1], axis=0)
    for h, (dq, dk, dv) in enumerate(backward(units)):
        dq2[h] = dq
        for lanes, value in ((head(h), dk), (head(HEADS + h), dv)):
            send[:, lanes] = value[:128].astype(BF)
            own2[:, lanes] = value[128:]


def third_back_kernel(q3, w3, e3, grad, drift, dq3, own3, cross3, send):
    core, chip = place()
    holder = lax.rem(core + chip, 2) == 1
    units = []
    for h in range(HEADS):
        units.append((q3[:, head(h)], w3[:, head(h)], w3[:, head(HEADS + h)], e3[h], grad[h], drift[h]))
    for h, (dq, dk, dv) in enumerate(backward(units)):
        dq3[h] = dq
        for lanes, value in ((head(h), dk), (head(HEADS + h), dv)):
            own3[:, lanes] = value[:64]
            send[:64, lanes] = value[64:128].astype(BF)
            cross3[:, lanes] = jnp.where(holder, value[128:160], value[160:])
            send[64:, lanes] = jnp.where(holder, value[160:], value[128:160]).astype(BF)


def coarse_grad(m, best, inv, g, delta):
    grads, drifts = [], []
    for c in range(2):
        r, half = slice(c * 128, (c + 1) * 128), slice(c * 64, (c + 1) * 64)
        share = jnp.exp2(expand(m[half]) - best[r]) * (2.0 * inv[r])
        grads.append(fold(share * g[r].astype(F32), 1))
        drifts.append(fold(share * delta[r], 1))
    return jnp.concatenate(grads, axis=0).astype(BF), jnp.concatenate(drifts, axis=0)


def outer_back_kernel(
    q0, q1, g_ref, r1, l1, e0, e1, m0, m1, best, inv_ref, delta_ref,
    dq0, dq1, d0, d1,
):
    core, _ = place()
    outer = part(core, 128)
    units = []
    for h in range(HEADS):
        kl, vl = head(h), head(HEADS + h)
        share = jnp.exp2(m0[h] - best[h, outer]) * inv_ref[h, outer]
        grad = (share * g_ref[outer, kl].astype(F32)).astype(BF)
        drift = share * delta_ref[h, outer]
        units.append((q0[outer, kl], r1[:128, kl], r1[:128, vl], e0[h], grad, drift))
        grad, drift = coarse_grad(m1[h], best[h], inv_ref[h], g_ref[:, kl], delta_ref[h])
        units.append((q1[:, kl], l1[:, kl], l1[:, vl], e1[h], grad, drift))
    results = backward(units)
    for h in range(HEADS):
        kl, vl = head(h), head(HEADS + h)
        dq0[h], d0[:, kl], d0[:, vl] = results[2 * h]
        dq1[h], d1[:, kl], d1[:, vl] = results[2 * h + 1]


def join_kernel(own2, d0, d1, got, msg1):
    core, _ = place()
    is0 = core == 0
    for j in range(2 * HEADS):
        lanes = head(j)
        msg1[192:, lanes] = (own2[:, lanes] + got[64:, lanes].astype(F32)).astype(BF)
        first = d1[:, lanes] + expand(0.5 * got[:64, lanes].astype(F32))
        low, high = first[:64], first[64:]
        msg1[128:192, lanes] = jnp.where(is0, low, high).astype(BF)
        msg1[:128, lanes] = (d0[:, lanes] + expand(0.5 * jnp.where(is0, high, low))).astype(BF)


def third_join_kernel(own3, cross3, got, msg2, msg3):
    msg2[...] = (own3[...] + got[:64].astype(F32)).astype(BF)
    msg3[...] = (cross3[...] + got[64:].astype(F32)).astype(BF)


def rest_kernel(
    q0, q1, g_ref, win, s1, e0, e1, m0, m1, best, inv_ref, delta_ref, dqo0, dqo1, dq2, dq3, att_ref, after,
    att, dq_out, acc, send,
    t0,
):
    core, _ = place()
    is0 = core == 0
    matrix = order_matrix(back=True)
    att[...] = reorder(matrix, att_ref[...])
    for h in range(HEADS):
        kl, vl = head(h), head(HEADS + h)
        grad, drift = coarse_grad(m1[h], best[h], inv_ref[h], g_ref[:, kl], delta_ref[h])
        units = [(q1[:, kl], s1[:, kl], s1[:, vl], e1[h], grad, drift)]
        for i, (number, keys) in enumerate(((1 - core, 384), (core, 256))):
            rows, kept = part(number, 128), slice(i * 128, (i + 1) * 128)
            share = jnp.exp2(m0[h, kept] - best[h, rows]) * inv_ref[h, rows]
            grad = (share * g_ref[rows, kl].astype(F32)).astype(BF)
            drift = share * delta_ref[h, rows]
            units.append((q0[rows, kl], win[:keys, kl], win[:keys, vl], e0[h, kept, :keys], grad, drift))
        (dq, dk, dv), (dq_in, dk_in, dv_in), (dq_out0, dk_out, dv_out) = backward(units)
        t0[h, part(1 - core, 128)] = dq_in
        t0[h, part(core, 128)] = dq_out0 + dqo0[h]
        acc[:, kl] = dk_in[:256] + dk_out
        acc[:, vl] = dv_in[:256] + dv_out
        dq = dq + dqo1[h] + expand(0.5 * (dq2[h] + expand(0.5 * dq3[h])))
        dq_out[:, kl] = reorder(matrix, (t0[h] + expand(0.5 * dq)).astype(BF))
        for lanes, value, fine in ((kl, dk, dk_in), (vl, dv, dv_in)):
            low, high = value[:64], value[64:]
            send[:128, lanes] = (fine[256:] + expand(0.5 * jnp.where(is0, low, high))).astype(BF)
            send[128:, lanes] = jnp.where(is0, high, low).astype(BF)


def send_kernel(r1, r2, send):
    send[...] = (r1[192:].astype(F32) + expand(0.5 * r2[32:].astype(F32))).astype(BF)


def add_kernel(own, r1, r2, after, acc):
    core, _ = place()
    is0 = core == 0
    for j in range(2 * HEADS):
        lanes = head(j)
        first = expand(0.25 * r2[:32, lanes].astype(F32), 2) + placed(r1[128:192, lanes].astype(F32), ~is0, 64)
        acc[:, lanes] = own[:, lanes] + expand(0.5 * first) + placed(r1[:128, lanes].astype(F32), is0, 128)


def cross_kernel(r3, after, second):
    second[...] = expand(0.5 * r3[...].astype(F32))


def final_kernel(acc, near, got, cross, dk, dv, done, sems):
    core, _ = place()
    is0 = core == 0
    matrix = order_matrix(back=True)
    copies = []
    for j in range(2 * HEADS):
        lanes = head(j)
        second = got[:, lanes].astype(F32) + cross[:, lanes]
        first = expand(0.5 * second) + placed(near[128:, lanes].astype(F32), is0, 64)
        total = acc[:, lanes] + expand(0.5 * first) + placed(near[:128, lanes].astype(F32), ~is0, 128)
        done[:, lanes] = reorder(matrix, total.astype(BF))
        target = (dk if j < HEADS else dv).at[:, head(j % HEADS)]
        copies.append(pltpu.make_async_copy(done.at[:, lanes], target, sems.at[j]))
        copies[-1].start()
    for copy in copies:
        copy.wait()


SPACES = {"v": pltpu.VMEM, "a": pl.ANY}


def call(kernel, outs, scratch=(), flops=0, specs=None, results=pltpu.VMEM):
    extra = {"in_specs": [pl.BlockSpec(memory_space=SPACES[s]) for s in specs]} if specs else {}
    if flops:
        extra["cost_estimate"] = pl.CostEstimate(flops=flops, bytes_accessed=1 << 20, transcendentals=0)
    return pl.pallas_call(
        kernel,
        out_shape=[jax.ShapeDtypeStruct(shape, dtype) for shape, dtype in outs],
        out_specs=[pl.BlockSpec(memory_space=results)] * len(outs),
        scratch_shapes=[s if not isinstance(s, tuple) else pltpu.VMEM(*s) for s in scratch],
        compiler_params=pltpu.CompilerParams(vmem_limit_bytes=VMEM_LIMIT),
        **extra,
    )


def per_device(query, key_rows, value_rows, out_grad):
    count = lax.axis_size("seq")
    sibling = [(i, i + 1) for i in range(0, count, 2)]
    next1 = [(i, i + 1) for i in range(1, count - 1, 2)]
    next2 = [(i, i + 5) for i in range(0, count - 5, 2)]
    forward = [(i, i + 1) for i in range(1, count, 4)]
    next3 = [(i, i + 6) for i in range(count - 6) if (i // 2) % 2 == 0]

    def swap(value, pairs):
        return lax.ppermute(value, "seq", pairs + [(b, a) for a, b in pairs])

    def rows(n, dtype=BF):
        return ((n, FULL), dtype)

    def heads(n, dtype=F32, lanes=HEAD):
        return ((HEADS, n, lanes), dtype)

    stat = heads(256)
    out = ((ROWS, D), BF)
    key_sib = swap(key_rows, sibling)
    value_sib = swap(value_rows, sibling)
    kv, l1, l3 = call(pre_kernel, [rows(256), rows(128), rows(32)])(
        jnp.concatenate([key_rows, value_rows], axis=1)
    )
    near, s1, msg1, msg2 = call(pack_kernel, [rows(128), rows(128), rows(256), rows(64)])(
        kv, l1, l3, key_sib, value_sib
    )
    r2 = swap(msg2, next2)
    r1 = swap(msg1, next1)
    r3 = swap(r2, forward)
    q0, g0, q1, q2, q3, win, e0, e1, m0, m1, top, zsum, ysum = call(
        local_kernel,
        [out, out, ((128, D), BF), ((64, D), BF), ((32, D), BF), rows(384)]
        + [heads(256, F32, 384), heads(128), stat, heads(128), stat, stat, stat],
        [heads(128), heads(128)],
        flops=1 << 33,
    )(query, out_grad, kv, near, s1)
    outer1, send = call(second_split_kernel, [rows(128), rows(128)], specs="va")(r1, top)
    (send3,) = call(third_split_kernel, [rows(128)], specs="vva")(r2, r3, send)
    got3 = swap(send3, sibling)
    got2 = swap(send, sibling)
    top, zsum, ysum, eo0, eo1, mo0, mo1 = call(
        outer_kernel,
        [stat] * 3 + [heads(128), heads(128), heads(128), heads(128)],
        [heads(128), heads(128)],
        flops=1 << 30,
    )(q0, q1, r1, outer1, top, zsum, ysum)
    w3, e3, m3, top, zsum, ysum = call(
        third_kernel, [rows(192), heads(32, F32, 192), heads(32), stat, stat, stat], flops=1 << 28
    )(q3, r2, r3, got3, top, zsum, ysum)
    att, best, inv, delta, grad3, drift3, dq2, own2, send = call(
        far_kernel,
        [out, stat, stat, stat, heads(32, BF), heads(32), heads(64), rows(64, F32), rows(128)],
        [rows(192)],
    )(q2, g0, top, zsum, ysum, r1, got2, m3)
    got2 = swap(send, sibling)
    dq3, own3, cross3, send = call(
        third_back_kernel, [heads(32), rows(64, F32), rows(32, F32), rows(96)], flops=1 << 28
    )(q3, w3, e3, grad3, drift3)
    got3 = swap(send, sibling)
    dqo0, dqo1, d0, d1 = call(
        outer_back_kernel, [heads(128), heads(128), rows(128, F32), rows(128, F32)], flops=1 << 30
    )(q0, q1, g0, r1, outer1, eo0, eo1, mo0, mo1, best, inv, delta)
    (msg1,) = call(join_kernel, [rows(256)])(own2, d0, d1, got2)
    msg2, msg3 = call(third_join_kernel, [rows(64), rows(32)], flops=1 << 33)(own3, cross3, got3)
    r1 = swap(msg1, next1)
    r2 = swap(msg2, next2)
    r3 = swap(msg3, next3)
    attended, query_grad, acc, send = call(
        rest_kernel,
        [out, out, rows(256, F32), rows(192)],
        [stat],
        flops=1 << 29,
        specs="v" * 17 + "a",
    )(q0, q1, g0, win, s1, e0, e1, m0, m1, best, inv, delta, dqo0, dqo1, dq2, dq3, att, msg1)
    near = swap(send, sibling)
    (send,) = call(send_kernel, [rows(64)], flops=1 << 34)(r1, r2)
    got = swap(send, sibling)
    (acc,) = call(add_kernel, [rows(256, F32)], specs="vvva")(acc, r1, r2, send)
    (cross,) = call(cross_kernel, [rows(64, F32)], flops=1 << 34, specs="va")(r3, acc)
    key_grad, value_grad = call(
        final_kernel, [out, out], [rows(256), pltpu.SemaphoreType.DMA((2 * HEADS,))], results=pl.ANY
    )(acc, near, got, cross)
    return attended, query_grad, key_grad, value_grad


def solution(mesh):
    spec = P(("batch", "seq"), None)
    return jax.shard_map(
        per_device, mesh=mesh, in_specs=(spec,) * 4, out_specs=(spec,) * 4, check_vma=False
    )
```
